512 devices in a mesh: dp: 8 (over y_lo, x), ctx: 64 (over z, y_hi, core).
Axes of the slice: x: 4, y: 4 (y_hi: 2, y_lo: 2; y = y_hi * 2 + y_lo), z: 16, core: 2. Of those that a mesh axis runs over, the one named last changes fastest.
Arguments:
- queries: bfloat16 [8, 8192, 1600], P('dp', 'ctx'), may hold values from -24 to 24
- key_vectors: bfloat16 [8, 8192, 320], P('dp', 'ctx'), may hold values from -24 to 24
- value_vectors: bfloat16 [8, 8192, 320], P('dp', 'ctx'), may hold values from -6 to 6
- meta_keys: bfloat16 [128, 320], replicated, may hold values from -6 to 6
- meta_values: bfloat16 [128, 320], replicated, may hold values from -6 to 6
- windows: int32 [25], replicated, may hold values from 1 to 1024, as said below
- ssm_input: bfloat16 [8, 8192, 1600], P('dp', 'ctx'), may hold values from -6 to 6
- input_map: bfloat16 [8, 8192, 16], P('dp', 'ctx'), may hold values from -0.59765625 to 0.59765625
- output_map: bfloat16 [8, 8192, 16], P('dp', 'ctx'), may hold values from -1.5 to 1.5
- log_decay: float32 [8, 8192, 25], P('dp', 'ctx'), may hold values from -1 to 0
- cotangent: bfloat16 [8, 8192, 1600], P('dp', 'ctx'), may hold values from -6 to 6
Outputs:
- grad_queries: bfloat16 [8, 8192, 1600], P('dp', 'ctx')
- grad_keys: bfloat16 [8, 8192, 320], P('dp', 'ctx')
- grad_values: bfloat16 [8, 8192, 320], P('dp', 'ctx')
- grad_meta: float32 [2, 128, 320], P(None, 'dp', 'ctx')
- grad_input: bfloat16 [8, 8192, 1600], P('dp', 'ctx')
- grad_input_map: float32 [8, 8192, 16], P('dp', 'ctx')
- grad_output_map: float32 [8, 8192, 16], P('dp', 'ctx')
The draws below stay inside these ranges and needn't reach their ends.
Inputs may be any that keep to these rules, and one draw needn't show every extreme that they name: `windows`: some head's look-back is exactly 1024.
All inputs are finite; a program needn't handle non-finite values.
Results may differ from the reference program's by a relative error of at most 0.011.
Values may be sent and summed in bfloat16 or wider, within the bound.
A program may use at most 128 MiB of HBM per device.

```python
import jax
import jax.numpy as jnp
from jax import lax

HEADS = 25
KV_HEADS = 5
HEAD_DIM = 64
SSM_HEADS = 25
STATE = 16
META = 128
WINDOW = 1024
TOK_DEV = 128
SERIES_SPAN = 8192
SERIES_TOTAL = 8
WIDTH = 1600
KV_WIDTH = 320


def drawn_base(key):
    return jax.random.normal(jax.random.fold_in(key, 100), (SERIES_TOTAL, SERIES_SPAN, KV_WIDTH), jnp.float32)


def draw_key_vectors(key, part):
    common = drawn_base(key)
    key = jax.random.fold_in(key, 1)
    values = jax.random.normal(key, common.shape, jnp.float32)
    return jnp.clip(values, -24.0, 24.0).astype(jnp.bfloat16)


def draw_queries(key, part):
    common = drawn_base(key)
    key = jax.random.fold_in(key, 2)
    spread = jnp.repeat(common.reshape(SERIES_TOTAL, SERIES_SPAN, KV_HEADS, HEAD_DIM), HEADS // KV_HEADS, axis=2).reshape(SERIES_TOTAL, SERIES_SPAN, WIDTH)
    values = jax.random.normal(key, spread.shape, jnp.float32)
    return jnp.clip(values, -24.0, 24.0).astype(jnp.bfloat16)


def draw_windows(key, part):
    key = jax.random.fold_in(key, 7)
    first_key, second_key = jax.random.split(key)
    drawn = jax.random.randint(first_key, (HEADS,), 1, WINDOW + 1)
    chosen = jax.random.randint(second_key, (), 0, HEADS)
    return jnp.where(jnp.arange(HEADS) == chosen, WINDOW, drawn).astype(jnp.int32)


def draw_log_decay(key, part):
    key = jax.random.fold_in(key, 3)
    collected_lookup_vectors = jax.random.split(key, 7)
    chance = 0.5
    fast = jax.random.uniform(collected_lookup_vectors[0], (SSM_HEADS,)) < chance
    fast_rate = jnp.exp(jax.random.uniform(collected_lookup_vectors[1], (SSM_HEADS,), jnp.float32, jnp.log(1.0 / 50.0), jnp.log(1.0 / 30.0)))
    slow_rate = jnp.exp(jax.random.uniform(collected_lookup_vectors[2], (SSM_HEADS,), jnp.float32, jnp.log(0.05), jnp.log(0.25))) / SERIES_SPAN
    dilation_speed = jnp.where(fast, fast_rate, slow_rate)
    accelerator_shards = jnp.exp(jax.random.uniform(collected_lookup_vectors[3], (SERIES_TOTAL, SERIES_SPAN // TOK_DEV, SSM_HEADS), jnp.float32, jnp.log(0.7), jnp.log(1.4)))
    accelerator_shards = jnp.repeat(accelerator_shards, TOK_DEV, axis=1)
    position_shards = jax.random.uniform(collected_lookup_vectors[4], (SERIES_TOTAL, SERIES_SPAN, SSM_HEADS), jnp.float32, 0.5, 1.5)
    pulse_place = jax.random.randint(collected_lookup_vectors[5], (SERIES_TOTAL, 2), 0, SERIES_SPAN)
    pulse_level_within = jax.random.uniform(collected_lookup_vectors[6], (SERIES_TOTAL, 2), jnp.float32, jnp.log(0.5), jnp.log(0.8))
    place_array = jnp.arange(SERIES_SPAN, dtype=jnp.int32)
    dropped_elements = (place_array[None, :, None] == pulse_place[:, None, :]).astype(jnp.float32)
    pulse_span = jnp.sum(dropped_elements * pulse_level_within[:, None, :], axis=2)
    return -dilation_speed[None, None, :] * accelerator_shards * position_shards + pulse_span[:, :, None]


def steps_of(stream_key, dims, shards, least, largest):
    loudness, own = 1.0, jax.random.fold_in(stream_key, 6)
    for position, blocks in shards:
        draws = jnp.exp(jax.random.uniform(jax.random.fold_in(own, position), (blocks,), jnp.float32, least / len(shards), largest / len(shards)))
        loudness = loudness * jnp.repeat(draws, dims[position] // blocks).reshape([-1 if axis == position else 1 for axis in range(len(dims))])
    return loudness


def scatter_about(key, extent, width, most, cuts=(), kind=jnp.bfloat16):
    values = jax.random.normal(key, extent, jnp.float32) * width
    if len(cuts) > 0:
        values = steps_of(key, extent, cuts, -0.22, 0.18) * values
    return jnp.clip(values, min=-most, max=most).astype(kind)


def setup_inputs(seed: int = 0) -> dict:
    key_of = jax.random.split(jax.random.key(seed), 12)
    queries = draw_queries(jax.random.fold_in(key_of[11], 71), 0)
    key_vectors = draw_key_vectors(jax.random.fold_in(key_of[11], 71), 0)
    value_vectors = scatter_about(key_of[2], (SERIES_TOTAL, SERIES_SPAN, KV_WIDTH), 1.0, 6.0, ((0, 8), (1, 64)))
    meta_keys = scatter_about(key_of[3], (META, KV_WIDTH), 1.0, 6.0)
    meta_values = scatter_about(key_of[4], (META, KV_WIDTH), 1.0, 6.0)
    windows = draw_windows(jax.random.fold_in(key_of[11], 71), 0)
    ssm_input = scatter_about(key_of[6], (SERIES_TOTAL, SERIES_SPAN, WIDTH), 1.0, 6.0, ((0, 8), (1, 64)))
    input_map = scatter_about(key_of[7], (SERIES_TOTAL, SERIES_SPAN, STATE), 0.1, 0.59765625, ((0, 8), (1, 64)))
    output_map = scatter_about(key_of[8], (SERIES_TOTAL, SERIES_SPAN, STATE), 0.25, 1.5, ((0, 8), (1, 64)))
    log_decay = draw_log_decay(jax.random.fold_in(key_of[11], 71), 0)
    cotangent = scatter_about(key_of[10], (SERIES_TOTAL, SERIES_SPAN, WIDTH), 1.0, 6.0, ((0, 8), (1, 64)))
    return {"queries": queries, "key_vectors": key_vectors, "value_vectors": value_vectors, "meta_keys": meta_keys, "meta_values": meta_values, "windows": windows, "ssm_input": ssm_input, "input_map": input_map, "output_map": output_map, "log_decay": log_decay, "cotangent": cotangent}


def attend_block(query_blk, key_blk, value_blk, grad_blk, meta_key, meta_value, windows, query_start, key_start):
    score_scale = HEAD_DIM ** -0.5
    group = HEADS // KV_HEADS
    query_f = query_blk.astype(jnp.float32)
    key_f = jnp.repeat(key_blk.astype(jnp.float32), group, axis=1)
    value_f = jnp.repeat(value_blk.astype(jnp.float32), group, axis=1)
    grad_f = grad_blk.astype(jnp.float32)
    mkey_f = jnp.repeat(meta_key.astype(jnp.float32), group, axis=1)
    mvalue_f = jnp.repeat(meta_value.astype(jnp.float32), group, axis=1)
    scores = score_scale * jnp.einsum('qhe,khe->hqk', query_f, key_f)
    sink_scores = score_scale * jnp.einsum('qhe,mhe->hqm', query_f, mkey_f)
    query_pos = query_start + jnp.arange(query_blk.shape[0], dtype=jnp.int32)
    key_pos = key_start + jnp.arange(key_blk.shape[0], dtype=jnp.int32)
    distance = query_pos[:, None] - key_pos[None, :]
    valid = (distance[None] >= 0) & (distance[None] < windows[:, None, None]) & (key_pos[None, None, :] >= 0)
    row_max = jnp.maximum(jnp.max(jnp.where(valid, scores, -jnp.inf), axis=2), jnp.max(sink_scores, axis=2))
    row_total = jnp.sum(jnp.where(valid, jnp.exp(scores - row_max[:, :, None]), 0.0), axis=2)
    row_total = row_total + jnp.sum(jnp.exp(sink_scores - row_max[:, :, None]), axis=2)
    log_total = row_max + jnp.log(row_total)
    attention = jnp.where(valid, jnp.exp(scores - log_total[:, :, None]), 0.0)
    sink_attention = jnp.exp(sink_scores - log_total[:, :, None])
    attention_half = lax.optimization_barrier(attention.astype(jnp.bfloat16)).astype(jnp.float32)
    sink_half = lax.optimization_barrier(sink_attention.astype(jnp.bfloat16)).astype(jnp.float32)
    attended = jnp.einsum('hqk,khe->qhe', attention_half, value_f) + jnp.einsum('hqm,mhe->qhe', sink_half, mvalue_f)
    delta_row = jnp.einsum('qhe,qhe->hq', grad_f, attended)
    grad_attention = jnp.einsum('qhe,khe->hqk', grad_f, value_f)
    grad_sink = jnp.einsum('qhe,mhe->hqm', grad_f, mvalue_f)
    dscores = attention * (grad_attention - delta_row[:, :, None])
    dscores = lax.optimization_barrier(dscores.astype(jnp.bfloat16)).astype(jnp.float32)
    dsink = sink_attention * (grad_sink - delta_row[:, :, None])
    dsink = lax.optimization_barrier(dsink.astype(jnp.bfloat16)).astype(jnp.float32)
    grad_q = score_scale * (jnp.einsum('hqk,khe->qhe', dscores, key_f) + jnp.einsum('hqm,mhe->qhe', dsink, mkey_f))
    grad_k = score_scale * jnp.einsum('hqk,qhe->khe', dscores, query_f)
    grad_v = jnp.einsum('hqk,qhe->khe', attention_half, grad_f)
    grad_mk = score_scale * jnp.einsum('hqm,qhe->mhe', dsink, query_f)
    grad_mv = jnp.einsum('hqm,qhe->mhe', sink_half, grad_f)

    def fold_group(term):
        return jnp.sum(term.reshape(term.shape[0], KV_HEADS, group, HEAD_DIM), axis=2)

    return grad_q, fold_group(grad_k), fold_group(grad_v), fold_group(grad_mk), fold_group(grad_mv)


def attention_sequence(seq_items, meta_key, meta_value, windows):
    queries_s, keys_s, values_s, grads_s = seq_items
    zeros_front = jnp.zeros((WINDOW, KV_WIDTH), keys_s.dtype)
    keys_pad = jnp.concatenate([zeros_front, keys_s], axis=0)
    values_pad = jnp.concatenate([zeros_front, values_s], axis=0)
    span_len = WINDOW + TOK_DEV

    def travel(term):
        flat = term.reshape(span_len, KV_WIDTH)
        halo_part = lax.optimization_barrier(flat[:WINDOW].astype(jnp.bfloat16)).astype(jnp.float32)
        return jnp.concatenate([halo_part, flat[WINDOW:]], axis=0)

    def block_step(running_sum, block_index):
        acc_keys, acc_values, acc_mkeys, acc_mvalues = running_sum
        start_pos = block_index * TOK_DEV
        query_blk = lax.dynamic_slice_in_dim(queries_s, start_pos, TOK_DEV, 0).reshape(TOK_DEV, HEADS, HEAD_DIM)
        grad_blk = lax.dynamic_slice_in_dim(grads_s, start_pos, TOK_DEV, 0).reshape(TOK_DEV, HEADS, HEAD_DIM)
        key_blk = lax.dynamic_slice_in_dim(keys_pad, start_pos, span_len, 0).reshape(span_len, KV_HEADS, HEAD_DIM)
        value_blk = lax.dynamic_slice_in_dim(values_pad, start_pos, span_len, 0).reshape(span_len, KV_HEADS, HEAD_DIM)
        grad_q, grad_k, grad_v, grad_mk, grad_mv = attend_block(query_blk, key_blk, value_blk, grad_blk, meta_key, meta_value, windows, start_pos, start_pos - WINDOW)
        old_keys = lax.dynamic_slice_in_dim(acc_keys, start_pos, span_len, 0)
        acc_keys = lax.dynamic_update_slice_in_dim(acc_keys, old_keys + travel(grad_k), start_pos, 0)
        old_values = lax.dynamic_slice_in_dim(acc_values, start_pos, span_len, 0)
        acc_values = lax.dynamic_update_slice_in_dim(acc_values, old_values + travel(grad_v), start_pos, 0)
        new_sum = (acc_keys, acc_values, acc_mkeys + grad_mk, acc_mvalues + grad_mv)
        return new_sum, grad_q.reshape(TOK_DEV, WIDTH).astype(jnp.bfloat16)

    begin = (jnp.zeros((SERIES_SPAN + WINDOW, KV_WIDTH), jnp.float32), jnp.zeros((SERIES_SPAN + WINDOW, KV_WIDTH), jnp.float32),
             jnp.zeros((META, KV_HEADS, HEAD_DIM), jnp.float32), jnp.zeros((META, KV_HEADS, HEAD_DIM), jnp.float32))
    final, grad_queries = lax.scan(block_step, begin, jnp.arange(SERIES_SPAN // TOK_DEV, dtype=jnp.int32))
    return (grad_queries.reshape(SERIES_SPAN, WIDTH), final[0][WINDOW:].astype(jnp.bfloat16),
            final[1][WINDOW:].astype(jnp.bfloat16), final[2], final[3])


def ssm_prepare(b_blk, c_blk, d_blk):
    running = jnp.cumsum(d_blk, axis=0)
    block_end = running[-1]
    order_pos = jnp.arange(TOK_DEV, dtype=jnp.int32)
    causal = order_pos[:, None] >= order_pos[None, :]
    running_t = running.T
    mixing = jnp.where(causal[None], jnp.exp(running_t[:, :, None] - running_t[:, None, :]), 0.0)
    inner_prod = jnp.dot(c_blk, b_blk.T, preferred_element_type=jnp.float32)
    weights = (mixing * inner_prod[None]).astype(jnp.bfloat16)
    tail_decay = jnp.exp(block_end[None, :] - running)
    head_decay = jnp.exp(running)
    inject = (tail_decay[:, :, None] * b_blk.astype(jnp.float32)[:, None, :]).astype(jnp.bfloat16)
    readout = (head_decay[:, :, None] * c_blk.astype(jnp.float32)[:, None, :]).astype(jnp.bfloat16)
    return running, mixing, weights, tail_decay, head_decay, inject, readout


def ssm_summaries(block_items):
    x_blk, g_blk, b_blk, c_blk, d_blk = block_items
    running, mixing, weights, tail_decay, head_decay, inject, readout = ssm_prepare(b_blk, c_blk, d_blk)
    inject_f = lax.optimization_barrier(inject).astype(jnp.float32)
    readout_f = lax.optimization_barrier(readout).astype(jnp.float32)
    block_state = jnp.einsum('lhn,lhp->hpn', inject_f, x_blk.astype(jnp.float32))
    block_adjoint = jnp.einsum('lhn,lhp->hpn', readout_f, g_blk.astype(jnp.float32))
    return jnp.exp(running[-1]), block_state, block_adjoint


def ssm_grads(block_items):
    x_blk, g_blk, b_blk, c_blk, d_blk, incoming, adjoint = block_items
    running, mixing, weights, tail_decay, head_decay, inject, readout = ssm_prepare(b_blk, c_blk, d_blk)
    x_f = x_blk.astype(jnp.float32)
    g_f = g_blk.astype(jnp.float32)
    weights_f = lax.optimization_barrier(weights).astype(jnp.float32)
    local_input = jnp.einsum('hts,thp->shp', weights_f, g_f)
    pair_prod = jnp.einsum('thp,shp->hts', g_f, x_f)
    grad_gram = jnp.sum(mixing * pair_prod, axis=0).astype(jnp.bfloat16)
    input_local = jnp.dot(grad_gram.T, c_blk, preferred_element_type=jnp.float32)
    output_local = jnp.dot(grad_gram, b_blk, preferred_element_type=jnp.float32)
    inject_f = lax.optimization_barrier(inject).astype(jnp.float32)
    carried_input = jnp.einsum('lhn,hpn->lhp', inject_f, adjoint, precision=lax.Precision.HIGHEST)
    input_carried = jnp.sum(tail_decay[:, :, None] * jnp.einsum('lhp,hpn->lhn', x_f, adjoint, precision=lax.Precision.HIGHEST), axis=1)
    output_carried = jnp.sum(head_decay[:, :, None] * jnp.einsum('lhp,hpn->lhn', g_f, incoming, precision=lax.Precision.HIGHEST), axis=1)
    grad_in = (local_input + carried_input).reshape(TOK_DEV, SSM_HEADS * HEAD_DIM).astype(jnp.bfloat16)
    return grad_in, input_local + input_carried, output_local + output_carried


def ssm_sequence(seq_items):
    inputs_s, bmap_s, cmap_s, decay_s, grads_s = seq_items
    blocks = SERIES_SPAN // TOK_DEV
    x_blocks = inputs_s.reshape(blocks, TOK_DEV, SSM_HEADS, HEAD_DIM)
    g_blocks = grads_s.reshape(blocks, TOK_DEV, SSM_HEADS, HEAD_DIM)
    b_blocks = bmap_s.reshape(blocks, TOK_DEV, STATE)
    c_blocks = cmap_s.reshape(blocks, TOK_DEV, STATE)
    d_blocks = decay_s.reshape(blocks, TOK_DEV, SSM_HEADS)
    decays, states, adjoints = lax.map(ssm_summaries, (x_blocks, g_blocks, b_blocks, c_blocks, d_blocks))

    def carry_step(state_now, pair_items):
        block_decay, block_term = pair_items
        return block_decay[:, None, None] * state_now + block_term, state_now

    zero_state = jnp.zeros((SSM_HEADS, HEAD_DIM, STATE), jnp.float32)
    final_state, incoming = lax.scan(carry_step, zero_state, (decays, states))
    first_adjoint, adjoint = lax.scan(carry_step, zero_state, (decays, adjoints), reverse=True)
    grad_in, grad_b, grad_c = lax.map(ssm_grads, (x_blocks, g_blocks, b_blocks, c_blocks, d_blocks, incoming, adjoint))
    return grad_in.reshape(SERIES_SPAN, SSM_HEADS * HEAD_DIM), grad_b.reshape(SERIES_SPAN, STATE), grad_c.reshape(SERIES_SPAN, STATE)


def reference(queries, key_vectors, value_vectors, meta_keys, meta_values, windows, ssm_input, input_map, output_map, log_decay, cotangent):
    meta_key = meta_keys.reshape(META, KV_HEADS, HEAD_DIM)
    meta_value = meta_values.reshape(META, KV_HEADS, HEAD_DIM)

    def attention_map(seq_items):
        return attention_sequence(seq_items, meta_key, meta_value, windows)

    grad_queries, grad_keys, grad_values, mkeys_all, mvalues_all = lax.map(attention_map, (queries, key_vectors, value_vectors, cotangent))
    grad_meta = jnp.stack([jnp.sum(mkeys_all, axis=0).reshape(META, KV_WIDTH), jnp.sum(mvalues_all, axis=0).reshape(META, KV_WIDTH)])
    grad_input, grad_input_map, grad_output_map = lax.map(ssm_sequence, (ssm_input, input_map, output_map, log_decay, cotangent))
    return grad_queries, grad_keys, grad_values, grad_meta, grad_input, grad_input_map, grad_output_map
```

```python
import functools

import jax
import jax.numpy as jnp
from jax import lax
from jax.experimental import pallas as pl
from jax.experimental.pallas import tpu as pltpu
from jax.sharding import PartitionSpec as P

BF = jnp.bfloat16
F32 = jnp.float32
MESH = pl.DeviceIdType.MESH
HEADS, KVH, GROUP, HD = 25, 5, 5, 64
TOK, WIDTH, KVW, STATE = 128, 1600, 320, 16
QL = 448
NT = (((1,), (1,)), ((), ()))
TN = (((0,), (0,)), ((), ()))


def dot(a, b, dims=(((1,), (0,)), ((), ()))):
    return lax.dot_general(a, b, dims, preferred_element_type=F32)


def split3(v):
    hi = v.astype(BF)
    rest = v - hi.astype(F32)
    mid = rest.astype(BF)
    low = (rest - mid.astype(F32)).astype(BF)
    return hi, mid, low


def dot3(v, onehot):
    hi, mid, low = split3(v)
    return dot(hi, onehot) + dot(mid, onehot) + dot(low, onehot)


def iota(shape, dim):
    return lax.broadcasted_iota(jnp.int32, shape, dim)


def places():
    dp, i = lax.axis_index("dp"), lax.axis_index("ctx")
    return dp, i, i % 2, (i // 2) % 2, i // 4


def ctx_kernel(
    key, val, x, g, bm, cm, ld,
    win, gin, gbm, gcm,
    own, xt, gt, texp, loc, stq, r1, d0, d1, s2, r2, d2s, d2, s3, r3, d3s, d3, ib, ob, inc, adj,
    own_sem, kv_send, kv_recv, c_send, c_recv, q1_send, q1_recv, q2_send, q2_recv, q3_send, q3_recv, q4_send, q4_recv,
):
    dp, i, core, yh, z = places()
    c = i % 4
    zl, zh = z % 4, z // 4
    up = ((z + 1) % 16) * 4 + c
    down = ((z + 15) % 16) * 4 + c
    base = i - c
    group = [base + (c + k) % 4 for k in (1, 2, 3)]
    near = [(zh * 4 + (zl + k) % 4) * 4 + c for k in (1, 2, 3)]
    far = [(((zh + k) % 4) * 4 + zl) * 4 + c for k in (1, 2, 3)]
    mate = base + (c + 1 - 2 * core)
    across = base + (c + 2) % 4

    barrier = pltpu.get_barrier_semaphore()
    for to in group + near + far + [down]:
        pl.semaphore_signal(barrier, inc=1, device_id=(dp, to), device_id_type=MESH)

    for k in range(KVH):
        own[k, :, 0:HD] = key[:, HD * k : HD * k + HD]
        own[k, :, HD : 2 * HD] = val[:, HD * k : HD * k + HD]
    pl.semaphore_wait(barrier, 10)

    def kv_copy(src, dst_slot, n, to):
        return pltpu.make_async_remote_copy(
            src_ref=src, dst_ref=win.at[dst_slot], send_sem=kv_send.at[n], recv_sem=kv_recv.at[n],
            device_id=(dp, to), device_id_type=MESH,
        )

    def mate_copy(src, d, n):
        there = (d + core * 9 + (1 - core)) % 10
        return pltpu.make_async_remote_copy(
            src_ref=src, dst_ref=win.at[there], send_sem=c_send.at[n], recv_sem=c_recv.at[n],
            device_id=(dp, mate), device_id_type=MESH,
        )

    keep = pltpu.make_async_copy(own, win.at[0], own_sem)
    step_a = kv_copy(own, 4, 0, up)
    step_y0 = kv_copy(own, 2, 1, across)
    step_y1 = kv_copy(win.at[4], 2, 1, across)
    step_b = kv_copy(win.at[2], 6, 2, up)
    step_c = kv_copy(win.at[4], 8, 3, up)
    mates = [mate_copy(own, 0, 0)] + [mate_copy(win.at[d], d, n + 1) for n, d in enumerate((4, 2, 8, 6))]
    step_a.start()

    @pl.when(yh == 0)
    def _():
        step_y0.start()

    keep.start()
    mates[0].start()

    rows, cols = iota((TOK, TOK), 0), iota((TOK, TOK), 1)
    tri = (rows >= cols).astype(BF)
    run = jnp.zeros((TOK, TOK), F32)
    ldv = jnp.concatenate([ld[...], jnp.zeros((TOK, TOK - HEADS), F32)], axis=1)
    for part in split3(ldv):
        run = run + dot(tri, part)
    run_t = run.T
    end = run[TOK - 1 : TOK, :]
    spread = (iota((32, WIDTH), 0) == iota((32, WIDTH), 1) // HD).astype(BF)
    tail_x = dot(jnp.exp(end - run)[:, :32].astype(BF), spread)
    texp[...] = tail_x
    xt[...] = (tail_x * x[...].astype(F32)).astype(BF)
    gt[...] = (dot(jnp.exp(run)[:, :32].astype(BF), spread) * g[...].astype(F32)).astype(BF)
    for w, terms in enumerate((dot(bm[...], xt[...], TN), dot(cm[...], gt[...], TN))):
        for q in range(4):
            n = min(QL, WIDTH - QL * q)
            stq[q, w] = jnp.concatenate(
                [terms[:, QL * q : QL * q + n], jnp.zeros((STATE, 512 - n), F32)], axis=1
            ).astype(BF)
    d0[...] = jnp.exp(jnp.broadcast_to(end, (8, TOK)))

    def pair(src, dst, send, recv, n, to):
        return pltpu.make_async_remote_copy(
            src_ref=src, dst_ref=dst, send_sem=send.at[n], recv_sem=recv.at[n],
            device_id=(dp, to), device_id_type=MESH,
        )

    q1 = []
    for n, k in enumerate((1, 2, 3)):
        q1.append(pair(stq.at[(c + k) % 4], r1.at[c], q1_send, q1_recv, n, group[n]))
        q1.append(pair(d0, d1.at[c], q1_send, q1_recv, 3 + n, group[n]))
    for copy in q1:
        copy.start()
    r1[c] = stq[c]
    d1[c] = d0[...]

    step_a.wait_recv()
    step_c.start()

    @pl.when(yh == 1)
    def _():
        step_y1.start()

    mates[1].start()

    row, lane = iota((32, 512), 0), iota((32, 512), 1)
    onehot = ((row == 7 * c + lane // HD) & (lane < QL)).astype(BF)

    def expand(d):
        wide = dot3(d[...].reshape(32, TOK)[:, :32], onehot)
        return [jnp.broadcast_to(wide[8 * j : 8 * j + 1], (STATE, 512)) for j in range(4)]

    for copy in q1:
        copy.wait_recv()
    dec1 = expand(d1)
    st1 = [r1[j, 0].astype(F32) for j in range(4)]
    ad1 = [r1[j, 1].astype(F32) for j in range(4)]
    total = st1[0]
    back = ad1[3]
    for j in range(1, 4):
        total = dec1[j] * total + st1[j]
        back = dec1[3 - j] * back + ad1[3 - j]
    s2[0] = total.astype(BF)
    s2[1] = back.astype(BF)
    d2s[...] = d1[0] * d1[1] * d1[2] * d1[3]
    q2 = []
    for n in range(3):
        q2.append(pair(s2, r2.at[zl], q2_send, q2_recv, n, near[n]))
        q2.append(pair(d2s, d2.at[zl], q2_send, q2_recv, 3 + n, near[n]))
    for copy in q2:
        copy.start()
    r2[zl] = s2[...]
    d2[zl] = d2s[...]

    inner_t = dot(bm[...], cm[...], NT)
    gram_t = jnp.zeros((TOK, TOK), F32)

    def local_head(h, gram_t):
        xh, gh = x[:, HD * h : HD * h + HD], g[:, HD * h : HD * h + HD]
        diff = run_t[h : h + 1, :] - run[:, h : h + 1]
        mix = jnp.where(cols >= rows, jnp.exp(diff), 0.0)
        loc[:, HD * h : HD * h + HD] = dot((mix * inner_t).astype(BF), gh)
        return gram_t + mix * dot(xh, gh, NT)

    for h in range(0, 13):
        gram_t = local_head(h, gram_t)

    step_y1.wait_recv()
    step_b.start()
    mates[2].start()

    for copy in q2:
        copy.wait_recv()
    dec2 = expand(d2)
    st2 = [r2[j, 0].astype(F32) for j in range(4)]
    ad2 = [r2[j, 1].astype(F32) for j in range(4)]
    total = st2[0]
    back = ad2[3]
    for j in range(1, 4):
        total = dec2[j] * total + st2[j]
        back = dec2[3 - j] * back + ad2[3 - j]
    s3[0] = total.astype(BF)
    s3[1] = back.astype(BF)
    d3s[...] = d2[0] * d2[1] * d2[2] * d2[3]
    q3 = []
    for n, k in enumerate((1, 2, 3)):
        there = (zh + k) % 4
        which = jnp.where(there > zh, 0, 1)
        q3.append(pair(s3.at[which], r3.at[zh], q3_send, q3_recv, n, far[n]))
        q3.append(pair(d3s, d3.at[zh], q3_send, q3_recv, 3 + n, far[n]))
    for copy in q3:
        copy.start()
    r3[zh] = s3[0]
    d3[zh] = d3s[...]

    for h in range(13, HEADS):
        gram_t = local_head(h, gram_t)
    gram_t = gram_t.astype(BF)
    in_local = dot(gram_t, cm[...])
    out_local = dot(gram_t, bm[...], TN)

    step_c.wait_recv()
    mates[3].start()
    step_b.wait_recv()
    mates[4].start()

    for copy in q3:
        copy.wait_recv()
    dec3 = expand(d3)
    zero = jnp.zeros((STATE, 512), F32)
    ahead, behind = zero, zero
    for j in range(4):
        ahead = jnp.where(j < zh, dec3[j] * ahead + r3[j].astype(F32), ahead)
        b = 3 - j
        behind = jnp.where(b > zh, dec3[b] * behind + r3[b].astype(F32), behind)
    for j in range(4):
        ahead = jnp.where(j < zl, dec2[j] * ahead + st2[j], ahead)
        b = 3 - j
        behind = jnp.where(b > zl, dec2[b] * behind + ad2[b], behind)
    for j in range(4):
        ib[j, 0] = ahead.astype(BF)
        ahead = dec1[j] * ahead + st1[j]
        b = 3 - j
        ib[b, 1] = behind.astype(BF)
        behind = dec1[b] * behind + ad1[b]
    q4 = [
        pair(ib.at[(c + k) % 4], ob.at[c], q4_send, q4_recv, n, group[n]) for n, k in enumerate((1, 2, 3))
    ]
    for copy in q4:
        copy.start()
    ob[c] = ib[c]
    for copy in q4:
        copy.wait_recv()
    for q in range(4):
        n = min(QL, WIDTH - QL * q)
        inc[:, QL * q : QL * q + n] = ob[q, 0].astype(F32)[:, :n]
        adj[:, QL * q : QL * q + n] = ob[q, 1].astype(F32)[:, :n]
    inc_h, adj_h = inc[...].astype(BF), adj[...].astype(BF)
    gin[...] = (loc[...] + texp[...] * dot(bm[...], adj_h)).astype(BF)
    gbm[...] = in_local + dot(xt[...], adj_h, NT)
    gcm[...] = out_local + dot(gt[...], inc_h, NT)

    keep.wait()
    for copy in mates:
        copy.wait_recv()
        copy.wait_send()
    for copy in [step_a, step_y1, step_b, step_c] + q1 + q2 + q3 + q4:
        copy.wait_send()


def run_ctx(key, val, x, g, bm, cm, ld):
    dma = pltpu.SemaphoreType.DMA
    vm = pltpu.VMEM
    return pl.pallas_call(
        ctx_kernel,
        out_shape=(
            jax.ShapeDtypeStruct((10, KVH, TOK, TOK), BF),
            jax.ShapeDtypeStruct((TOK, WIDTH), BF),
            jax.ShapeDtypeStruct((TOK, STATE), F32),
            jax.ShapeDtypeStruct((TOK, STATE), F32),
        ),
        in_specs=[pl.BlockSpec(memory_space=vm)] * 7,
        out_specs=(pl.BlockSpec(memory_space=pl.ANY),) + (pl.BlockSpec(memory_space=vm),) * 3,
        scratch_shapes=[
            vm((KVH, TOK, TOK), BF),
            vm((TOK, WIDTH), BF),
            vm((TOK, WIDTH), BF),
            vm((TOK, WIDTH), F32),
            vm((TOK, WIDTH), F32),
            vm((4, 2, STATE, 512), BF),
            vm((4, 2, STATE, 512), BF),
            vm((8, TOK), F32),
            vm((4, 8, TOK), F32),
            vm((2, STATE, 512), BF),
            vm((4, 2, STATE, 512), BF),
            vm((8, TOK), F32),
            vm((4, 8, TOK), F32),
            vm((2, STATE, 512), BF),
            vm((4, STATE, 512), BF),
            vm((8, TOK), F32),
            vm((4, 8, TOK), F32),
            vm((4, 2, STATE, 512), BF),
            vm((4, 2, STATE, 512), BF),
            vm((STATE, WIDTH), F32),
            vm((STATE, WIDTH), F32),
            dma,
            dma((4,)), dma((4,)), dma((5,)), dma((5,)),
            dma((6,)), dma((6,)), dma((6,)), dma((6,)), dma((6,)), dma((6,)), dma((3,)), dma((3,)),
        ],
        compiler_params=pltpu.CompilerParams(
            collective_id=0, has_side_effects=True, vmem_limit_bytes=40 * 1024 * 1024
        ),
        name="halo_and_scan",
    )(key, val, x, g, bm, cm, ld)


def attention_kernel(wins, qs, gs, win, mk, mv, gq, pieces, own, sink, qg, metas, dist, ps, dqs):
    i = lax.axis_index("ctx")
    zeros = jnp.zeros((TOK, HD), BF)
    for k in range(KVH):
        metas[k, :, 0:HD] = mk[:, HD * k : HD * k + HD]
        metas[k, :, HD : 2 * HD] = mv[:, HD * k : HD * k + HD]
        for j in range(GROUP):
            h = GROUP * k + j
            top = 2 * TOK * j
            qg[k, top : top + TOK, 0:HD] = (qs[:, HD * h : HD * h + HD].astype(F32) * 0.125).astype(BF)
            qg[k, top : top + TOK, HD : 2 * HD] = zeros
            qg[k, top + TOK : top + 2 * TOK, 0:HD] = zeros
            qg[k, top + TOK : top + 2 * TOK, HD : 2 * HD] = gs[:, HD * h : HD * h + HD]
    back = iota((TOK, TOK), 0) - iota((TOK, TOK), 1)
    never = jnp.int32(1 << 20)
    dist[:, 0:TOK] = jnp.zeros((TOK, TOK), jnp.int32)
    dist[:, TOK : 2 * TOK] = jnp.where(back >= 0, back, never)
    for d in range(1, 9):
        dist[:, TOK * (d + 1) : TOK * (d + 2)] = jnp.where(i >= d, back + TOK * d, never)
    pieces[0] = jnp.zeros((KVH, TOK, TOK), BF)
    pieces[9] = jnp.zeros((KVH, TOK, TOK), BF)

    def one(k, carry):
        kv = jnp.concatenate([metas[k], win[0:9, k].reshape(9 * TOK, TOK)], axis=0)
        for j in range(GROUP):
            h = GROUP * k + j
            top = 2 * TOK * j
            both = dot(qg[k, top : top + 2 * TOK, :], kv, NT)
            s, dp = both[:TOK], both[TOK:]
            s = jnp.where(dist[...] < wins[h], s, -1e30)
            e = jnp.exp(s - jnp.max(s, axis=1, keepdims=True))
            inv = 1.0 / jnp.sum(e, axis=1, keepdims=True)
            delta = jnp.sum(e * dp, axis=1, keepdims=True) * inv
            p = e * inv
            ds = (p * (dp - delta)).astype(BF)
            ps[top : top + TOK, :] = ds
            ps[top + TOK : top + 2 * TOK, :] = p.astype(BF)
            dqs[h] = dot(ds, kv)
        back_t = dot(qg[k], ps[...], TN)
        turned = back_t[:, :TOK].T
        sink[:, k] = turned.reshape(16, 8, TOK)
        own[k] = back_t[:, TOK : 2 * TOK]
        for d in range(1, 9):
            pieces[d, k] = back_t[:, TOK * (d + 1) : TOK * (d + 2)].astype(BF)
        return carry

    lax.fori_loop(0, KVH, one, 0)
    for h in range(HEADS):
        gq[:, HD * h : HD * h + HD] = (dqs[h, :, 0:HD] * 0.125).astype(BF)


def run_attention(windows, q, g, win, mk, mv):
    vm = pltpu.VMEM
    return pl.pallas_call(
        attention_kernel,
        out_shape=(
            jax.ShapeDtypeStruct((TOK, WIDTH), BF),
            jax.ShapeDtypeStruct((10, KVH, TOK, TOK), BF),
            jax.ShapeDtypeStruct((KVH, TOK, TOK), F32),
            jax.ShapeDtypeStruct((16, KVH, 8, TOK), F32),
        ),
        in_specs=[pl.BlockSpec(memory_space=pltpu.SMEM)] + [pl.BlockSpec(memory_space=vm)] * 5,
        out_specs=(pl.BlockSpec(memory_space=vm),) * 4,
        scratch_shapes=[
            vm((KVH, 2 * TOK * GROUP, TOK), BF),
            vm((KVH, TOK, TOK), BF),
            vm((TOK, 10 * TOK), jnp.int32),
            vm((2 * TOK * GROUP, 10 * TOK), BF),
            vm((HEADS, TOK, TOK), F32),
        ],
        compiler_params=pltpu.CompilerParams(vmem_limit_bytes=48 * 1024 * 1024),
        name="attention_grads",
    )(windows, q, g, win, mk, mv)


def grad_kernel(
    pieces, own, sink, gk, gv, gm,
    rc, ry, rz, sc, sb, sy, sa, k0, a0, k1, a1, k2, a2, k3, a3, k4, a4, k5,
    c_send, c_recv, kv_send, kv_recv, m_send, m_recv,
):
    dp, i, core, yh, z = places()
    c = i % 4
    zl, zh = z % 4, z // 4
    xx, yl = dp % 4, dp // 4
    up = ((z + 1) % 16) * 4 + c
    down = ((z + 15) % 16) * 4 + c
    base = i - c
    mate = base + (c + 1 - 2 * core)
    across = base + (c + 2) % 4
    near = [(dp, (zh * 4 + (zl + k) % 4) * 4 + c) for k in (1, 2, 3)]
    far = [(dp, (((zh + k) % 4) * 4 + zl) * 4 + c) for k in (1, 2, 3)]
    along_x = [(yl * 4 + (xx + k) % 4, i) for k in (1, 2, 3)]
    other = (1 - yl) * 4 + xx
    along_y = [(dp, across), (other, i), (other, across)]

    barrier = pltpu.get_barrier_semaphore()
    for to in [(dp, mate), (dp, up)] + near + far + along_x + along_y:
        pl.semaphore_signal(barrier, inc=1, device_id=to, device_id_type=MESH)
    pl.semaphore_wait(barrier, 14)

    def pair(src, dst, send, recv, n, to):
        return pltpu.make_async_remote_copy(
            src_ref=src, dst_ref=dst, send_sem=send.at[n], recv_sem=recv.at[n],
            device_id=to, device_id_type=MESH,
        )

    order = (8, 6, 2, 4, 0)
    mates = [
        pair(pieces.at[(d + core + 9 * (1 - core)) % 10], rc.at[n], c_send, c_recv, n, (dp, mate))
        for n, d in enumerate(order)
    ]
    for copy in mates[:2]:
        copy.start()
    m0 = pair(sink.at[1 - core], k0, m_send, m_recv, 0, (dp, mate))
    m0.start()
    for copy in mates[2:]:
        copy.start()

    step_c = pair(sc, rz.at[0], kv_send, kv_recv, 0, (dp, down))
    step_b = pair(sb, rz.at[1], kv_send, kv_recv, 1, (dp, down))
    step_y = pair(sy, ry, kv_send, kv_recv, 2, (dp, across))
    step_a = pair(sa, rz.at[2], kv_send, kv_recv, 3, (dp, down))

    mates[0].wait_recv()
    sc[...] = (pieces[8].astype(F32) + rc[0].astype(F32)).astype(BF)
    step_c.start()
    mates[1].wait_recv()
    sb[...] = (pieces[6].astype(F32) + rc[1].astype(F32)).astype(BF)
    step_b.start()

    m0.wait_recv()
    a0[...] = sink[core] + k0[...]
    m1 = [pair(a0.at[(xx + k) % 4], k1.at[n], m_send, m_recv, 1 + n, along_x[n]) for n, k in enumerate((1, 2, 3))]
    for copy in m1:
        copy.start()

    mates[2].wait_recv()
    sum_y = pieces[2].astype(F32) + rc[2].astype(F32)
    step_b.wait_recv()
    sy[...] = (sum_y + rz[1].astype(F32)).astype(BF)
    step_y.start()

    for copy in m1:
        copy.wait_recv()
    a1[...] = a0[xx] + k1[0] + k1[1] + k1[2]
    m2 = [
        pair(a1.at[yl if n == 0 else 1 - yl], k2.at[n], m_send, m_recv, 4 + n, along_y[n]) for n in range(3)
    ]
    for copy in m2:
        copy.start()

    mates[3].wait_recv()
    step_c.wait_recv()
    mates[4].wait_recv()

    for copy in m2:
        copy.wait_recv()
    a2[...] = a1[yl] + k2[0] + k2[1] + k2[2]
    m3 = [pair(a2, k3.at[n], m_send, m_recv, 7 + n, near[n]) for n in range(3)]
    for copy in m3:
        copy.start()

    step_y.wait_recv()
    here = jnp.where(yh == 1, 1.0, 0.0)
    sum_a = pieces[4].astype(F32) + rc[3].astype(F32) + rz[0].astype(F32)
    sa[...] = (sum_a + here * ry[...].astype(F32)).astype(BF)
    step_a.start()

    for copy in m3:
        copy.wait_recv()
    a3[...] = a2[...] + k3[0] + k3[1] + k3[2]
    m4 = [pair(a3, k4.at[n], m_send, m_recv, 10 + n, far[n]) for n in range(3)]
    for copy in m4:
        copy.start()
    mine = own[...] + rc[4].astype(F32) + (1.0 - here) * ry[...].astype(F32)
    for copy in m4:
        copy.wait_recv()
    a4[...] = a3[...] + k4[0] + k4[1] + k4[2]
    m5 = pair(a4, k5, m_send, m_recv, 13, (dp, mate))
    m5.start()

    step_a.wait_recv()
    mine = mine + rz[2].astype(F32)
    for k in range(KVH):
        turned = mine[k].T
        gk[:, HD * k : HD * k + HD] = turned[:, :HD].astype(BF)
        gv[:, HD * k : HD * k + HD] = turned[:, HD:].astype(BF)

    m5.wait_recv()
    lane, col = iota((TOK, TOK), 0), iota((TOK, TOK), 1)
    first = jnp.zeros((8, TOK), F32)
    second = jnp.zeros((8, TOK), F32)
    for k in range(KVH):
        feature = 5 * i + col % 8 - HD * k
        pick = (col % 8 < 5) & (col < 16) & (feature >= 0) & (feature < HD) & (lane == feature + HD * (col // 8))
        pick = pick.astype(BF)
        mine_k, other_k = a4[k], k5[k]
        first = first + dot3(mine_k, pick)
        second = second + dot3(other_k, pick)
    top = jnp.where(core == 0, first, second)
    low = jnp.where(core == 0, second, first)
    gm[0, 0:8] = top[:, 0:5]
    gm[0, 8:16] = low[:, 0:5]
    gm[1, 0:8] = top[:, 8:13]
    gm[1, 8:16] = low[:, 8:13]

    for copy in mates + [m0, step_a, step_b, step_c, step_y] + m1 + m2 + m3 + m4 + [m5]:
        copy.wait_send()


def run_grads(pieces, own, sink):
    dma = pltpu.SemaphoreType.DMA
    vm = pltpu.VMEM
    block = (KVH, TOK, TOK)
    part = (KVH, 8, TOK)
    return pl.pallas_call(
        grad_kernel,
        out_shape=(
            jax.ShapeDtypeStruct((TOK, KVW), BF),
            jax.ShapeDtypeStruct((TOK, KVW), BF),
            jax.ShapeDtypeStruct((2, 16, 5), F32),
        ),
        in_specs=[pl.BlockSpec(memory_space=vm)] * 3,
        out_specs=(pl.BlockSpec(memory_space=vm),) * 3,
        scratch_shapes=[
            vm((5,) + block, BF), vm(block, BF), vm((3,) + block, BF),
            vm(block, BF), vm(block, BF), vm(block, BF), vm(block, BF),
            vm((4, 2) + part, F32), vm((4, 2) + part, F32),
            vm((3, 2) + part, F32), vm((2,) + part, F32),
            vm((3,) + part, F32), vm(part, F32),
            vm((3,) + part, F32), vm(part, F32),
            vm((3,) + part, F32), vm(part, F32),
            vm(part, F32),
            dma((5,)), dma((5,)), dma((4,)), dma((4,)), dma((14,)), dma((14,)),
        ],
        compiler_params=pltpu.CompilerParams(
            collective_id=1, has_side_effects=True, vmem_limit_bytes=40 * 1024 * 1024
        ),
        name="gradient_sums",
    )(pieces, own, sink)


def local(
    queries, key_vectors, value_vectors, meta_keys, meta_values, windows,
    ssm_input, input_map, output_map, log_decay, cotangent,
):
    win, grad_input, grad_bm, grad_cm = run_ctx(
        key_vectors[0], value_vectors[0], ssm_input[0], cotangent[0], input_map[0], output_map[0], log_decay[0]
    )
    grad_q, pieces, own, sink = run_attention(windows, queries[0], cotangent[0], win, meta_keys, meta_values)
    sink = sink.reshape(2, 4, 2, KVH, 8, TOK).transpose(2, 1, 0, 3, 4, 5)
    grad_k, grad_v, grad_meta = run_grads(pieces, own, sink)
    return (
        grad_q[None], grad_k[None], grad_v[None], grad_meta, grad_input[None], grad_bm[None], grad_cm[None],
    )


def solution(mesh):
    seq = P("dp", "ctx", None)
    return jax.shard_map(
        local,
        mesh=mesh,
        in_specs=(seq, seq, seq, P(), P(), P(), seq, seq, seq, seq, seq),
        out_specs=(seq, seq, seq, P(None, "dp", "ctx"), seq, seq, seq),
        check_vma=False,
    )
```

```python
import functools

import jax
import jax.numpy as jnp
from jax import lax
from jax.experimental import pallas as pl
from jax.experimental.pallas import tpu as pltpu
from jax.sharding import PartitionSpec as P

BF = jnp.bfloat16
F32 = jnp.float32
MESH = pl.DeviceIdType.MESH
HEADS, KVH, GROUP, HD = 25, 5, 5, 64
TOK, WIDTH, KVW, STATE = 128, 1600, 320, 16
QL = 448
NT = (((1,), (1,)), ((), ()))
TN = (((0,), (0,)), ((), ()))


def dot(a, b, dims=(((1,), (0,)), ((), ()))):
    return lax.dot_general(a, b, dims, preferred_element_type=F32)


def split3(v):
    hi = v.astype(BF)
    rest = v - hi.astype(F32)
    mid = rest.astype(BF)
    low = (rest - mid.astype(F32)).astype(BF)
    return hi, mid, low


def dot3(v, onehot):
    hi, mid, low = split3(v)
    return dot(hi, onehot) + dot(mid, onehot) + dot(low, onehot)


def iota(shape, dim):
    return lax.broadcasted_iota(jnp.int32, shape, dim)


def places():
    dp, i = lax.axis_index("dp"), lax.axis_index("ctx")
    return dp, i, i % 2, (i // 2) % 2, i // 4


def layer_kernel(
    wins, key, val, xin, gin_, qin, bmin, cmin, ldin, mkin, mvin,
    gq, gk, gv, gm, gin, gbm, gcm,
    x, g, q, bm, cm, ldv, ldp, xt, gt, loc, win, metas, qg, dist, ps, pieces, own, sink,
    stq, r1, d0, d1, s2, r2, d2s, d2, s3, r3, d3s, d3, ib, ob, inc, adj,
    rc, ry, rz, sc, sb, sy, sa, k0, a0, k1, a1, k2, a2, k3, a3, k4, a4, k5,
    in_sem, kv_send, kv_recv, c_send, c_recv, q1_send, q1_recv, q2_send, q2_recv, q3_send, q3_recv,
    q4_send, q4_recv, e_send, e_recv, t_send, t_recv, m_send, m_recv,
):
    dp, i, core, yh, z = places()
    c = i % 4
    zl, zh = z % 4, z // 4
    xx, yl = dp % 4, dp // 4
    base = i - c
    ahead2, ahead4 = (i + 2) % 64, (i + 4) % 64
    back2, back4 = (i + 62) % 64, (i + 60) % 64
    group = [base + (c + k) % 4 for k in (1, 2, 3)]
    near = [(zh * 4 + (zl + k) % 4) * 4 + c for k in (1, 2, 3)]
    far = [(((zh + k) % 4) * 4 + zl) * 4 + c for k in (1, 2, 3)]
    mate = base + (c + 1 - 2 * core)
    across = base + (c + 2) % 4
    along_x = [(yl * 4 + (xx + k) % 4, i) for k in (1, 2, 3)]
    other = (1 - yl) * 4 + xx
    along_y = [(dp, across), (other, i), (other, across)]

    barrier = pltpu.get_barrier_semaphore()
    here = [(dp, to) for to in group + near + far + [ahead2, ahead4, back2, back4]]
    for to in here + along_x + along_y[1:]:
        pl.semaphore_signal(barrier, inc=1, device_id=to, device_id_type=MESH)

    def fetch(n, src, dst):
        copy = pltpu.make_async_copy(src, dst, in_sem.at[n])
        copy.start()
        return copy

    first_in = [fetch(0, key, win.at[0, :, 0:HD, :]), fetch(1, val, win.at[0, :, HD : 2 * HD, :])]
    scan_in = [fetch(2, ldin, ldv), fetch(3, xin, x), fetch(4, gin_, g), fetch(5, bmin, bm), fetch(6, cmin, cm)]
    late_in = [
        fetch(7, qin, q), fetch(8, mkin, metas.at[:, 0:HD, :]), fetch(9, mvin, metas.at[:, HD : 2 * HD, :])
    ]

    def pair(src, dst, send, recv, n, to):
        return pltpu.make_async_remote_copy(
            src_ref=src, dst_ref=dst, send_sem=send.at[n], recv_sem=recv.at[n],
            device_id=to, device_id_type=MESH,
        )

    for copy in scan_in:
        copy.wait()
    rows, cols = iota((TOK, TOK), 0), iota((TOK, TOK), 1)
    tri = (rows >= cols).astype(BF)
    ldp[...] = jnp.zeros((32, TOK), F32)
    for h in range(HEADS):
        ldp[h : h + 1, :] = ldv[h]
    run = jnp.zeros((TOK, 32), F32)
    run_t = jnp.zeros((32, TOK), F32)
    for part in split3(ldp[...]):
        run = run + dot(tri, part, NT)
        run_t = run_t + dot(part, tri, NT)
    end = run_t[:, TOK - 1 : TOK]
    tail = jnp.exp(end - run_t)
    head = jnp.exp(run_t)
    for h in range(HEADS):
        f = slice(HD * h, HD * h + HD)
        xt[f, :] = (tail[h : h + 1, :] * x[f, :].astype(F32)).astype(BF)
        gt[f, :] = (head[h : h + 1, :] * g[f, :].astype(F32)).astype(BF)
    for w, terms in enumerate((dot(bm[...], xt[...], NT), dot(cm[...], gt[...], NT))):
        for p in range(4):
            n = min(QL, WIDTH - QL * p)
            stq[p, w] = jnp.concatenate(
                [terms[:, QL * p : QL * p + n], jnp.zeros((STATE, 512 - n), F32)], axis=1
            ).astype(BF)
    d0[...] = jnp.broadcast_to(jnp.exp(run[TOK - 1 : TOK, :]), (8, 32))
    for copy in first_in:
        copy.wait()
    pl.semaphore_wait(barrier, 18)

    def mate_copy(d, n):
        return pair(win.at[d], win.at[(d + core * 9 + (1 - core)) % 10], c_send, c_recv, n, (dp, mate))

    step_a = pair(win.at[0], win.at[4], kv_send, kv_recv, 0, (dp, ahead4))
    step_y = pair(win.at[0], win.at[2], kv_send, kv_recv, 1, (dp, ahead2))
    step_b = pair(win.at[2], win.at[6], kv_send, kv_recv, 2, (dp, ahead4))
    step_c = pair(win.at[4], win.at[8], kv_send, kv_recv, 3, (dp, ahead4))
    mates = [mate_copy(d, n) for n, d in enumerate((0, 4, 2, 8, 6))]
    step_y.start()
    step_a.start()
    mates[0].start()

    q1 = []
    for n, k in enumerate((1, 2, 3)):
        q1.append(pair(stq.at[(c + k) % 4], r1.at[c], q1_send, q1_recv, n, (dp, group[n])))
        q1.append(pair(d0, d1.at[c], q1_send, q1_recv, 3 + n, (dp, group[n])))
    for copy in q1:
        copy.start()
    r1[c] = stq[c]
    d1[c] = d0[...]

    inner = dot(cm[...], bm[...], TN)

    def local_head(h, gram):
        f = slice(HD * h, HD * h + HD)
        diff = run[:, h : h + 1] - run_t[h : h + 1, :]
        mix = jnp.where(rows >= cols, jnp.exp(diff), 0.0)
        loc[f, :] = dot(g[f, :], (mix * inner).astype(BF))
        return gram + mix * dot(g[f, :], x[f, :], TN)

    gram = jnp.zeros((TOK, TOK), F32)
    for h in range(0, 10):
        gram = local_head(h, gram)
    step_a.wait_recv()
    step_c.start()
    mates[1].start()
    for h in range(10, 18):
        gram = local_head(h, gram)
    step_y.wait_recv()
    step_b.start()
    mates[2].start()

    row, lane = iota((32, 512), 0), iota((32, 512), 1)
    onehot = ((row == 7 * c + lane // HD) & (lane < QL)).astype(BF)

    def expand(d):
        wide = dot3(d[...].reshape(32, 32), onehot)
        return [jnp.broadcast_to(wide[8 * j : 8 * j + 1], (STATE, 512)) for j in range(4)]

    def sums(dec, terms):
        total, back = terms[0, 0].astype(F32), terms[3, 1].astype(F32)
        for j in range(1, 4):
            total = dec[j] * total + terms[j, 0].astype(F32)
            back = dec[3 - j] * back + terms[3 - j, 1].astype(F32)
        return total.astype(BF), back.astype(BF)

    q2 = []
    for n in range(3):
        q2.append(pair(s2, r2.at[zl], q2_send, q2_recv, n, (dp, near[n])))
        q2.append(pair(d2s, d2.at[zl], q2_send, q2_recv, 3 + n, (dp, near[n])))
    q3 = []
    for n, k in enumerate((1, 2, 3)):
        there = (zh + k) % 4
        which = jnp.where(there > zh, 0, 1)
        q3.append(pair(s3.at[which], r3.at[zh], q3_send, q3_recv, n, (dp, far[n])))
        q3.append(pair(d3s, d3.at[zh], q3_send, q3_recv, 3 + n, (dp, far[n])))
    q4 = [
        pair(ib.at[(c + k) % 4], ob.at[c], q4_send, q4_recv, n, (dp, group[n]))
        for n, k in enumerate((1, 2, 3))
    ]

    def scan_second():
        for copy in q1:
            copy.wait_recv()
        s2[0], s2[1] = sums(expand(d1), r1)
        d2s[...] = d1[0] * d1[1] * d1[2] * d1[3]
        for copy in q2:
            copy.start()
        r2[zl] = s2[...]
        d2[zl] = d2s[...]

    def scan_third():
        for copy in q2:
            copy.wait_recv()
        s3[0], s3[1] = sums(expand(d2), r2)
        d3s[...] = d2[0] * d2[1] * d2[2] * d2[3]
        for copy in q3:
            copy.start()
        r3[zh] = s3[0]
        d3[zh] = d3s[...]

    def scan_fourth():
        for copy in q3:
            copy.wait_recv()
        dec1, dec2, dec3 = expand(d1), expand(d2), expand(d3)
        ahead = jnp.zeros((STATE, 512), F32)
        behind = ahead
        for j in range(4):
            b = 3 - j
            ahead = jnp.where(j < zh, dec3[j] * ahead + r3[j].astype(F32), ahead)
            behind = jnp.where(b > zh, dec3[b] * behind + r3[b].astype(F32), behind)
        for j in range(4):
            b = 3 - j
            ahead = jnp.where(j < zl, dec2[j] * ahead + r2[j, 0].astype(F32), ahead)
            behind = jnp.where(b > zl, dec2[b] * behind + r2[b, 1].astype(F32), behind)
        for j in range(4):
            b = 3 - j
            ib[j, 0] = ahead.astype(BF)
            ahead = dec1[j] * ahead + r1[j, 0].astype(F32)
            ib[b, 1] = behind.astype(BF)
            behind = dec1[b] * behind + r1[b, 1].astype(F32)
        for copy in q4:
            copy.start()
        ob[c] = ib[c]

    scan_second()
    for h in range(18, HEADS):
        gram = local_head(h, gram)
    gram = gram.astype(BF)
    gbm[...] = dot(cm[...], gram)
    gcm[...] = dot(bm[...], gram, NT)

    for copy in late_in:
        copy.wait()
    zeros = jnp.zeros((HD, TOK), BF)
    for k in range(KVH):
        for j in range(GROUP):
            f = slice(HD * (GROUP * k + j), HD * (GROUP * k + j) + HD)
            at = 2 * TOK * j
            qg[k, 0:HD, at : at + TOK] = (q[f, :].astype(F32) * 0.125).astype(BF)
            qg[k, 0:HD, at + TOK : at + 2 * TOK] = zeros
            qg[k, HD : 2 * HD, at : at + TOK] = zeros
            qg[k, HD : 2 * HD, at + TOK : at + 2 * TOK] = g[f, :]
    behind_by = rows - cols
    never = jnp.int32(1 << 20)
    dist[:, 0:TOK] = jnp.zeros((TOK, TOK), jnp.int32)
    dist[:, TOK : 2 * TOK] = jnp.where(behind_by >= 0, behind_by, never)
    for d in range(1, 9):
        dist[:, TOK * (d + 1) : TOK * (d + 2)] = jnp.where(i >= d, behind_by + TOK * d, never)
    pieces[9] = jnp.zeros((KVH, TOK, TOK), BF)

    step_c.wait_recv()
    mates[3].start()
    step_b.wait_recv()
    mates[4].start()
    for copy in mates:
        copy.wait_recv()

    def keys_of(k):
        return jnp.concatenate([metas[k]] + [win[d, k] for d in range(9)], axis=1)

    def probs_of(k, carry):
        kv = keys_of(k)
        for j in range(GROUP):
            at = 2 * TOK * j
            both = dot(qg[k, :, at : at + 2 * TOK], kv, TN)
            s, dpr = both[:TOK], both[TOK:]
            s = jnp.where(dist[...] < wins[GROUP * k + j], s, -1e30)
            e = jnp.exp(s - jnp.max(s, axis=1, keepdims=True))
            inv = 1.0 / jnp.sum(e, axis=1, keepdims=True)
            delta = jnp.sum(e * dpr, axis=1, keepdims=True) * inv
            p = e * inv
            ps[k, at : at + TOK, :] = (p * (dpr - delta)).astype(BF)
            ps[k, at + TOK : at + 2 * TOK, :] = p.astype(BF)
        turned = dot(qg[k], ps[k, :, 0:TOK]).T
        for r in range(16):
            sink[r % 2, (r // 2) % 4, r // 8, k] = turned[8 * r : 8 * r + 8]

        @pl.when(k == 0)
        def _():
            scan_third()

        @pl.when(k == 3)
        def _():
            scan_fourth()

        return carry

    lax.fori_loop(0, KVH, probs_of, 0)

    m0 = pair(sink.at[1 - core], k0, m_send, m_recv, 0, (dp, mate))
    m1 = [pair(a0.at[(xx + k) % 4], k1.at[n], m_send, m_recv, 1 + n, along_x[n]) for n, k in enumerate((1, 2, 3))]
    m2 = [pair(a1.at[yl if n == 0 else 1 - yl], k2.at[n], m_send, m_recv, 4 + n, along_y[n]) for n in range(3)]
    m3 = [pair(a2, k3.at[n], m_send, m_recv, 7 + n, (dp, near[n])) for n in range(3)]
    m4 = [pair(a3, k4.at[n], m_send, m_recv, 10 + n, (dp, far[n])) for n in range(3)]
    m5 = pair(a4, k5, m_send, m_recv, 13, (dp, mate))

    def pass_on(arrived, result, value, following):
        for copy in arrived:
            copy.wait_recv()
        result[...] = value()
        for copy in following:
            copy.start()

    m0.start()

    def grads_of(k, carry):
        kv = keys_of(k)
        for j in range(GROUP):
            at = 2 * TOK * j
            dq = dot(kv[0:HD], ps[k, at : at + TOK, :], NT) * 0.125
            gq[pl.ds(pl.multiple_of(HD * (GROUP * k + j), HD), HD), :] = dq.astype(BF)
        back_t = dot(qg[k], ps[k, :, TOK:])
        own[k] = back_t[:, :TOK]
        for d in range(1, 9):
            pieces[d, k] = back_t[:, TOK * d : TOK * (d + 1)].astype(BF)

        @pl.when(k == 0)
        def _():
            pass_on([m0], a0, lambda: sink[core] + k0[...], m1)

        @pl.when(k == 2)
        def _():
            pass_on(m1, a1, lambda: a0[xx] + k1[0] + k1[1] + k1[2], m2)

        @pl.when(k == 4)
        def _():
            pass_on(m2, a2, lambda: a1[yl] + k2[0] + k2[1] + k2[2], m3)

        return carry

    lax.fori_loop(0, KVH, grads_of, 0)

    give = [
        pair(pieces.at[(d + core + 9 * (1 - core)) % 10], rc.at[n], e_send, e_recv, n, (dp, mate))
        for n, d in enumerate((8, 6, 2, 4, 0))
    ]
    for copy in give:
        copy.start()
    back_c = pair(sc, rz.at[0], t_send, t_recv, 0, (dp, back4))
    back_b = pair(sb, rz.at[1], t_send, t_recv, 1, (dp, back4))
    back_y = pair(sy, ry, t_send, t_recv, 2, (dp, back2))
    back_a = pair(sa, rz.at[2], t_send, t_recv, 3, (dp, back4))
    give[1].wait_recv()
    sb[...] = (pieces[6].astype(F32) + rc[1].astype(F32)).astype(BF)
    back_b.start()
    give[0].wait_recv()
    sc[...] = (pieces[8].astype(F32) + rc[0].astype(F32)).astype(BF)
    back_c.start()
    pass_on(m3, a3, lambda: a2[...] + k3[0] + k3[1] + k3[2], m4)

    for copy in q4:
        copy.wait_recv()
    for p in range(4):
        n = min(QL, WIDTH - QL * p)
        inc[:, QL * p : QL * p + n] = ob[p, 0].astype(F32)[:, :n]
        adj[:, QL * p : QL * p + n] = ob[p, 1].astype(F32)[:, :n]
    inc_h, adj_h = inc[...].astype(BF), adj[...].astype(BF)
    gbm[...] = gbm[...] + dot(adj_h, xt[...])
    gcm[...] = gcm[...] + dot(inc_h, gt[...])

    for copy in give[2:]:
        copy.wait_recv()
    sum_y = pieces[2].astype(F32) + rc[2].astype(F32)
    back_b.wait_recv()
    sy[...] = (sum_y + rz[1].astype(F32)).astype(BF)
    back_y.start()
    sum_a = pieces[4].astype(F32) + rc[3].astype(F32)
    back_c.wait_recv()
    sa[...] = (sum_a + rz[0].astype(F32)).astype(BF)
    back_a.start()

    carried = dot(adj_h, bm[...], TN)
    tail = jnp.exp(end - run_t)
    for h in range(HEADS):
        f = slice(HD * h, HD * h + HD)
        gin[f, :] = (loc[f, :] + tail[h : h + 1, :] * carried[f]).astype(BF)

    pass_on(m4, a4, lambda: a3[...] + k4[0] + k4[1] + k4[2], [m5])
    back_y.wait_recv()
    back_a.wait_recv()
    for k in range(KVH):
        mine = own[k] + rc[4, k].astype(F32) + ry[k].astype(F32) + rz[2, k].astype(F32)
        gk[HD * k : HD * k + HD, :] = mine[:HD].astype(BF)
        gv[HD * k : HD * k + HD, :] = mine[HD:].astype(BF)

    m5.wait_recv()
    row, lane = iota((16, TOK), 0), iota((16, TOK), 1)
    first = jnp.zeros((16, 8), F32)
    second = jnp.zeros((16, 8), F32)
    for k in range(KVH):
        feature = 5 * i + row % 8 - HD * k
        pick = (row % 8 < 5) & (feature >= 0) & (feature < HD) & (lane == feature + HD * (row // 8))
        pick = pick.astype(BF)
        for part in split3(a4[k]):
            first = first + dot(pick, part, NT)
        for part in split3(k5[k]):
            second = second + dot(pick, part, NT)
    left = jnp.where(core == 0, first, second)
    right = jnp.where(core == 0, second, first)
    for j in range(5):
        for w in range(2):
            gm[j, w : w + 1, 0:8] = left[8 * w + j : 8 * w + j + 1]
            gm[j, w : w + 1, 8:16] = right[8 * w + j : 8 * w + j + 1]

    for copy in [step_a, step_y, step_b, step_c] + mates + q1 + q2 + q3 + q4:
        copy.wait_send()
    for copy in give + [back_a, back_b, back_c, back_y, m0, m5] + m1 + m2 + m3 + m4:
        copy.wait_send()


OUTS = (
    ((WIDTH, TOK), BF), ((KVW, TOK), BF), ((KVW, TOK), BF), ((5, 2, 16), F32),
    ((WIDTH, TOK), BF), ((STATE, TOK), F32), ((STATE, TOK), F32),
)


def run_layer(*args):
    dma = pltpu.SemaphoreType.DMA
    vm = pltpu.VMEM
    block = (KVH, TOK, TOK)
    part = (KVH, 8, TOK)
    quarter = (2, STATE, 512)
    return pl.pallas_call(
        layer_kernel,
        out_shape=tuple(jax.ShapeDtypeStruct(s, t) for s, t in OUTS),
        in_specs=[pl.BlockSpec(memory_space=pltpu.SMEM)] + [pl.BlockSpec(memory_space=pl.ANY)] * 10,
        out_specs=(pl.BlockSpec(memory_space=vm),) * 7,
        scratch_shapes=[
            vm((WIDTH, TOK), BF), vm((WIDTH, TOK), BF), vm((WIDTH, TOK), BF),
            vm((STATE, TOK), BF), vm((STATE, TOK), BF), vm((HEADS, 1, TOK), F32), vm((32, TOK), F32),
            vm((WIDTH, TOK), BF), vm((WIDTH, TOK), BF), vm((WIDTH, TOK), F32),
            vm((10,) + block, BF), vm(block, BF), vm((KVH, TOK, 2 * TOK * GROUP), BF),
            vm((TOK, 10 * TOK), jnp.int32), vm((KVH, 2 * TOK * GROUP, 10 * TOK), BF),
            vm((10,) + block, BF), vm(block, F32), vm((2, 4, 2) + part, F32),
            vm((4,) + quarter, BF), vm((4,) + quarter, BF), vm((8, 32), F32), vm((4, 8, 32), F32),
            vm(quarter, BF), vm((4,) + quarter, BF), vm((8, 32), F32), vm((4, 8, 32), F32),
            vm(quarter, BF), vm((4, STATE, 512), BF), vm((8, 32), F32), vm((4, 8, 32), F32),
            vm((4,) + quarter, BF), vm((4,) + quarter, BF), vm((STATE, WIDTH), F32), vm((STATE, WIDTH), F32),
            vm((5,) + block, BF), vm(block, BF), vm((3,) + block, BF),
            vm(block, BF), vm(block, BF), vm(block, BF), vm(block, BF),
            vm((4, 2) + part, F32), vm((4, 2) + part, F32),
            vm((3, 2) + part, F32), vm((2,) + part, F32),
            vm((3,) + part, F32), vm(part, F32),
            vm((3,) + part, F32), vm(part, F32),
            vm((3,) + part, F32), vm(part, F32),
            vm(part, F32),
            dma((10,)), dma((4,)), dma((4,)), dma((5,)), dma((5,)),
            dma((6,)), dma((6,)), dma((6,)), dma((6,)), dma((6,)), dma((6,)), dma((3,)), dma((3,)),
            dma((5,)), dma((5,)), dma((4,)), dma((4,)), dma((14,)), dma((14,)),
        ],
        compiler_params=pltpu.CompilerParams(
            collective_id=0, has_side_effects=True, vmem_limit_bytes=56 * 1024 * 1024
        ),
        name="layer_grads",
    )(*args)


def hand_out_kernel(*refs):
    sources, targets, through, sem = refs[:7], refs[7:14], refs[14:21], refs[21]
    arrive = [pltpu.make_async_copy(a, b, sem.at[n]) for n, (a, b) in enumerate(zip(sources, through))]
    leave = [pltpu.make_async_copy(a, b, sem.at[7 + n]) for n, (a, b) in enumerate(zip(through, targets))]
    for copy in arrive:
        copy.start()
    for first, then in zip(arrive, leave):
        first.wait()
        then.start()
    for copy in leave:
        copy.wait()


def hand_out(arrays):
    return pl.pallas_call(
        hand_out_kernel,
        out_shape=tuple(jax.ShapeDtypeStruct(s, t) for s, t in OUTS),
        in_specs=[pl.BlockSpec(memory_space=pl.ANY)] * 7,
        out_specs=(pl.BlockSpec(memory_space=pl.ANY),) * 7,
        scratch_shapes=[pltpu.VMEM(s, t) for s, t in OUTS] + [pltpu.SemaphoreType.DMA((14,))],
        compiler_params=pltpu.CompilerParams(vmem_limit_bytes=60 * 1024 * 1024),
        name="hand_out",
    )(*arrays)


def local(
    queries, key_vectors, value_vectors, meta_keys, meta_values, windows,
    ssm_input, input_map, output_map, log_decay, cotangent,
):
    def turn(a):
        return jnp.swapaxes(a, -1, -2)

    def by_head(a):
        return turn(a).reshape(KVH, HD, TOK)

    grad_q, grad_k, grad_v, grad_meta, grad_input, grad_bm, grad_cm = hand_out(
        run_layer(
            windows, by_head(key_vectors[0]), by_head(value_vectors[0]), turn(ssm_input[0]), turn(cotangent[0]),
            turn(queries[0]), turn(input_map[0]), turn(output_map[0]), log_decay.transpose(2, 0, 1),
            by_head(meta_keys), by_head(meta_values),
        )
    )
    return (
        turn(grad_q)[None], turn(grad_k)[None], turn(grad_v)[None], grad_meta.transpose(1, 2, 0),
        turn(grad_input)[None], turn(grad_bm)[None], turn(grad_cm)[None],
    )


def solution(mesh):
    seq = P("dp", "ctx", None)
    return jax.shard_map(
        local,
        mesh=mesh,
        in_specs=(seq, seq, seq, P(), P(), P(), seq, seq, seq, seq, seq),
        out_specs=(seq, seq, seq, P(None, "dp", "ctx"), seq, seq, seq),
        check_vma=False,
    )
```

```python
import functools

import jax
import jax.numpy as jnp
from jax import lax
from jax.experimental import pallas as pl
from jax.experimental.pallas import tpu as pltpu
from jax.sharding import PartitionSpec as P

BF = jnp.bfloat16
F32 = jnp.float32
MESH = pl.DeviceIdType.MESH
HEADS, KVH, GROUP, HD = 25, 5, 5, 64
TOK, WIDTH, KVW, STATE = 128, 1600, 320, 16
QL = 448
NT = (((1,), (1,)), ((), ()))
TN = (((0,), (0,)), ((), ()))


def dot(a, b, dims=(((1,), (0,)), ((), ()))):
    return lax.dot_general(a, b, dims, preferred_element_type=F32)


def split3(v):
    hi = v.astype(BF)
    rest = v - hi.astype(F32)
    mid = rest.astype(BF)
    low = (rest - mid.astype(F32)).astype(BF)
    return hi, mid, low


def dot3(v, onehot):
    hi, mid, low = split3(v)
    return dot(hi, onehot) + dot(mid, onehot) + dot(low, onehot)


def iota(shape, dim):
    return lax.broadcasted_iota(jnp.int32, shape, dim)


def places():
    dp, i = lax.axis_index("dp"), lax.axis_index("ctx")
    return dp, i, i % 2, (i // 2) % 2, i // 4


def layer_kernel(
    wins, key, val, xin, gin_, qin, bmin, cmin, ldin, mkin, mvin,
    gq, gk, gv, gm, gin, gbm, gcm,
    x, g, q, bm, cm, ldv, ldp, xt, gt, loc, win, metas, qg, dist, ps, pieces, own, sink,
    stq, r1, d0, d1, s2, r2, d2s, d2, s3, r3, d3s, d3, ib, ob, inc, adj,
    rc, ry, rz, sc, sb, sy, sa, k0, a0, k1, a2, k4, a4, k5,
    in_sem, kv_send, kv_recv, c_send, c_recv, q1_send, q1_recv, q2_send, q2_recv, q3_send, q3_recv,
    q4_send, q4_recv, e_send, e_recv, t_send, t_recv, m_send, m_recv,
):
    dp, i, core, yh, z = places()
    c = i % 4
    zl, zh = z % 4, z // 4
    xx, yl = dp % 4, dp // 4
    base = i - c
    ahead2, ahead4 = (i + 2) % 64, (i + 4) % 64
    back2, back4 = (i + 62) % 64, (i + 60) % 64
    along_z = [(z + k) % 16 for k in range(1, 16)]
    group = [base + (c + k) % 4 for k in (1, 2, 3)]
    near = [(zh * 4 + (zl + k) % 4) * 4 + c for k in (1, 2, 3)]
    far = [(((zh + k) % 4) * 4 + zl) * 4 + c for k in (1, 2, 3)]
    mate = base + (c + 1 - 2 * core)
    across = base + (c + 2) % 4
    diag = across + 1 - 2 * core
    along_xy = [
        (((yl + a) % 2) * 4 + (xx + k) % 4, base + ((yh + b) % 2) * 2 + core)
        for k in range(4) for a in range(2) for b in range(2) if k + a + b > 0
    ]

    barrier = pltpu.get_barrier_semaphore()
    for to in [(dp, 4 * there + c) for there in along_z] + along_xy + [(dp, o) for o in (mate, diag, ahead2, back2)]:
        pl.semaphore_signal(barrier, inc=1, device_id=to, device_id_type=MESH)

    def fetch(n, src, dst):
        copy = pltpu.make_async_copy(src, dst, in_sem.at[n])
        copy.start()
        return copy

    first_in = [fetch(0, key, win.at[0, :, 0:HD, :]), fetch(1, val, win.at[0, :, HD : 2 * HD, :])]
    scan_in = [fetch(2, ldin, ldv), fetch(3, xin, x), fetch(4, gin_, g), fetch(5, bmin, bm), fetch(6, cmin, cm)]
    late_in = [
        fetch(7, qin, q), fetch(8, mkin, metas.at[:, 0:HD, :]), fetch(9, mvin, metas.at[:, HD : 2 * HD, :])
    ]

    def pair(src, dst, send, recv, n, to):
        return pltpu.make_async_remote_copy(
            src_ref=src, dst_ref=dst, send_sem=send.at[n], recv_sem=recv.at[n],
            device_id=to, device_id_type=MESH,
        )

    for copy in scan_in:
        copy.wait()
    rows, cols = iota((TOK, TOK), 0), iota((TOK, TOK), 1)
    tri = (rows >= cols).astype(BF)
    ldp[...] = jnp.zeros((32, TOK), F32)
    for h in range(HEADS):
        ldp[h : h + 1, :] = ldv[h]
    run = jnp.zeros((TOK, 32), F32)
    run_t = jnp.zeros((32, TOK), F32)
    for part in split3(ldp[...]):
        run = run + dot(tri, part, NT)
        run_t = run_t + dot(part, tri, NT)
    end = run_t[:, TOK - 1 : TOK]
    tail = jnp.exp(end - run_t)
    head = jnp.exp(run_t)
    for h in range(HEADS):
        f = slice(HD * h, HD * h + HD)
        xt[f, :] = (tail[h : h + 1, :] * x[f, :].astype(F32)).astype(BF)
        gt[f, :] = (head[h : h + 1, :] * g[f, :].astype(F32)).astype(BF)
    for w, terms in enumerate((dot(bm[...], xt[...], NT), dot(cm[...], gt[...], NT))):
        for p in range(4):
            n = min(QL, WIDTH - QL * p)
            stq[p, w] = jnp.concatenate(
                [terms[:, QL * p : QL * p + n], jnp.zeros((STATE, 512 - n), F32)], axis=1
            ).astype(BF)
    d0[...] = jnp.broadcast_to(jnp.exp(run[TOK - 1 : TOK, :]), (8, 32))
    for copy in first_in:
        copy.wait()
    pl.semaphore_wait(barrier, 34)

    def kv_copies(n, lo, hi):
        def step(src, dst, m, to):
            return pair(win.at[src, lo:hi], win.at[dst, lo:hi], kv_send, kv_recv, 4 * n + m, (dp, to))

        def to_mate(d, m):
            there = (d + core * 9 + (1 - core)) % 10
            return pair(win.at[d, lo:hi], win.at[there, lo:hi], c_send, c_recv, 5 * n + m, (dp, mate))

        steps = (step(0, 2, 0, ahead2), step(0, 4, 1, ahead4), step(2, 6, 2, ahead4), step(4, 8, 3, ahead4))
        return steps, [to_mate(d, m) for m, d in enumerate((0, 2, 4, 6, 8))]

    halves = [kv_copies(0, 0, 2), kv_copies(1, 2, KVH)]
    for steps, mates in halves:
        steps[0].start()
        steps[1].start()
        mates[0].start()

    def forward(n):
        steps, mates = halves[n]
        steps[0].wait_recv()
        steps[2].start()
        mates[1].start()
        steps[1].wait_recv()
        steps[3].start()
        mates[2].start()

    def finish(n):
        steps, mates = halves[n]
        steps[2].wait_recv()
        mates[3].start()
        steps[3].wait_recv()
        mates[4].start()

    q1 = []
    for n, k in enumerate((1, 2, 3)):
        q1.append(pair(stq.at[(c + k) % 4], r1.at[c], q1_send, q1_recv, n, (dp, group[n])))
        q1.append(pair(d0, d1.at[c], q1_send, q1_recv, 3 + n, (dp, group[n])))
    for copy in q1:
        copy.start()
    r1[c] = stq[c]
    d1[c] = d0[...]

    inner = dot(cm[...], bm[...], TN)

    def local_head(h, gram):
        f = slice(HD * h, HD * h + HD)
        diff = run[:, h : h + 1] - run_t[h : h + 1, :]
        mix = jnp.where(rows >= cols, jnp.exp(diff), 0.0)
        loc[f, :] = dot(g[f, :], (mix * inner).astype(BF))
        return gram + mix * dot(g[f, :], x[f, :], TN)

    gram = jnp.zeros((TOK, TOK), F32)
    for h in range(0, 10):
        gram = local_head(h, gram)
    forward(0)
    for h in range(10, 16):
        gram = local_head(h, gram)

    row, lane = iota((32, 512), 0), iota((32, 512), 1)
    onehot = ((row == 7 * c + lane // HD) & (lane < QL)).astype(BF)

    def expand(d):
        wide = dot3(d[...].reshape(32, 32), onehot)
        return [jnp.broadcast_to(wide[8 * j : 8 * j + 1], (STATE, 512)) for j in range(4)]

    def sums(dec, terms):
        total, back = terms[0, 0].astype(F32), terms[3, 1].astype(F32)
        for j in range(1, 4):
            total = dec[j] * total + terms[j, 0].astype(F32)
            back = dec[3 - j] * back + terms[3 - j, 1].astype(F32)
        return total.astype(BF), back.astype(BF)

    q2 = []
    for n in range(3):
        q2.append(pair(s2, r2.at[zl], q2_send, q2_recv, n, (dp, near[n])))
        q2.append(pair(d2s, d2.at[zl], q2_send, q2_recv, 3 + n, (dp, near[n])))
    q3 = []
    for n, k in enumerate((1, 2, 3)):
        there = (zh + k) % 4
        which = jnp.where(there > zh, 0, 1)
        q3.append(pair(s3.at[which], r3.at[zh], q3_send, q3_recv, n, (dp, far[n])))
        q3.append(pair(d3s, d3.at[zh], q3_send, q3_recv, 3 + n, (dp, far[n])))
    q4 = [
        pair(ib.at[(c + k) % 4], ob.at[c], q4_send, q4_recv, n, (dp, group[n]))
        for n, k in enumerate((1, 2, 3))
    ]

    def scan_second():
        for copy in q1:
            copy.wait_recv()
        s2[0], s2[1] = sums(expand(d1), r1)
        d2s[...] = d1[0] * d1[1] * d1[2] * d1[3]
        for copy in q2:
            copy.start()
        r2[zl] = s2[...]
        d2[zl] = d2s[...]

    def scan_third():
        for copy in q2:
            copy.wait_recv()
        s3[0], s3[1] = sums(expand(d2), r2)
        d3s[...] = d2[0] * d2[1] * d2[2] * d2[3]
        for copy in q3:
            copy.start()
        r3[zh] = s3[0]
        d3[zh] = d3s[...]

    def scan_fourth():
        for copy in q3:
            copy.wait_recv()
        dec1, dec2, dec3 = expand(d1), expand(d2), expand(d3)
        ahead = jnp.zeros((STATE, 512), F32)
        behind = ahead
        for j in range(4):
            b = 3 - j
            ahead = jnp.where(j < zh, dec3[j] * ahead + r3[j].astype(F32), ahead)
            behind = jnp.where(b > zh, dec3[b] * behind + r3[b].astype(F32), behind)
        for j in range(4):
            b = 3 - j
            ahead = jnp.where(j < zl, dec2[j] * ahead + r2[j, 0].astype(F32), ahead)
            behind = jnp.where(b > zl, dec2[b] * behind + r2[b, 1].astype(F32), behind)
        for j in range(4):
            b = 3 - j
            ib[j, 0] = ahead.astype(BF)
            ahead = dec1[j] * ahead + r1[j, 0].astype(F32)
            ib[b, 1] = behind.astype(BF)
            behind = dec1[b] * behind + r1[b, 1].astype(F32)
        for copy in q4:
            copy.start()
        ob[c] = ib[c]

    scan_second()
    for h in range(16, HEADS):
        gram = local_head(h, gram)
    forward(1)
    gram = gram.astype(BF)
    gbm[...] = dot(cm[...], gram)
    gcm[...] = dot(bm[...], gram, NT)

    for copy in late_in:
        copy.wait()
    zeros = jnp.zeros((HD, TOK), BF)
    for k in range(KVH):
        for j in range(GROUP):
            f = slice(HD * (GROUP * k + j), HD * (GROUP * k + j) + HD)
            at = 2 * TOK * j
            qg[k, 0:HD, at : at + TOK] = (q[f, :].astype(F32) * 0.125).astype(BF)
            qg[k, 0:HD, at + TOK : at + 2 * TOK] = zeros
            qg[k, HD : 2 * HD, at : at + TOK] = zeros
            qg[k, HD : 2 * HD, at + TOK : at + 2 * TOK] = g[f, :]
    behind_by = rows - cols
    never = jnp.int32(1 << 20)
    dist[:, 0:TOK] = jnp.zeros((TOK, TOK), jnp.int32)
    dist[:, TOK : 2 * TOK] = jnp.where(behind_by >= 0, behind_by, never)
    for d in range(1, 9):
        dist[:, TOK * (d + 1) : TOK * (d + 2)] = jnp.where(i >= d, behind_by + TOK * d, never)
    pieces[9] = jnp.zeros((KVH, TOK, TOK), BF)

    finish(0)
    for copy in halves[0][1]:
        copy.wait_recv()

    def keys_of(k):
        return jnp.concatenate([metas[k]] + [win[d, k] for d in range(9)], axis=1)

    def probs_of(k, carry):
        kv = keys_of(k)
        for j in range(GROUP):
            at = 2 * TOK * j
            both = dot(qg[k, :, at : at + 2 * TOK], kv, TN)
            s, dpr = both[:TOK], both[TOK:]
            s = jnp.where(dist[...] < wins[GROUP * k + j], s, -1e30)
            e = jnp.exp(s - jnp.max(s, axis=1, keepdims=True))
            inv = 1.0 / jnp.sum(e, axis=1, keepdims=True)
            delta = jnp.sum(e * dpr, axis=1, keepdims=True) * inv
            p = e * inv
            ps[k, at : at + TOK, :] = (p * (dpr - delta)).astype(BF)
            ps[k, at + TOK : at + 2 * TOK, :] = p.astype(BF)
        turned = dot(qg[k], ps[k, :, 0:TOK]).T
        for r in range(16):
            sink[r % 2, (r // 2) % 4, r // 8, k] = turned[8 * r : 8 * r + 8]

        @pl.when(k == 0)
        def _():
            finish(1)
            scan_third()

        @pl.when(k == 1)
        def _():
            for copy in halves[1][1]:
                copy.wait_recv()

        @pl.when(k == 4)
        def _():
            scan_fourth()

        return carry

    lax.fori_loop(0, KVH, probs_of, 0)

    held = (20 * z) // 64 - (20 * z) // 256
    m0 = pair(sink.at[1 - core], k0, m_send, m_recv, 0, (dp, mate))
    m1 = [
        pair(a0.at[to[0] % 4, to[0] // 4], k1.at[n], m_send, m_recv, 1 + n, to) for n, to in enumerate(along_xy)
    ]
    m2 = [
        pair(a2.at[pl.ds((20 * to) // 64 - (20 * to) // 256, 2)], k4.at[n], m_send, m_recv, 16 + n, (dp, 4 * to + c))
        for n, to in enumerate(along_z)
    ]
    m3 = pair(a4, k5, m_send, m_recv, 31, (dp, mate))

    def total(own_part, parts):
        for n in range(15):
            own_part = own_part + parts[n]
        return own_part

    def pass_on(arrived, result, value, following):
        for copy in arrived:
            copy.wait_recv()
        result[...] = value()
        for copy in following:
            copy.start()

    m0.start()

    parts = ((0, 3), (3, KVH))
    order = (6, 8, 2, 4, 0)
    gives = [
        [
            pair(
                pieces.at[(d + core + 9 * (1 - core)) % 10, lo:hi], rc.at[m, lo:hi],
                e_send, e_recv, 5 * n + m, (dp, mate),
            )
            for m, d in enumerate(order)
        ]
        for n, (lo, hi) in enumerate(parts)
    ]
    backs = [
        [
            pair(src.at[lo:hi], dst.at[lo:hi], t_send, t_recv, 4 * n + m, (dp, to))
            for m, (src, dst, to) in enumerate(
                ((sb, rz.at[1], back4), (sc, rz.at[0], back4), (sy, ry, back2), (sa, rz.at[2], back4))
            )
        ]
        for n, (lo, hi) in enumerate(parts)
    ]

    def send_far(n):
        lo, hi = parts[n]
        for m, out in ((0, sb), (1, sc)):
            gives[n][m].wait_recv()
            out[lo:hi] = (pieces[order[m], lo:hi].astype(F32) + rc[m, lo:hi].astype(F32)).astype(BF)
            backs[n][m].start()

    def send_near(n, m, out, arrived):
        lo, hi = parts[n]
        gives[n][m].wait_recv()
        backs[n][m - 2].wait_recv()
        part = pieces[order[m], lo:hi].astype(F32) + rc[m, lo:hi].astype(F32)
        out[lo:hi] = (part + rz[arrived, lo:hi].astype(F32)).astype(BF)
        backs[n][m].start()

    def grads_of(k, carry):
        kv = keys_of(k)
        for j in range(GROUP):
            at = 2 * TOK * j
            dq = dot(kv[0:HD], ps[k, at : at + TOK, :], NT) * 0.125
            gq[pl.ds(pl.multiple_of(HD * (GROUP * k + j), HD), HD), :] = dq.astype(BF)
        back_t = dot(qg[k], ps[k, :, TOK:])
        own[k] = back_t[:, :TOK]
        for d in range(1, 9):
            pieces[d, k] = back_t[:, TOK * d : TOK * (d + 1)].astype(BF)

        @pl.when(k == 0)
        def _():
            pass_on([m0], a0, lambda: sink[core] + k0[...], m1)

        @pl.when(k == 2)
        def _():
            for copy in gives[0]:
                copy.start()

        @pl.when(k == 3)
        def _():
            send_far(0)

        @pl.when(k == 4)
        def _():
            for copy in gives[1]:
                copy.start()
            pass_on(m1, a2, lambda: total(a0[xx, yl], k1), m2)

        return carry

    lax.fori_loop(0, KVH, grads_of, 0)

    send_far(1)
    send_near(0, 2, sy, 1)
    send_near(0, 3, sa, 0)

    for copy in q4:
        copy.wait_recv()
    for p in range(4):
        n = min(QL, WIDTH - QL * p)
        inc[:, QL * p : QL * p + n] = ob[p, 0].astype(F32)[:, :n]
        adj[:, QL * p : QL * p + n] = ob[p, 1].astype(F32)[:, :n]
    inc_h, adj_h = inc[...].astype(BF), adj[...].astype(BF)
    gbm[...] = gbm[...] + dot(adj_h, xt[...])
    gcm[...] = gcm[...] + dot(inc_h, gt[...])

    send_near(1, 2, sy, 1)
    send_near(1, 3, sa, 0)

    carried = dot(adj_h, bm[...], TN)
    tail = jnp.exp(end - run_t)
    for h in range(HEADS):
        f = slice(HD * h, HD * h + HD)
        gin[f, :] = (loc[f, :] + tail[h : h + 1, :] * carried[f]).astype(BF)

    pass_on(m2, a4, lambda: total(a2[pl.ds(held, 2)], k4), [m3])
    for n in range(2):
        gives[n][4].wait_recv()
        backs[n][2].wait_recv()
        backs[n][3].wait_recv()
    for k in range(KVH):
        mine = own[k] + rc[4, k].astype(F32) + ry[k].astype(F32) + rz[2, k].astype(F32)
        gk[HD * k : HD * k + HD, :] = mine[:HD].astype(BF)
        gv[HD * k : HD * k + HD, :] = mine[HD:].astype(BF)

    m3.wait_recv()
    row, lane = iota((16, TOK), 0), iota((16, TOK), 1)
    first = jnp.zeros((16, 8), F32)
    second = jnp.zeros((16, 8), F32)
    for k in range(2):
        feature = 5 * i + row % 8 - HD * (held + k)
        pick = (row % 8 < 5) & (feature >= 0) & (feature < HD) & (lane == feature + HD * (row // 8))
        pick = pick.astype(BF)
        for part in split3(a4[k]):
            first = first + dot(pick, part, NT)
        for part in split3(k5[k]):
            second = second + dot(pick, part, NT)
    left = jnp.where(core == 0, first, second)
    right = jnp.where(core == 0, second, first)
    for j in range(5):
        for w in range(2):
            gm[j, w : w + 1, 0:8] = left[8 * w + j : 8 * w + j + 1]
            gm[j, w : w + 1, 8:16] = right[8 * w + j : 8 * w + j + 1]

    for copy in q1 + q2 + q3 + q4 + [m0, m3] + m1 + m2:
        copy.wait_send()
    for n in range(2):
        for copy in list(halves[n][0]) + halves[n][1] + gives[n] + backs[n]:
            copy.wait_send()


OUTS = (
    ((WIDTH, TOK), BF), ((KVW, TOK), BF), ((KVW, TOK), BF), ((5, 2, 16), F32),
    ((WIDTH, TOK), BF), ((STATE, TOK), F32), ((STATE, TOK), F32),
)


def run_layer(*args):
    dma = pltpu.SemaphoreType.DMA
    vm = pltpu.VMEM
    block = (KVH, TOK, TOK)
    part = (KVH, 8, TOK)
    quarter = (2, STATE, 512)
    return pl.pallas_call(
        layer_kernel,
        out_shape=tuple(jax.ShapeDtypeStruct(s, t) for s, t in OUTS),
        in_specs=[pl.BlockSpec(memory_space=pltpu.SMEM)] + [pl.BlockSpec(memory_space=pl.ANY)] * 10,
        out_specs=(pl.BlockSpec(memory_space=vm),) * 7,
        scratch_shapes=[
            vm((WIDTH, TOK), BF), vm((WIDTH, TOK), BF), vm((WIDTH, TOK), BF),
            vm((STATE, TOK), BF), vm((STATE, TOK), BF), vm((HEADS, 1, TOK), F32), vm((32, TOK), F32),
            vm((WIDTH, TOK), BF), vm((WIDTH, TOK), BF), vm((WIDTH, TOK), F32),
            vm((10,) + block, BF), vm(block, BF), vm((KVH, TOK, 2 * TOK * GROUP), BF),
            vm((TOK, 10 * TOK), jnp.int32), vm((KVH, 2 * TOK * GROUP, 10 * TOK), BF),
            vm((10,) + block, BF), vm(block, F32), vm((2, 4, 2) + part, F32),
            vm((4,) + quarter, BF), vm((4,) + quarter, BF), vm((8, 32), F32), vm((4, 8, 32), F32),
            vm(quarter, BF), vm((4,) + quarter, BF), vm((8, 32), F32), vm((4, 8, 32), F32),
            vm(quarter, BF), vm((4, STATE, 512), BF), vm((8, 32), F32), vm((4, 8, 32), F32),
            vm((4,) + quarter, BF), vm((4,) + quarter, BF), vm((STATE, WIDTH), F32), vm((STATE, WIDTH), F32),
            vm((5,) + block, BF), vm(block, BF), vm((3,) + block, BF),
            vm(block, BF), vm(block, BF), vm(block, BF), vm(block, BF),
            vm((4, 2) + part, F32), vm((4, 2) + part, F32),
            vm((15,) + part, F32), vm(part, F32), vm((15, 2, 8, TOK), F32), vm((2, 8, TOK), F32), vm((2, 8, TOK), F32),
            dma((10,)), dma((8,)), dma((8,)), dma((10,)), dma((10,)),
            dma((6,)), dma((6,)), dma((6,)), dma((6,)), dma((6,)), dma((6,)), dma((3,)), dma((3,)),
            dma((10,)), dma((10,)), dma((8,)), dma((8,)), dma((32,)), dma((32,)),
        ],
        compiler_params=pltpu.CompilerParams(
            collective_id=0, has_side_effects=True, vmem_limit_bytes=56 * 1024 * 1024
        ),
        name="layer_grads",
    )(*args)


def hand_out_kernel(*refs):
    sources, targets, through, sem = refs[:7], refs[7:14], refs[14:21], refs[21]
    arrive = [pltpu.make_async_copy(a, b, sem.at[n]) for n, (a, b) in enumerate(zip(sources, through))]
    leave = [pltpu.make_async_copy(a, b, sem.at[7 + n]) for n, (a, b) in enumerate(zip(through, targets))]
    for copy in arrive:
        copy.start()
    for first, then in zip(arrive, leave):
        first.wait()
        then.start()
    for copy in leave:
        copy.wait()


def hand_out(arrays):
    return pl.pallas_call(
        hand_out_kernel,
        out_shape=tuple(jax.ShapeDtypeStruct(s, t) for s, t in OUTS),
        in_specs=[pl.BlockSpec(memory_space=pl.ANY)] * 7,
        out_specs=(pl.BlockSpec(memory_space=pl.ANY),) * 7,
        scratch_shapes=[pltpu.VMEM(s, t) for s, t in OUTS] + [pltpu.SemaphoreType.DMA((14,))],
        compiler_params=pltpu.CompilerParams(vmem_limit_bytes=60 * 1024 * 1024),
        name="hand_out",
    )(*arrays)


def local(
    queries, key_vectors, value_vectors, meta_keys, meta_values, windows,
    ssm_input, input_map, output_map, log_decay, cotangent,
):
    def turn(a):
        return jnp.swapaxes(a, -1, -2)

    def by_head(a):
        return turn(a).reshape(KVH, HD, TOK)

    grad_q, grad_k, grad_v, grad_meta, grad_input, grad_bm, grad_cm = hand_out(
        run_layer(
            windows, by_head(key_vectors[0]), by_head(value_vectors[0]), turn(ssm_input[0]), turn(cotangent[0]),
            turn(queries[0]), turn(input_map[0]), turn(output_map[0]), log_decay.transpose(2, 0, 1),
            by_head(meta_keys), by_head(meta_values),
        )
    )
    return (
        turn(grad_q)[None], turn(grad_k)[None], turn(grad_v)[None], grad_meta.transpose(1, 2, 0),
        turn(grad_input)[None], turn(grad_bm)[None], turn(grad_cm)[None],
    )


def solution(mesh):
    seq = P("dp", "ctx", None)
    return jax.shard_map(
        local,
        mesh=mesh,
        in_specs=(seq, seq, seq, P(), P(), P(), seq, seq, seq, seq, seq),
        out_specs=(seq, seq, seq, P(None, "dp", "ctx"), seq, seq, seq),
        check_vma=False,
    )
```

```python
import functools

import jax
import jax.numpy as jnp
from jax import lax
from jax.experimental import pallas as pl
from jax.experimental.pallas import tpu as pltpu
from jax.sharding import PartitionSpec as P

BF = jnp.bfloat16
F32 = jnp.float32
MESH = pl.DeviceIdType.MESH
HEADS, KVH, GROUP, HD = 25, 5, 5, 64
TOK, WIDTH, KVW, STATE = 128, 1600, 320, 16
QL = 448
NT = (((1,), (1,)), ((), ()))
TN = (((0,), (0,)), ((), ()))


def dot(a, b, dims=(((1,), (0,)), ((), ()))):
    return lax.dot_general(a, b, dims, preferred_element_type=F32)


def split3(v):
    hi = v.astype(BF)
    rest = v - hi.astype(F32)
    mid = rest.astype(BF)
    low = (rest - mid.astype(F32)).astype(BF)
    return hi, mid, low


def dot3(v, onehot):
    hi, mid, low = split3(v)
    return dot(hi, onehot) + dot(mid, onehot) + dot(low, onehot)


def iota(shape, dim):
    return lax.broadcasted_iota(jnp.int32, shape, dim)


def places():
    dp, i = lax.axis_index("dp"), lax.axis_index("ctx")
    return dp, i, i % 2, (i // 2) % 2, i // 4


def layer_kernel(
    wins, key, val, xin, gin_, qin, bmin, cmin, ldin, mkin, mvin,
    gq, gk, gv, gm, gin, gbm, gcm,
    x, g, q, bm, cm, ldv, ldp, xt, gt, loc, win, metas, qg, dist, ps, pieces, own, sink,
    stq, r1, d0, d1, s2, r2, d2s, d2, s3, r3, d3s, d3, ib, ob, inc, adj,
    rc, ry, rz, sc, sb, sy, sa, k0, a0, k1, a2, k4, a4, k5,
    in_sem, kv_send, kv_recv, c_send, c_recv, q1_send, q1_recv, q2_send, q2_recv, q3_send, q3_recv,
    q4_send, q4_recv, e_send, e_recv, t_send, t_recv, m_send, m_recv, vouch,
):
    dp, i, core, yh, z = places()
    c = i % 4
    zl, zh = z % 4, z // 4
    xx, yl = dp % 4, dp // 4
    base = i - c
    ahead2, ahead4 = (i + 2) % 64, (i + 4) % 64
    back2, back4 = (i + 62) % 64, (i + 60) % 64
    along_z = [(z + k) % 16 for k in range(1, 16)]
    group = [base + (c + k) % 4 for k in (1, 2, 3)]
    near = [(zh * 4 + (zl + k) % 4) * 4 + c for k in (1, 2, 3)]
    far = [(((zh + k) % 4) * 4 + zl) * 4 + c for k in (1, 2, 3)]
    mate = base + (c + 1 - 2 * core)
    across = base + (c + 2) % 4
    diag = across + 1 - 2 * core
    along_xy = [
        (((yl + a) % 2) * 4 + (xx + k) % 4, base + ((yh + b) % 2) * 2 + core)
        for k in range(4) for a in range(2) for b in range(2) if k + a + b > 0
    ]

    barrier = pltpu.get_barrier_semaphore()
    close = [(z + k) % 16 for k in (1, 2, 3, 4, 12, 13, 14, 15)]
    for to in [(dp, 4 * there + c) for there in close] + along_xy + [(dp, o) for o in (mate, diag, ahead2, back2)]:
        pl.semaphore_signal(barrier, inc=1, device_id=to, device_id_type=MESH)

    def fetch(n, src, dst):
        copy = pltpu.make_async_copy(src, dst, in_sem.at[n])
        copy.start()
        return copy

    first_in = [fetch(0, key, win.at[0, :, 0:HD, :]), fetch(1, val, win.at[0, :, HD : 2 * HD, :])]
    scan_in = [fetch(2, ldin, ldv), fetch(3, xin, x), fetch(4, gin_, g), fetch(5, bmin, bm), fetch(6, cmin, cm)]
    late_in = [
        fetch(7, qin, q), fetch(8, mkin, metas.at[:, 0:HD, :]), fetch(9, mvin, metas.at[:, HD : 2 * HD, :])
    ]

    def pair(src, dst, send, recv, n, to):
        return pltpu.make_async_remote_copy(
            src_ref=src, dst_ref=dst, send_sem=send.at[n], recv_sem=recv.at[n],
            device_id=to, device_id_type=MESH,
        )

    for copy in scan_in:
        copy.wait()
    rows, cols = iota((TOK, TOK), 0), iota((TOK, TOK), 1)
    tri = (rows >= cols).astype(BF)
    ldp[...] = jnp.zeros((32, TOK), F32)
    for h in range(HEADS):
        ldp[h : h + 1, :] = ldv[h]
    run = jnp.zeros((TOK, 32), F32)
    run_t = jnp.zeros((32, TOK), F32)
    for part in split3(ldp[...]):
        run = run + dot(tri, part, NT)
        run_t = run_t + dot(part, tri, NT)
    end = run_t[:, TOK - 1 : TOK]
    tail = jnp.exp(end - run_t)
    head = jnp.exp(run_t)
    for h in range(HEADS):
        f = slice(HD * h, HD * h + HD)
        xt[f, :] = (tail[h : h + 1, :] * x[f, :].astype(F32)).astype(BF)
        gt[f, :] = (head[h : h + 1, :] * g[f, :].astype(F32)).astype(BF)
    for w, terms in enumerate((dot(bm[...], xt[...], NT), dot(cm[...], gt[...], NT))):
        for p in range(4):
            n = min(QL, WIDTH - QL * p)
            stq[p, w] = jnp.concatenate(
                [terms[:, QL * p : QL * p + n], jnp.zeros((STATE, 512 - n), F32)], axis=1
            ).astype(BF)
    d0[...] = jnp.broadcast_to(jnp.exp(run[TOK - 1 : TOK, :]), (8, 32))
    for copy in first_in:
        copy.wait()
    pl.semaphore_wait(barrier, 27)
    for k in (4, 12):
        pl.semaphore_signal(
            vouch, inc=1, device_id=(dp, 4 * ((z + k) % 16) + c), device_id_type=MESH
        )

    def kv_copies(n, lo, hi):
        def step(src, dst, m, to):
            return pair(win.at[src, lo:hi], win.at[dst, lo:hi], kv_send, kv_recv, 4 * n + m, (dp, to))

        def to_mate(d, m):
            there = (d + core * 9 + (1 - core)) % 10
            return pair(win.at[d, lo:hi], win.at[there, lo:hi], c_send, c_recv, 5 * n + m, (dp, mate))

        steps = (step(0, 2, 0, ahead2), step(0, 4, 1, ahead4), step(2, 6, 2, ahead4), step(4, 8, 3, ahead4))
        return steps, [to_mate(d, m) for m, d in enumerate((0, 2, 4, 6, 8))]

    halves = [kv_copies(0, 0, 2), kv_copies(1, 2, KVH)]
    for steps, mates in halves:
        steps[0].start()
        steps[1].start()
        mates[0].start()

    def forward(n):
        steps, mates = halves[n]
        steps[0].wait_recv()
        steps[2].start()
        mates[1].start()
        steps[1].wait_recv()
        steps[3].start()
        mates[2].start()

    def finish(n):
        steps, mates = halves[n]
        steps[2].wait_recv()
        mates[3].start()
        steps[3].wait_recv()
        mates[4].start()

    q1 = []
    for n, k in enumerate((1, 2, 3)):
        q1.append(pair(stq.at[(c + k) % 4], r1.at[c], q1_send, q1_recv, n, (dp, group[n])))
        q1.append(pair(d0, d1.at[c], q1_send, q1_recv, 3 + n, (dp, group[n])))
    for copy in q1:
        copy.start()
    r1[c] = stq[c]
    d1[c] = d0[...]

    inner = dot(cm[...], bm[...], TN)

    def local_head(h, gram):
        f = slice(HD * h, HD * h + HD)
        diff = run[:, h : h + 1] - run_t[h : h + 1, :]
        mix = jnp.where(rows >= cols, jnp.exp(diff), 0.0)
        loc[f, :] = dot(g[f, :], (mix * inner).astype(BF))
        return gram + mix * dot(g[f, :], x[f, :], TN)

    gram = jnp.zeros((TOK, TOK), F32)
    for h in range(0, 10):
        gram = local_head(h, gram)
    forward(0)
    for h in range(10, 16):
        gram = local_head(h, gram)

    row, lane = iota((32, 512), 0), iota((32, 512), 1)
    onehot = ((row == 7 * c + lane // HD) & (lane < QL)).astype(BF)

    def expand(d):
        wide = dot3(d[...].reshape(32, 32), onehot)
        return [jnp.broadcast_to(wide[8 * j : 8 * j + 1], (STATE, 512)) for j in range(4)]

    def sums(dec, terms):
        total, back = terms[0, 0].astype(F32), terms[3, 1].astype(F32)
        for j in range(1, 4):
            total = dec[j] * total + terms[j, 0].astype(F32)
            back = dec[3 - j] * back + terms[3 - j, 1].astype(F32)
        return total.astype(BF), back.astype(BF)

    q2 = []
    for n in range(3):
        q2.append(pair(s2, r2.at[zl], q2_send, q2_recv, n, (dp, near[n])))
        q2.append(pair(d2s, d2.at[zl], q2_send, q2_recv, 3 + n, (dp, near[n])))
    q3 = []
    for n, k in enumerate((1, 2, 3)):
        there = (zh + k) % 4
        which = jnp.where(there > zh, 0, 1)
        q3.append(pair(s3.at[which], r3.at[zh], q3_send, q3_recv, n, (dp, far[n])))
        q3.append(pair(d3s, d3.at[zh], q3_send, q3_recv, 3 + n, (dp, far[n])))
    q4 = [
        pair(ib.at[(c + k) % 4], ob.at[c], q4_send, q4_recv, n, (dp, group[n]))
        for n, k in enumerate((1, 2, 3))
    ]

    def scan_second():
        for copy in q1:
            copy.wait_recv()
        s2[0], s2[1] = sums(expand(d1), r1)
        d2s[...] = d1[0] * d1[1] * d1[2] * d1[3]
        for copy in q2:
            copy.start()
        r2[zl] = s2[...]
        d2[zl] = d2s[...]

    def scan_third():
        for copy in q2:
            copy.wait_recv()
        pl.semaphore_wait(vouch, 2)
        s3[0], s3[1] = sums(expand(d2), r2)
        d3s[...] = d2[0] * d2[1] * d2[2] * d2[3]
        for copy in q3:
            copy.start()
        r3[zh] = s3[0]
        d3[zh] = d3s[...]

    def scan_fourth():
        for copy in q3:
            copy.wait_recv()
        dec1, dec2, dec3 = expand(d1), expand(d2), expand(d3)
        ahead = jnp.zeros((STATE, 512), F32)
        behind = ahead
        for j in range(4):
            b = 3 - j
            ahead = jnp.where(j < zh, dec3[j] * ahead + r3[j].astype(F32), ahead)
            behind = jnp.where(b > zh, dec3[b] * behind + r3[b].astype(F32), behind)
        for j in range(4):
            b = 3 - j
            ahead = jnp.where(j < zl, dec2[j] * ahead + r2[j, 0].astype(F32), ahead)
            behind = jnp.where(b > zl, dec2[b] * behind + r2[b, 1].astype(F32), behind)
        for j in range(4):
            b = 3 - j
            ib[j, 0] = ahead.astype(BF)
            ahead = dec1[j] * ahead + r1[j, 0].astype(F32)
            ib[b, 1] = behind.astype(BF)
            behind = dec1[b] * behind + r1[b, 1].astype(F32)
        for copy in q4:
            copy.start()
        ob[c] = ib[c]

    scan_second()
    for h in range(16, HEADS):
        gram = local_head(h, gram)
    finish(0)
    forward(1)
    gram = gram.astype(BF)
    gbm[...] = dot(cm[...], gram)
    gcm[...] = dot(bm[...], gram, NT)

    for copy in late_in:
        copy.wait()
    zeros = jnp.zeros((HD, TOK), BF)
    for k in range(KVH):
        for j in range(GROUP):
            f = slice(HD * (GROUP * k + j), HD * (GROUP * k + j) + HD)
            at = 2 * TOK * j
            qg[k, 0:HD, at : at + TOK] = (q[f, :].astype(F32) * 0.125).astype(BF)
            qg[k, 0:HD, at + TOK : at + 2 * TOK] = zeros
            qg[k, HD : 2 * HD, at : at + TOK] = zeros
            qg[k, HD : 2 * HD, at + TOK : at + 2 * TOK] = g[f, :]
    behind_by = rows - cols
    never = jnp.int32(1 << 20)
    dist[:, 0:TOK] = jnp.zeros((TOK, TOK), jnp.int32)
    dist[:, TOK : 2 * TOK] = jnp.where(behind_by >= 0, behind_by, never)
    for d in range(1, 9):
        dist[:, TOK * (d + 1) : TOK * (d + 2)] = jnp.where(i >= d, behind_by + TOK * d, never)
    pieces[9] = jnp.zeros((KVH, TOK, TOK), BF)

    for copy in halves[0][1]:
        copy.wait_recv()

    def keys_of(k):
        return jnp.concatenate([metas[k]] + [win[d, k] for d in range(9)], axis=1)

    def probs_of(k, carry):
        kv = keys_of(k)
        for j in range(GROUP):
            at = 2 * TOK * j
            both = dot(qg[k, :, at : at + 2 * TOK], kv, TN)
            s, dpr = both[:TOK], both[TOK:]
            s = jnp.where(dist[...] < wins[GROUP * k + j], s, -1e30)
            e = jnp.exp(s - jnp.max(s, axis=1, keepdims=True))
            inv = 1.0 / jnp.sum(e, axis=1, keepdims=True)
            delta = jnp.sum(e * dpr, axis=1, keepdims=True) * inv
            p = e * inv
            ps[k, at : at + TOK, :] = (p * (dpr - delta)).astype(BF)
            ps[k, at + TOK : at + 2 * TOK, :] = p.astype(BF)
        turned = dot(qg[k], ps[k, :, 0:TOK]).T
        for r in range(16):
            sink[r % 2, (r // 2) % 4, r // 8, k] = turned[8 * r : 8 * r + 8]

        @pl.when(k == 0)
        def _():
            finish(1)
            scan_third()

        @pl.when(k == 1)
        def _():
            for copy in halves[1][1]:
                copy.wait_recv()

        @pl.when(k == 4)
        def _():
            scan_fourth()

        return carry

    lax.fori_loop(0, KVH, probs_of, 0)

    held = (20 * z) // 64 - (20 * z) // 256
    m0 = pair(sink.at[1 - core], k0, m_send, m_recv, 0, (dp, mate))
    m1 = [
        pair(a0.at[to[0] % 4, to[0] // 4], k1.at[n], m_send, m_recv, 1 + n, to) for n, to in enumerate(along_xy)
    ]
    m2 = [
        pair(a2.at[pl.ds((20 * to) // 64 - (20 * to) // 256, 2)], k4.at[n], m_send, m_recv, 16 + n, (dp, 4 * to + c))
        for n, to in enumerate(along_z)
    ]
    m3 = pair(a4, k5, m_send, m_recv, 31, (dp, mate))

    def total(own_part, parts):
        for n in range(15):
            own_part = own_part + parts[n]
        return own_part

    def pass_on(arrived, result, value, following):
        for copy in arrived:
            copy.wait_recv()
        result[...] = value()
        for copy in following:
            copy.start()

    m0.start()

    parts = ((0, 2), (2, 4), (4, KVH))
    order = (6, 8, 2, 4, 0)
    gives = [
        [
            pair(
                pieces.at[(d + core + 9 * (1 - core)) % 10, lo:hi], rc.at[m, lo:hi],
                e_send, e_recv, 5 * n + m, (dp, mate),
            )
            for m, d in enumerate(order)
        ]
        for n, (lo, hi) in enumerate(parts)
    ]
    backs = [
        [
            pair(src.at[lo:hi], dst.at[lo:hi], t_send, t_recv, 4 * n + m, (dp, to))
            for m, (src, dst, to) in enumerate(
                ((sb, rz.at[1], back4), (sc, rz.at[0], back4), (sy, ry, back2), (sa, rz.at[2], back4))
            )
        ]
        for n, (lo, hi) in enumerate(parts)
    ]

    def send_far(n):
        lo, hi = parts[n]
        for m, out in ((0, sb), (1, sc)):
            gives[n][m].wait_recv()
            out[lo:hi] = (pieces[order[m], lo:hi].astype(F32) + rc[m, lo:hi].astype(F32)).astype(BF)
            backs[n][m].start()

    def send_near(n, m, out, arrived):
        lo, hi = parts[n]
        gives[n][m].wait_recv()
        backs[n][m - 2].wait_recv()
        part = pieces[order[m], lo:hi].astype(F32) + rc[m, lo:hi].astype(F32)
        out[lo:hi] = (part + rz[arrived, lo:hi].astype(F32)).astype(BF)
        backs[n][m].start()

    def grads_of(k, carry):
        kv = keys_of(k)
        for j in range(GROUP):
            at = 2 * TOK * j
            dq = dot(kv[0:HD], ps[k, at : at + TOK, :], NT) * 0.125
            gq[pl.ds(pl.multiple_of(HD * (GROUP * k + j), HD), HD), :] = dq.astype(BF)
        back_t = dot(qg[k], ps[k, :, TOK:])
        own[k] = back_t[:, :TOK]
        for d in range(1, 9):
            pieces[d, k] = back_t[:, TOK * d : TOK * (d + 1)].astype(BF)

        @pl.when(k == 0)
        def _():
            pass_on([m0], a0, lambda: sink[core] + k0[...], m1)

        @pl.when(k == 1)
        def _():
            for copy in gives[0]:
                copy.start()

        @pl.when(k == 2)
        def _():
            send_far(0)

        @pl.when(k == 3)
        def _():
            for copy in gives[1]:
                copy.start()

        @pl.when(k == 4)
        def _():
            for copy in gives[2]:
                copy.start()
            send_far(1)
            pass_on(m1, a2, lambda: total(a0[xx, yl], k1), m2)

        return carry

    lax.fori_loop(0, KVH, grads_of, 0)

    send_far(2)
    for n in (0, 1):
        send_near(n, 2, sy, 1)
        send_near(n, 3, sa, 0)

    for copy in q4:
        copy.wait_recv()
    for p in range(4):
        n = min(QL, WIDTH - QL * p)
        inc[:, QL * p : QL * p + n] = ob[p, 0].astype(F32)[:, :n]
        adj[:, QL * p : QL * p + n] = ob[p, 1].astype(F32)[:, :n]
    inc_h, adj_h = inc[...].astype(BF), adj[...].astype(BF)
    gbm[...] = gbm[...] + dot(adj_h, xt[...])
    gcm[...] = gcm[...] + dot(inc_h, gt[...])

    send_near(2, 2, sy, 1)
    send_near(2, 3, sa, 0)

    carried = dot(adj_h, bm[...], TN)
    tail = jnp.exp(end - run_t)
    for h in range(HEADS):
        f = slice(HD * h, HD * h + HD)
        gin[f, :] = (loc[f, :] + tail[h : h + 1, :] * carried[f]).astype(BF)

    pass_on(m2, a4, lambda: total(a2[pl.ds(held, 2)], k4), [m3])
    for n in range(3):
        gives[n][4].wait_recv()
        backs[n][2].wait_recv()
        backs[n][3].wait_recv()
    for k in range(KVH):
        mine = own[k] + rc[4, k].astype(F32) + ry[k].astype(F32) + rz[2, k].astype(F32)
        gk[HD * k : HD * k + HD, :] = mine[:HD].astype(BF)
        gv[HD * k : HD * k + HD, :] = mine[HD:].astype(BF)

    m3.wait_recv()
    row, lane = iota((16, TOK), 0), iota((16, TOK), 1)
    first = jnp.zeros((16, 8), F32)
    second = jnp.zeros((16, 8), F32)
    for k in range(2):
        feature = 5 * i + row % 8 - HD * (held + k)
        pick = (row % 8 < 5) & (feature >= 0) & (feature < HD) & (lane == feature + HD * (row // 8))
        pick = pick.astype(BF)
        for part in split3(a4[k]):
            first = first + dot(pick, part, NT)
        for part in split3(k5[k]):
            second = second + dot(pick, part, NT)
    left = jnp.where(core == 0, first, second)
    right = jnp.where(core == 0, second, first)
    for j in range(5):
        for w in range(2):
            gm[j, w : w + 1, 0:8] = left[8 * w + j : 8 * w + j + 1]
            gm[j, w : w + 1, 8:16] = right[8 * w + j : 8 * w + j + 1]

    for copy in q1 + q2 + q3 + q4 + [m0, m3] + m1 + m2:
        copy.wait_send()
    for steps, mates in halves:
        for copy in list(steps) + mates:
            copy.wait_send()
    for copy in sum(gives, []) + sum(backs, []):
        copy.wait_send()


OUTS = (
    ((WIDTH, TOK), BF), ((KVW, TOK), BF), ((KVW, TOK), BF), ((5, 2, 16), F32),
    ((WIDTH, TOK), BF), ((STATE, TOK), F32), ((STATE, TOK), F32),
)


def run_layer(*args):
    dma = pltpu.SemaphoreType.DMA
    vm = pltpu.VMEM
    block = (KVH, TOK, TOK)
    part = (KVH, 8, TOK)
    quarter = (2, STATE, 512)
    return pl.pallas_call(
        layer_kernel,
        out_shape=tuple(jax.ShapeDtypeStruct(s, t) for s, t in OUTS),
        in_specs=[pl.BlockSpec(memory_space=pltpu.SMEM)] + [pl.BlockSpec(memory_space=pl.ANY)] * 10,
        out_specs=(pl.BlockSpec(memory_space=vm),) * 7,
        scratch_shapes=[
            vm((WIDTH, TOK), BF), vm((WIDTH, TOK), BF), vm((WIDTH, TOK), BF),
            vm((STATE, TOK), BF), vm((STATE, TOK), BF), vm((HEADS, 1, TOK), F32), vm((32, TOK), F32),
            vm((WIDTH, TOK), BF), vm((WIDTH, TOK), BF), vm((WIDTH, TOK), F32),
            vm((10,) + block, BF), vm(block, BF), vm((KVH, TOK, 2 * TOK * GROUP), BF),
            vm((TOK, 10 * TOK), jnp.int32), vm((KVH, 2 * TOK * GROUP, 10 * TOK), BF),
            vm((10,) + block, BF), vm(block, F32), vm((2, 4, 2) + part, F32),
            vm((4,) + quarter, BF), vm((4,) + quarter, BF), vm((8, 32), F32), vm((4, 8, 32), F32),
            vm(quarter, BF), vm((4,) + quarter, BF), vm((8, 32), F32), vm((4, 8, 32), F32),
            vm(quarter, BF), vm((4, STATE, 512), BF), vm((8, 32), F32), vm((4, 8, 32), F32),
            vm((4,) + quarter, BF), vm((4,) + quarter, BF), vm((STATE, WIDTH), F32), vm((STATE, WIDTH), F32),
            vm((5,) + block, BF), vm(block, BF), vm((3,) + block, BF),
            vm(block, BF), vm(block, BF), vm(block, BF), vm(block, BF),
            vm((4, 2) + part, F32), vm((4, 2) + part, F32),
            vm((15,) + part, F32), vm(part, F32), vm((15, 2, 8, TOK), F32), vm((2, 8, TOK), F32), vm((2, 8, TOK), F32),
            dma((10,)), dma((8,)), dma((8,)), dma((10,)), dma((10,)),
            dma((6,)), dma((6,)), dma((6,)), dma((6,)), dma((6,)), dma((6,)), dma((3,)), dma((3,)),
            dma((15,)), dma((15,)), dma((12,)), dma((12,)), dma((32,)), dma((32,)), pltpu.SemaphoreType.REGULAR,
        ],
        compiler_params=pltpu.CompilerParams(
            collective_id=0, has_side_effects=True, vmem_limit_bytes=56 * 1024 * 1024
        ),
        name="layer_grads",
    )(*args)


def hand_out_kernel(*refs):
    sources, targets, through, sem = refs[:7], refs[7:14], refs[14:21], refs[21]
    arrive = [pltpu.make_async_copy(a, b, sem.at[n]) for n, (a, b) in enumerate(zip(sources, through))]
    leave = [pltpu.make_async_copy(a, b, sem.at[7 + n]) for n, (a, b) in enumerate(zip(through, targets))]
    for copy in arrive:
        copy.start()
    for first, then in zip(arrive, leave):
        first.wait()
        then.start()
    for copy in leave:
        copy.wait()


def hand_out(arrays):
    return pl.pallas_call(
        hand_out_kernel,
        out_shape=tuple(jax.ShapeDtypeStruct(s, t) for s, t in OUTS),
        in_specs=[pl.BlockSpec(memory_space=pl.ANY)] * 7,
        out_specs=(pl.BlockSpec(memory_space=pl.ANY),) * 7,
        scratch_shapes=[pltpu.VMEM(s, t) for s, t in OUTS] + [pltpu.SemaphoreType.DMA((14,))],
        compiler_params=pltpu.CompilerParams(vmem_limit_bytes=60 * 1024 * 1024),
        name="hand_out",
    )(*arrays)


def local(
    queries, key_vectors, value_vectors, meta_keys, meta_values, windows,
    ssm_input, input_map, output_map, log_decay, cotangent,
):
    def turn(a):
        return jnp.swapaxes(a, -1, -2)

    def by_head(a):
        return turn(a).reshape(KVH, HD, TOK)

    grad_q, grad_k, grad_v, grad_meta, grad_input, grad_bm, grad_cm = hand_out(
        run_layer(
            windows, by_head(key_vectors[0]), by_head(value_vectors[0]), turn(ssm_input[0]), turn(cotangent[0]),
            turn(queries[0]), turn(input_map[0]), turn(output_map[0]), log_decay.transpose(2, 0, 1),
            by_head(meta_keys), by_head(meta_values),
        )
    )
    return (
        turn(grad_q)[None], turn(grad_k)[None], turn(grad_v)[None], grad_meta.transpose(1, 2, 0),
        turn(grad_input)[None], turn(grad_bm)[None], turn(grad_cm)[None],
    )


def solution(mesh):
    seq = P("dp", "ctx", None)
    return jax.shard_map(
        local,
        mesh=mesh,
        in_specs=(seq, seq, seq, P(), P(), P(), seq, seq, seq, seq, seq),
        out_specs=(seq, seq, seq, P(None, "dp", "ctx"), seq, seq, seq),
        check_vma=False,
    )
```

```python
import functools

import jax
import jax.numpy as jnp
from jax import lax
from jax.experimental import pallas as pl
from jax.experimental.pallas import tpu as pltpu
from jax.sharding import PartitionSpec as P

BF = jnp.bfloat16
F32 = jnp.float32
MESH = pl.DeviceIdType.MESH
HEADS, KVH, GROUP, HD = 25, 5, 5, 64
TOK, WIDTH, KVW, STATE = 128, 1600, 320, 16
QL = 448
NT = (((1,), (1,)), ((), ()))
TN = (((0,), (0,)), ((), ()))


def dot(a, b, dims=(((1,), (0,)), ((), ()))):
    return lax.dot_general(a, b, dims, preferred_element_type=F32)


def split3(v):
    hi = v.astype(BF)
    rest = v - hi.astype(F32)
    mid = rest.astype(BF)
    low = (rest - mid.astype(F32)).astype(BF)
    return hi, mid, low


def dot3(v, onehot):
    hi, mid, low = split3(v)
    return dot(hi, onehot) + dot(mid, onehot) + dot(low, onehot)


def iota(shape, dim):
    return lax.broadcasted_iota(jnp.int32, shape, dim)


def places():
    dp, i = lax.axis_index("dp"), lax.axis_index("ctx")
    return dp, i, i % 2, (i // 2) % 2, i // 4


def layer_kernel(
    wins, key, val, xin, gin_, qin, bmin, cmin, ldin, mkin, mvin,
    gq, gk, gv, gm, gin, gbm, gcm,
    x, g, q, bm, cm, ldv, ldp, xt, gt, loc, win, metas, qg, dist, ps, pieces, own, sink,
    stq, r1, d0, d1, s2, r2, d2s, d2, s3, r3, d3s, d3, ib, ob, inc, adj,
    rc, ry, rz, sc, sb, sy, sa, k0, a0, k1, a2, k4, a4, k5,
    in_sem, kv_send, kv_recv, c_send, c_recv, q1_send, q1_recv, q2_send, q2_recv, q3_send, q3_recv,
    q4_send, q4_recv, e_send, e_recv, t_send, t_recv, m_send, m_recv, vouch,
):
    dp, i, core, yh, z = places()
    c = i % 4
    zl, zh = z % 4, z // 4
    xx, yl = dp % 4, dp // 4
    base = i - c
    ahead2, ahead4 = (i + 2) % 64, (i + 4) % 64
    back2, back4 = (i + 62) % 64, (i + 60) % 64
    along_z = [(z + k) % 16 for k in range(1, 16)]
    group = [base + (c + k) % 4 for k in (1, 2, 3)]
    near = [(zh * 4 + (zl + k) % 4) * 4 + c for k in (1, 2, 3)]
    far = [(((zh + k) % 4) * 4 + zl) * 4 + c for k in (1, 2, 3)]
    mate = base + (c + 1 - 2 * core)
    across = base + (c + 2) % 4
    diag = across + 1 - 2 * core
    along_xy = [
        (((yl + a) % 2) * 4 + (xx + k) % 4, base + ((yh + b) % 2) * 2 + core)
        for k in range(4) for a in range(2) for b in range(2) if k + a + b > 0
    ]

    barrier = pltpu.get_barrier_semaphore()
    close = [(z + k) % 16 for k in (1, 2, 3, 4, 12, 13, 14, 15)]
    for to in [(dp, 4 * there + c) for there in close] + along_xy + [(dp, o) for o in (mate, diag, ahead2, back2)]:
        pl.semaphore_signal(barrier, inc=1, device_id=to, device_id_type=MESH)

    def fetch(n, src, dst):
        copy = pltpu.make_async_copy(src, dst, in_sem.at[n])
        copy.start()
        return copy

    first_in = [fetch(0, key, win.at[0, :, 0:HD, :]), fetch(1, val, win.at[0, :, HD : 2 * HD, :])]
    scan_in = [fetch(2, ldin, ldv), fetch(3, xin, x), fetch(4, gin_, g), fetch(5, bmin, bm), fetch(6, cmin, cm)]
    late_in = [
        fetch(7, qin, q), fetch(8, mkin, metas.at[:, 0:HD, :]), fetch(9, mvin, metas.at[:, HD : 2 * HD, :])
    ]

    def pair(src, dst, send, recv, n, to):
        return pltpu.make_async_remote_copy(
            src_ref=src, dst_ref=dst, send_sem=send.at[n], recv_sem=recv.at[n],
            device_id=to, device_id_type=MESH,
        )

    for copy in first_in:
        copy.wait()
    pl.semaphore_wait(barrier, 27)
    for k in (4, 12):
        pl.semaphore_signal(
            vouch, inc=1, device_id=(dp, 4 * ((z + k) % 16) + c), device_id_type=MESH
        )

    def kv_copies(n, lo, hi):
        def step(src, dst, m, to):
            return pair(win.at[src, lo:hi], win.at[dst, lo:hi], kv_send, kv_recv, 4 * n + m, (dp, to))

        def to_mate(d, m):
            there = (d + core * 9 + (1 - core)) % 10
            return pair(win.at[d, lo:hi], win.at[there, lo:hi], c_send, c_recv, 5 * n + m, (dp, mate))

        steps = (step(0, 2, 0, ahead2), step(0, 4, 1, ahead4), step(2, 6, 2, ahead4), step(4, 8, 3, ahead4))
        return steps, [to_mate(d, m) for m, d in enumerate((0, 2, 4, 6, 8))]

    halves = [kv_copies(0, 0, 2), kv_copies(1, 2, KVH)]
    for steps, mates in halves:
        steps[0].start()
        steps[1].start()
        mates[0].start()

    def forward(n):
        steps, mates = halves[n]
        steps[0].wait_recv()
        steps[2].start()
        mates[1].start()
        steps[1].wait_recv()
        steps[3].start()
        mates[2].start()

    def finish(n):
        steps, mates = halves[n]
        steps[2].wait_recv()
        mates[3].start()
        steps[3].wait_recv()
        mates[4].start()

    for copy in scan_in:
        copy.wait()
    rows, cols = iota((TOK, TOK), 0), iota((TOK, TOK), 1)
    tri = (rows >= cols).astype(BF)
    ldp[...] = jnp.zeros((32, TOK), F32)
    for h in range(HEADS):
        ldp[h : h + 1, :] = ldv[h]
    run = jnp.zeros((TOK, 32), F32)
    run_t = jnp.zeros((32, TOK), F32)
    for part in split3(ldp[...]):
        run = run + dot(tri, part, NT)
        run_t = run_t + dot(part, tri, NT)
    end = run_t[:, TOK - 1 : TOK]
    tail = jnp.exp(end - run_t)
    head = jnp.exp(run_t)
    for h in range(HEADS):
        f = slice(HD * h, HD * h + HD)
        xt[f, :] = (tail[h : h + 1, :] * x[f, :].astype(F32)).astype(BF)
        gt[f, :] = (head[h : h + 1, :] * g[f, :].astype(F32)).astype(BF)
    for w, terms in enumerate((dot(bm[...], xt[...], NT), dot(cm[...], gt[...], NT))):
        for p in range(4):
            n = min(QL, WIDTH - QL * p)
            stq[p, w] = jnp.concatenate(
                [terms[:, QL * p : QL * p + n], jnp.zeros((STATE, 512 - n), F32)], axis=1
            ).astype(BF)
    d0[...] = jnp.broadcast_to(jnp.exp(run[TOK - 1 : TOK, :]), (8, 32))
    q1 = []
    for n, k in enumerate((1, 2, 3)):
        q1.append(pair(stq.at[(c + k) % 4], r1.at[c], q1_send, q1_recv, n, (dp, group[n])))
        q1.append(pair(d0, d1.at[c], q1_send, q1_recv, 3 + n, (dp, group[n])))
    for copy in q1:
        copy.start()
    r1[c] = stq[c]
    d1[c] = d0[...]

    inner = dot(cm[...], bm[...], TN)

    def local_head(h, gram):
        f = slice(HD * h, HD * h + HD)
        diff = run[:, h : h + 1] - run_t[h : h + 1, :]
        mix = jnp.where(rows >= cols, jnp.exp(diff), 0.0)
        loc[f, :] = dot(g[f, :], (mix * inner).astype(BF))
        return gram + mix * dot(g[f, :], x[f, :], TN)

    gram = jnp.zeros((TOK, TOK), F32)
    for h in range(0, 8):
        gram = local_head(h, gram)
    forward(0)

    for copy in late_in:
        copy.wait()
    zeros = jnp.zeros((HD, TOK), BF)
    for k in range(KVH):
        for j in range(GROUP):
            f = slice(HD * (GROUP * k + j), HD * (GROUP * k + j) + HD)
            at = 2 * TOK * j
            qg[k, 0:HD, at : at + TOK] = (q[f, :].astype(F32) * 0.125).astype(BF)
            qg[k, 0:HD, at + TOK : at + 2 * TOK] = zeros
            qg[k, HD : 2 * HD, at : at + TOK] = zeros
            qg[k, HD : 2 * HD, at + TOK : at + 2 * TOK] = g[f, :]
    behind_by = rows - cols
    never = jnp.int32(1 << 20)
    dist[:, 0:TOK] = jnp.zeros((TOK, TOK), jnp.int32)
    dist[:, TOK : 2 * TOK] = jnp.where(behind_by >= 0, behind_by, never)
    for d in range(1, 9):
        dist[:, TOK * (d + 1) : TOK * (d + 2)] = jnp.where(i >= d, behind_by + TOK * d, never)
    pieces[9] = jnp.zeros((KVH, TOK, TOK), BF)

    for h in range(8, 14):
        gram = local_head(h, gram)
    finish(0)
    forward(1)

    row, lane = iota((32, 512), 0), iota((32, 512), 1)
    onehot = ((row == 7 * c + lane // HD) & (lane < QL)).astype(BF)

    def expand(d):
        wide = dot3(d[...].reshape(32, 32), onehot)
        return [jnp.broadcast_to(wide[8 * j : 8 * j + 1], (STATE, 512)) for j in range(4)]

    def sums(dec, terms):
        total, back = terms[0, 0].astype(F32), terms[3, 1].astype(F32)
        for j in range(1, 4):
            total = dec[j] * total + terms[j, 0].astype(F32)
            back = dec[3 - j] * back + terms[3 - j, 1].astype(F32)
        return total.astype(BF), back.astype(BF)

    q2 = []
    for n in range(3):
        q2.append(pair(s2, r2.at[zl], q2_send, q2_recv, n, (dp, near[n])))
        q2.append(pair(d2s, d2.at[zl], q2_send, q2_recv, 3 + n, (dp, near[n])))
    q3 = []
    for n, k in enumerate((1, 2, 3)):
        there = (zh + k) % 4
        which = jnp.where(there > zh, 0, 1)
        q3.append(pair(s3.at[which], r3.at[zh], q3_send, q3_recv, n, (dp, far[n])))
        q3.append(pair(d3s, d3.at[zh], q3_send, q3_recv, 3 + n, (dp, far[n])))
    q4 = [
        pair(ib.at[(c + k) % 4], ob.at[c], q4_send, q4_recv, n, (dp, group[n]))
        for n, k in enumerate((1, 2, 3))
    ]

    def scan_second():
        for copy in q1:
            copy.wait_recv()
        s2[0], s2[1] = sums(expand(d1), r1)
        d2s[...] = d1[0] * d1[1] * d1[2] * d1[3]
        for copy in q2:
            copy.start()
        r2[zl] = s2[...]
        d2[zl] = d2s[...]

    def scan_third():
        for copy in q2:
            copy.wait_recv()
        pl.semaphore_wait(vouch, 2)
        s3[0], s3[1] = sums(expand(d2), r2)
        d3s[...] = d2[0] * d2[1] * d2[2] * d2[3]
        for copy in q3:
            copy.start()
        r3[zh] = s3[0]
        d3[zh] = d3s[...]

    def scan_fourth():
        for copy in q3:
            copy.wait_recv()
        dec1, dec2, dec3 = expand(d1), expand(d2), expand(d3)
        ahead = jnp.zeros((STATE, 512), F32)
        behind = ahead
        for j in range(4):
            b = 3 - j
            ahead = jnp.where(j < zh, dec3[j] * ahead + r3[j].astype(F32), ahead)
            behind = jnp.where(b > zh, dec3[b] * behind + r3[b].astype(F32), behind)
        for j in range(4):
            b = 3 - j
            ahead = jnp.where(j < zl, dec2[j] * ahead + r2[j, 0].astype(F32), ahead)
            behind = jnp.where(b > zl, dec2[b] * behind + r2[b, 1].astype(F32), behind)
        for j in range(4):
            b = 3 - j
            ib[j, 0] = ahead.astype(BF)
            ahead = dec1[j] * ahead + r1[j, 0].astype(F32)
            ib[b, 1] = behind.astype(BF)
            behind = dec1[b] * behind + r1[b, 1].astype(F32)
        for copy in q4:
            copy.start()
        ob[c] = ib[c]

    scan_second()
    for copy in halves[0][1]:
        copy.wait_recv()

    def keys_of(k):
        return jnp.concatenate([metas[k]] + [win[d, k] for d in range(9)], axis=1)

    def probs_of(k, carry):
        kv = keys_of(k)
        for j in range(GROUP):
            at = 2 * TOK * j
            both = dot(qg[k, :, at : at + 2 * TOK], kv, TN)
            s, dpr = both[:TOK], both[TOK:]
            s = jnp.where(dist[...] < wins[GROUP * k + j], s, -1e30)
            e = jnp.exp(s - jnp.max(s, axis=1, keepdims=True))
            inv = 1.0 / jnp.sum(e, axis=1, keepdims=True)
            delta = jnp.sum(e * dpr, axis=1, keepdims=True) * inv
            p = e * inv
            ps[k, at : at + TOK, :] = (p * (dpr - delta)).astype(BF)
            ps[k, at + TOK : at + 2 * TOK, :] = p.astype(BF)
        turned = dot(qg[k], ps[k, :, 0:TOK]).T
        for r in range(16):
            sink[r % 2, (r // 2) % 4, r // 8, k] = turned[8 * r : 8 * r + 8]

        @pl.when(k == 0)
        def _():
            finish(1)

        @pl.when(k == 1)
        def _():
            for copy in halves[1][1]:
                copy.wait_recv()
            scan_third()

        return carry

    lax.fori_loop(0, KVH, probs_of, 0)

    held = (20 * z) // 64 - (20 * z) // 256
    m0 = pair(sink.at[1 - core], k0, m_send, m_recv, 0, (dp, mate))
    m1 = [
        pair(a0.at[to[0] % 4, to[0] // 4], k1.at[n], m_send, m_recv, 1 + n, to) for n, to in enumerate(along_xy)
    ]
    m2 = [
        pair(a2.at[pl.ds((20 * to) // 64 - (20 * to) // 256, 2)], k4.at[n], m_send, m_recv, 16 + n, (dp, 4 * to + c))
        for n, to in enumerate(along_z)
    ]
    m3 = pair(a4, k5, m_send, m_recv, 31, (dp, mate))

    def total(own_part, parts):
        for n in range(15):
            own_part = own_part + parts[n]
        return own_part

    def pass_on(arrived, result, value, following):
        for copy in arrived:
            copy.wait_recv()
        result[...] = value()
        for copy in following:
            copy.start()

    m0.start()

    parts = ((0, 2), (2, 4), (4, KVH))
    order = (6, 8, 2, 4, 0)
    gives = [
        [
            pair(
                pieces.at[(d + core + 9 * (1 - core)) % 10, lo:hi], rc.at[m, lo:hi],
                e_send, e_recv, 5 * n + m, (dp, mate),
            )
            for m, d in enumerate(order)
        ]
        for n, (lo, hi) in enumerate(parts)
    ]
    backs = [
        [
            pair(src.at[lo:hi], dst.at[lo:hi], t_send, t_recv, 4 * n + m, (dp, to))
            for m, (src, dst, to) in enumerate(
                ((sb, rz.at[1], back4), (sc, rz.at[0], back4), (sy, ry, back2), (sa, rz.at[2], back4))
            )
        ]
        for n, (lo, hi) in enumerate(parts)
    ]

    def send_far(n):
        lo, hi = parts[n]
        for m, out in ((0, sb), (1, sc)):
            gives[n][m].wait_recv()
            out[lo:hi] = (pieces[order[m], lo:hi].astype(F32) + rc[m, lo:hi].astype(F32)).astype(BF)
            backs[n][m].start()

    def send_near(n, m, out, arrived):
        lo, hi = parts[n]
        gives[n][m].wait_recv()
        backs[n][m - 2].wait_recv()
        part = pieces[order[m], lo:hi].astype(F32) + rc[m, lo:hi].astype(F32)
        out[lo:hi] = (part + rz[arrived, lo:hi].astype(F32)).astype(BF)
        backs[n][m].start()

    def grads_of(k, carry):
        kv = keys_of(k)
        for j in range(GROUP):
            at = 2 * TOK * j
            dq = dot(kv[0:HD], ps[k, at : at + TOK, :], NT) * 0.125
            gq[pl.ds(pl.multiple_of(HD * (GROUP * k + j), HD), HD), :] = dq.astype(BF)
        back_t = dot(qg[k], ps[k, :, TOK:])
        own[k] = back_t[:, :TOK]
        for d in range(1, 9):
            pieces[d, k] = back_t[:, TOK * d : TOK * (d + 1)].astype(BF)

        @pl.when(k == 0)
        def _():
            pass_on([m0], a0, lambda: sink[core] + k0[...], m1)
            scan_fourth()

        @pl.when(k == 1)
        def _():
            for copy in gives[0]:
                copy.start()

        @pl.when(k == 2)
        def _():
            send_far(0)

        @pl.when(k == 3)
        def _():
            for copy in gives[1]:
                copy.start()

        @pl.when(k == 4)
        def _():
            for copy in gives[2]:
                copy.start()
            send_far(1)
            pass_on(m1, a2, lambda: total(a0[xx, yl], k1), m2)

        return carry

    lax.fori_loop(0, KVH, grads_of, 0)

    send_far(2)
    for n in (0, 1):
        send_near(n, 2, sy, 1)
        send_near(n, 3, sa, 0)

    for copy in q4:
        copy.wait_recv()
    for p in range(4):
        n = min(QL, WIDTH - QL * p)
        inc[:, QL * p : QL * p + n] = ob[p, 0].astype(F32)[:, :n]
        adj[:, QL * p : QL * p + n] = ob[p, 1].astype(F32)[:, :n]
    inc_h, adj_h = inc[...].astype(BF), adj[...].astype(BF)
    grad_bm = dot(adj_h, xt[...])
    grad_cm = dot(inc_h, gt[...])

    send_near(2, 2, sy, 1)
    send_near(2, 3, sa, 0)

    for h in range(14, HEADS):
        gram = local_head(h, gram)
    gram = gram.astype(BF)
    gbm[...] = grad_bm + dot(cm[...], gram)
    gcm[...] = grad_cm + dot(bm[...], gram, NT)
    carried = dot(adj_h, bm[...], TN)
    tail = jnp.exp(end - run_t)
    for h in range(HEADS):
        f = slice(HD * h, HD * h + HD)
        gin[f, :] = (loc[f, :] + tail[h : h + 1, :] * carried[f]).astype(BF)

    pass_on(m2, a4, lambda: total(a2[pl.ds(held, 2)], k4), [m3])
    for n in range(3):
        gives[n][4].wait_recv()
        backs[n][2].wait_recv()
        backs[n][3].wait_recv()
    for k in range(KVH):
        mine = own[k] + rc[4, k].astype(F32) + ry[k].astype(F32) + rz[2, k].astype(F32)
        gk[HD * k : HD * k + HD, :] = mine[:HD].astype(BF)
        gv[HD * k : HD * k + HD, :] = mine[HD:].astype(BF)

    m3.wait_recv()
    row, lane = iota((16, TOK), 0), iota((16, TOK), 1)
    first = jnp.zeros((16, 8), F32)
    second = jnp.zeros((16, 8), F32)
    for k in range(2):
        feature = 5 * i + row % 8 - HD * (held + k)
        pick = (row % 8 < 5) & (feature >= 0) & (feature < HD) & (lane == feature + HD * (row // 8))
        pick = pick.astype(BF)
        for part in split3(a4[k]):
            first = first + dot(pick, part, NT)
        for part in split3(k5[k]):
            second = second + dot(pick, part, NT)
    left = jnp.where(core == 0, first, second)
    right = jnp.where(core == 0, second, first)
    for j in range(5):
        for w in range(2):
            gm[j, w : w + 1, 0:8] = left[8 * w + j : 8 * w + j + 1]
            gm[j, w : w + 1, 8:16] = right[8 * w + j : 8 * w + j + 1]

    for copy in q1 + q2 + q3 + q4 + [m0, m3] + m1 + m2:
        copy.wait_send()
    for steps, mates in halves:
        for copy in list(steps) + mates:
            copy.wait_send()
    for copy in sum(gives, []) + sum(backs, []):
        copy.wait_send()


OUTS = (
    ((WIDTH, TOK), BF), ((KVW, TOK), BF), ((KVW, TOK), BF), ((5, 2, 16), F32),
    ((WIDTH, TOK), BF), ((STATE, TOK), F32), ((STATE, TOK), F32),
)


def run_layer(*args):
    dma = pltpu.SemaphoreType.DMA
    vm = pltpu.VMEM
    block = (KVH, TOK, TOK)
    part = (KVH, 8, TOK)
    quarter = (2, STATE, 512)
    return pl.pallas_call(
        layer_kernel,
        out_shape=tuple(jax.ShapeDtypeStruct(s, t) for s, t in OUTS),
        in_specs=[pl.BlockSpec(memory_space=pltpu.SMEM)] + [pl.BlockSpec(memory_space=pl.ANY)] * 10,
        out_specs=(pl.BlockSpec(memory_space=vm),) * 7,
        scratch_shapes=[
            vm((WIDTH, TOK), BF), vm((WIDTH, TOK), BF), vm((WIDTH, TOK), BF),
            vm((STATE, TOK), BF), vm((STATE, TOK), BF), vm((HEADS, 1, TOK), F32), vm((32, TOK), F32),
            vm((WIDTH, TOK), BF), vm((WIDTH, TOK), BF), vm((WIDTH, TOK), F32),
            vm((10,) + block, BF), vm(block, BF), vm((KVH, TOK, 2 * TOK * GROUP), BF),
            vm((TOK, 10 * TOK), jnp.int32), vm((KVH, 2 * TOK * GROUP, 10 * TOK), BF),
            vm((10,) + block, BF), vm(block, F32), vm((2, 4, 2) + part, F32),
            vm((4,) + quarter, BF), vm((4,) + quarter, BF), vm((8, 32), F32), vm((4, 8, 32), F32),
            vm(quarter, BF), vm((4,) + quarter, BF), vm((8, 32), F32), vm((4, 8, 32), F32),
            vm(quarter, BF), vm((4, STATE, 512), BF), vm((8, 32), F32), vm((4, 8, 32), F32),
            vm((4,) + quarter, BF), vm((4,) + quarter, BF), vm((STATE, WIDTH), F32), vm((STATE, WIDTH), F32),
            vm((5,) + block, BF), vm(block, BF), vm((3,) + block, BF),
            vm(block, BF), vm(block, BF), vm(block, BF), vm(block, BF),
            vm((4, 2) + part, F32), vm((4, 2) + part, F32),
            vm((15,) + part, F32), vm(part, F32), vm((15, 2, 8, TOK), F32), vm((2, 8, TOK), F32), vm((2, 8, TOK), F32),
            dma((10,)), dma((8,)), dma((8,)), dma((10,)), dma((10,)),
            dma((6,)), dma((6,)), dma((6,)), dma((6,)), dma((6,)), dma((6,)), dma((3,)), dma((3,)),
            dma((15,)), dma((15,)), dma((12,)), dma((12,)), dma((32,)), dma((32,)), pltpu.SemaphoreType.REGULAR,
        ],
        compiler_params=pltpu.CompilerParams(
            collective_id=0, has_side_effects=True, vmem_limit_bytes=56 * 1024 * 1024
        ),
        name="layer_grads",
    )(*args)


def hand_out_kernel(*refs):
    sources, targets, through, sem = refs[:7], refs[7:14], refs[14:21], refs[21]
    arrive = [pltpu.make_async_copy(a, b, sem.at[n]) for n, (a, b) in enumerate(zip(sources, through))]
    leave = [pltpu.make_async_copy(a, b, sem.at[7 + n]) for n, (a, b) in enumerate(zip(through, targets))]
    for copy in arrive:
        copy.start()
    for first, then in zip(arrive, leave):
        first.wait()
        then.start()
    for copy in leave:
        copy.wait()


def hand_out(arrays):
    return pl.pallas_call(
        hand_out_kernel,
        out_shape=tuple(jax.ShapeDtypeStruct(s, t) for s, t in OUTS),
        in_specs=[pl.BlockSpec(memory_space=pl.ANY)] * 7,
        out_specs=(pl.BlockSpec(memory_space=pl.ANY),) * 7,
        scratch_shapes=[pltpu.VMEM(s, t) for s, t in OUTS] + [pltpu.SemaphoreType.DMA((14,))],
        compiler_params=pltpu.CompilerParams(vmem_limit_bytes=60 * 1024 * 1024),
        name="hand_out",
    )(*arrays)


def local(
    queries, key_vectors, value_vectors, meta_keys, meta_values, windows,
    ssm_input, input_map, output_map, log_decay, cotangent,
):
    def turn(a):
        return jnp.swapaxes(a, -1, -2)

    def by_head(a):
        return turn(a).reshape(KVH, HD, TOK)

    grad_q, grad_k, grad_v, grad_meta, grad_input, grad_bm, grad_cm = hand_out(
        run_layer(
            windows, by_head(key_vectors[0]), by_head(value_vectors[0]), turn(ssm_input[0]), turn(cotangent[0]),
            turn(queries[0]), turn(input_map[0]), turn(output_map[0]), log_decay.transpose(2, 0, 1),
            by_head(meta_keys), by_head(meta_values),
        )
    )
    return (
        turn(grad_q)[None], turn(grad_k)[None], turn(grad_v)[None], grad_meta.transpose(1, 2, 0),
        turn(grad_input)[None], turn(grad_bm)[None], turn(grad_cm)[None],
    )


def solution(mesh):
    seq = P("dp", "ctx", None)
    return jax.shard_map(
        local,
        mesh=mesh,
        in_specs=(seq, seq, seq, P(), P(), P(), seq, seq, seq, seq, seq),
        out_specs=(seq, seq, seq, P(None, "dp", "ctx"), seq, seq, seq),
        check_vma=False,
    )
```

```python
import functools

import jax
import jax.numpy as jnp
from jax import lax
from jax.experimental import pallas as pl
from jax.experimental.pallas import tpu as pltpu
from jax.sharding import PartitionSpec as P

BF = jnp.bfloat16
F32 = jnp.float32
MESH = pl.DeviceIdType.MESH
HEADS, KVH, GROUP, HD = 25, 5, 5, 64
TOK, WIDTH, KVW, STATE = 128, 1600, 320, 16
QL = 448
NT = (((1,), (1,)), ((), ()))
TN = (((0,), (0,)), ((), ()))


def dot(a, b, dims=(((1,), (0,)), ((), ()))):
    return lax.dot_general(a, b, dims, preferred_element_type=F32)


def split3(v):
    hi = v.astype(BF)
    rest = v - hi.astype(F32)
    mid = rest.astype(BF)
    low = (rest - mid.astype(F32)).astype(BF)
    return hi, mid, low


def dot3(v, onehot):
    hi, mid, low = split3(v)
    return dot(hi, onehot) + dot(mid, onehot) + dot(low, onehot)


def iota(shape, dim):
    return lax.broadcasted_iota(jnp.int32, shape, dim)


def places():
    dp, i = lax.axis_index("dp"), lax.axis_index("ctx")
    return dp, i, i % 2, (i // 2) % 2, i // 4


def layer_kernel(
    wins, key, val, xin, gin_, qin, bmin, cmin, ldin, mkin, mvin,
    gq, gk, gv, gm, gin, gbm, gcm,
    x, g, q, bm, cm, ldv, ldp, xt, gt, loc, win, metas, qg, dist, ps, pieces, own, sink,
    stq, r1, d0, d1, s2, r2, d2s, d2, s3, r3, d3s, d3, ib, ob, inc, adj,
    rc, ry, rz, sc, sb, sy, sa, k0, a0, k1, a2, k4, a4, k5,
    in_sem, kv_send, kv_recv, c_send, c_recv, q1_send, q1_recv, q2_send, q2_recv, q3_send, q3_recv,
    q4_send, q4_recv, e_send, e_recv, t_send, t_recv, m_send, m_recv, vouch,
):
    dp, i, core, yh, z = places()
    c = i % 4
    zl, zh = z % 4, z // 4
    xx, yl = dp % 4, dp // 4
    base = i - c
    ahead2, ahead4 = (i + 2) % 64, (i + 4) % 64
    back2, back4 = (i + 62) % 64, (i + 60) % 64
    along_z = [(z + k) % 16 for k in range(1, 16)]
    group = [base + (c + k) % 4 for k in (1, 2, 3)]
    near = [(zh * 4 + (zl + k) % 4) * 4 + c for k in (1, 2, 3)]
    far = [(((zh + k) % 4) * 4 + zl) * 4 + c for k in (1, 2, 3)]
    mate = base + (c + 1 - 2 * core)
    across = base + (c + 2) % 4
    diag = across + 1 - 2 * core
    along_xy = [
        (((yl + a) % 2) * 4 + (xx + k) % 4, base + ((yh + b) % 2) * 2 + core)
        for k in range(4) for a in range(2) for b in range(2) if k + a + b > 0
    ]

    barrier = pltpu.get_barrier_semaphore()
    close = [(z + k) % 16 for k in (1, 2, 3, 4, 12, 13, 14, 15)]
    for to in [(dp, 4 * there + c) for there in close] + along_xy + [(dp, o) for o in (mate, diag, ahead2, back2)]:
        pl.semaphore_signal(barrier, inc=1, device_id=to, device_id_type=MESH)

    def fetch(n, src, dst):
        copy = pltpu.make_async_copy(src, dst, in_sem.at[n])
        copy.start()
        return copy

    first_in = [fetch(0, key, win.at[0, :, 0:HD, :]), fetch(1, val, win.at[0, :, HD : 2 * HD, :])]
    scan_in = [fetch(2, ldin, ldv), fetch(3, xin, x), fetch(4, gin_, g), fetch(5, bmin, bm), fetch(6, cmin, cm)]
    late_in = [
        fetch(7, qin, q), fetch(8, mkin, metas.at[:, 0:HD, :]), fetch(9, mvin, metas.at[:, HD : 2 * HD, :])
    ]

    def pair(src, dst, send, recv, n, to):
        return pltpu.make_async_remote_copy(
            src_ref=src, dst_ref=dst, send_sem=send.at[n], recv_sem=recv.at[n],
            device_id=to, device_id_type=MESH,
        )

    for copy in first_in:
        copy.wait()
    pl.semaphore_wait(barrier, 27)
    for k in (4, 12):
        pl.semaphore_signal(
            vouch, inc=1, device_id=(dp, 4 * ((z + k) % 16) + c), device_id_type=MESH
        )

    def kv_copies(n, lo, hi):
        def step(src, dst, m, to):
            return pair(win.at[src, lo:hi], win.at[dst, lo:hi], kv_send, kv_recv, 4 * n + m, (dp, to))

        def to_mate(d, m):
            there = (d + core * 9 + (1 - core)) % 10
            return pair(win.at[d, lo:hi], win.at[there, lo:hi], c_send, c_recv, 5 * n + m, (dp, mate))

        steps = (step(0, 2, 0, ahead2), step(0, 4, 1, ahead4), step(2, 6, 2, ahead4), step(4, 8, 3, ahead4))
        return steps, [to_mate(d, m) for m, d in enumerate((0, 2, 4, 6, 8))]

    halves = [kv_copies(0, 0, 2), kv_copies(1, 2, KVH)]
    for steps, mates in halves:
        steps[0].start()
        steps[1].start()
        mates[0].start()

    def forward(n):
        steps, mates = halves[n]
        steps[0].wait_recv()
        steps[2].start()
        mates[1].start()
        steps[1].wait_recv()
        steps[3].start()
        mates[2].start()

    def finish(n):
        steps, mates = halves[n]
        steps[2].wait_recv()
        mates[3].start()
        steps[3].wait_recv()
        mates[4].start()

    for copy in scan_in:
        copy.wait()
    rows, cols = iota((TOK, TOK), 0), iota((TOK, TOK), 1)
    tri = (rows >= cols).astype(BF)
    ldp[...] = jnp.zeros((32, TOK), F32)
    for h in range(HEADS):
        ldp[h : h + 1, :] = ldv[h]
    run = jnp.zeros((TOK, 32), F32)
    run_t = jnp.zeros((32, TOK), F32)
    for part in split3(ldp[...]):
        run = run + dot(tri, part, NT)
        run_t = run_t + dot(part, tri, NT)
    end = run_t[:, TOK - 1 : TOK]
    tail = jnp.exp(end - run_t)
    head = jnp.exp(run_t)
    for h in range(HEADS):
        f = slice(HD * h, HD * h + HD)
        xt[f, :] = (tail[h : h + 1, :] * x[f, :].astype(F32)).astype(BF)
        gt[f, :] = (head[h : h + 1, :] * g[f, :].astype(F32)).astype(BF)
    for w, terms in enumerate((dot(bm[...], xt[...], NT), dot(cm[...], gt[...], NT))):
        for p in range(4):
            n = min(QL, WIDTH - QL * p)
            stq[p, w] = jnp.concatenate(
                [terms[:, QL * p : QL * p + n], jnp.zeros((STATE, 512 - n), F32)], axis=1
            ).astype(BF)
    d0[...] = jnp.broadcast_to(jnp.exp(run[TOK - 1 : TOK, :]), (8, 32))
    q1 = []
    for n, k in enumerate((1, 2, 3)):
        q1.append(pair(stq.at[(c + k) % 4], r1.at[c], q1_send, q1_recv, n, (dp, group[n])))
        q1.append(pair(d0, d1.at[c], q1_send, q1_recv, 3 + n, (dp, group[n])))
    for copy in q1:
        copy.start()
    r1[c] = stq[c]
    d1[c] = d0[...]

    inner = dot(cm[...], bm[...], TN)

    def local_head(h, gram):
        f = slice(HD * h, HD * h + HD)
        diff = run[:, h : h + 1] - run_t[h : h + 1, :]
        mix = jnp.where(rows >= cols, jnp.exp(diff), 0.0)
        loc[f, :] = dot(g[f, :], (mix * inner).astype(BF))
        return gram + mix * dot(g[f, :], x[f, :], TN)

    gram = jnp.zeros((TOK, TOK), F32)
    for h in range(0, 8):
        gram = local_head(h, gram)
    forward(0)

    for copy in late_in:
        copy.wait()
    zeros = jnp.zeros((HD, TOK), BF)
    for k in range(KVH):
        for j in range(GROUP):
            f = slice(HD * (GROUP * k + j), HD * (GROUP * k + j) + HD)
            at = 2 * TOK * j
            qg[k, 0:HD, at : at + TOK] = (q[f, :].astype(F32) * 0.125).astype(BF)
            qg[k, 0:HD, at + TOK : at + 2 * TOK] = zeros
            qg[k, HD : 2 * HD, at : at + TOK] = zeros
            qg[k, HD : 2 * HD, at + TOK : at + 2 * TOK] = g[f, :]
    behind_by = rows - cols
    never = jnp.int32(1 << 20)
    dist[:, 0:TOK] = jnp.zeros((TOK, TOK), jnp.int32)
    dist[:, TOK : 2 * TOK] = jnp.where(behind_by >= 0, behind_by, never)
    for d in range(1, 9):
        dist[:, TOK * (d + 1) : TOK * (d + 2)] = jnp.where(i >= d, behind_by + TOK * d, never)
    pieces[9] = jnp.zeros((KVH, TOK, TOK), BF)

    for h in range(8, 14):
        gram = local_head(h, gram)
    finish(0)
    forward(1)

    row, lane = iota((32, 512), 0), iota((32, 512), 1)
    onehot = ((row == 7 * c + lane // HD) & (lane < QL)).astype(BF)

    def expand(d):
        wide = dot3(d[...].reshape(32, 32), onehot)
        return [jnp.broadcast_to(wide[8 * j : 8 * j + 1], (STATE, 512)) for j in range(4)]

    def sums(dec, terms):
        total, back = terms[0, 0].astype(F32), terms[3, 1].astype(F32)
        for j in range(1, 4):
            total = dec[j] * total + terms[j, 0].astype(F32)
            back = dec[3 - j] * back + terms[3 - j, 1].astype(F32)
        return total.astype(BF), back.astype(BF)

    q2 = []
    for n in range(3):
        q2.append(pair(s2, r2.at[zl], q2_send, q2_recv, n, (dp, near[n])))
        q2.append(pair(d2s, d2.at[zl], q2_send, q2_recv, 3 + n, (dp, near[n])))
    q3 = []
    for n, k in enumerate((1, 2, 3)):
        there = (zh + k) % 4
        which = jnp.where(there > zh, 0, 1)
        q3.append(pair(s3.at[which], r3.at[zh], q3_send, q3_recv, n, (dp, far[n])))
        q3.append(pair(d3s, d3.at[zh], q3_send, q3_recv, 3 + n, (dp, far[n])))
    q4 = [
        pair(ib.at[(c + k) % 4], ob.at[c], q4_send, q4_recv, n, (dp, group[n]))
        for n, k in enumerate((1, 2, 3))
    ]

    def scan_second():
        for copy in q1:
            copy.wait_recv()
        s2[0], s2[1] = sums(expand(d1), r1)
        d2s[...] = d1[0] * d1[1] * d1[2] * d1[3]
        for copy in q2:
            copy.start()
        r2[zl] = s2[...]
        d2[zl] = d2s[...]

    def scan_third():
        for copy in q2:
            copy.wait_recv()
        pl.semaphore_wait(vouch, 2)
        s3[0], s3[1] = sums(expand(d2), r2)
        d3s[...] = d2[0] * d2[1] * d2[2] * d2[3]
        for copy in q3:
            copy.start()
        r3[zh] = s3[0]
        d3[zh] = d3s[...]

    def scan_fourth():
        for copy in q3:
            copy.wait_recv()
        dec1, dec2, dec3 = expand(d1), expand(d2), expand(d3)
        ahead = jnp.zeros((STATE, 512), F32)
        behind = ahead
        for j in range(4):
            b = 3 - j
            ahead = jnp.where(j < zh, dec3[j] * ahead + r3[j].astype(F32), ahead)
            behind = jnp.where(b > zh, dec3[b] * behind + r3[b].astype(F32), behind)
        for j in range(4):
            b = 3 - j
            ahead = jnp.where(j < zl, dec2[j] * ahead + r2[j, 0].astype(F32), ahead)
            behind = jnp.where(b > zl, dec2[b] * behind + r2[b, 1].astype(F32), behind)
        for j in range(4):
            b = 3 - j
            ib[j, 0] = ahead.astype(BF)
            ahead = dec1[j] * ahead + r1[j, 0].astype(F32)
            ib[b, 1] = behind.astype(BF)
            behind = dec1[b] * behind + r1[b, 1].astype(F32)
        for copy in q4:
            copy.start()
        ob[c] = ib[c]

    scan_second()
    for copy in halves[0][1]:
        copy.wait_recv()

    def keys_of(k):
        return jnp.concatenate([metas[k]] + [win[d, k] for d in range(9)], axis=1)

    def probs_of(k, carry):
        kv = keys_of(k)
        for j in range(GROUP):
            at = 2 * TOK * j
            both = dot(qg[k, :, at : at + 2 * TOK], kv, TN)
            s, dpr = both[:TOK], both[TOK:]
            s = jnp.where(dist[...] < wins[GROUP * k + j], s, -1e30)
            e = jnp.exp(s - jnp.max(s, axis=1, keepdims=True))
            inv = 1.0 / jnp.sum(e, axis=1, keepdims=True)
            delta = jnp.sum(e * dpr, axis=1, keepdims=True) * inv
            p = e * inv
            ps[k, at : at + TOK, :] = (p * (dpr - delta)).astype(BF)
            ps[k, at + TOK : at + 2 * TOK, :] = p.astype(BF)
        turned = dot(qg[k], ps[k, :, 0:TOK]).T
        for r in range(16):
            sink[r % 2, (r // 2) % 4, r // 8, k] = turned[8 * r : 8 * r + 8]

        @pl.when(k == 0)
        def _():
            finish(1)

        @pl.when(k == 1)
        def _():
            for copy in halves[1][1]:
                copy.wait_recv()
            scan_third()

        return carry

    lax.fori_loop(0, KVH, probs_of, 0)

    held = (20 * z) // 64 - (20 * z) // 256
    m0 = pair(sink.at[1 - core], k0, m_send, m_recv, 0, (dp, mate))
    m1 = [
        pair(a0.at[to[0] % 4, to[0] // 4], k1.at[n], m_send, m_recv, 1 + n, to) for n, to in enumerate(along_xy)
    ]
    m2 = [
        pair(a2.at[pl.ds((20 * to) // 64 - (20 * to) // 256, 2)], k4.at[n], m_send, m_recv, 16 + n, (dp, 4 * to + c))
        for n, to in enumerate(along_z)
    ]
    m3 = pair(a4, k5, m_send, m_recv, 31, (dp, mate))

    def total(own_part, parts):
        for n in range(15):
            own_part = own_part + parts[n]
        return own_part

    def pass_on(arrived, result, value, following):
        for copy in arrived:
            copy.wait_recv()
        result[...] = value()
        for copy in following:
            copy.start()

    m0.start()

    parts = ((0, 2), (2, 4), (4, KVH))
    order = (6, 8, 2, 4, 0)
    gives = [
        [
            pair(
                pieces.at[(d + core + 9 * (1 - core)) % 10, lo:hi], rc.at[m, lo:hi],
                e_send, e_recv, 5 * n + m, (dp, mate),
            )
            for m, d in enumerate(order)
        ]
        for n, (lo, hi) in enumerate(parts)
    ]
    backs = [
        [
            pair(src.at[lo:hi], dst.at[lo:hi], t_send, t_recv, 4 * n + m, (dp, to))
            for m, (src, dst, to) in enumerate(
                ((sb, rz.at[1], back4), (sc, rz.at[0], back4), (sy, ry, back2), (sa, rz.at[2], back4))
            )
        ]
        for n, (lo, hi) in enumerate(parts)
    ]

    def send_far(n):
        lo, hi = parts[n]
        for m, out in ((0, sb), (1, sc)):
            gives[n][m].wait_recv()
            out[lo:hi] = (pieces[order[m], lo:hi].astype(F32) + rc[m, lo:hi].astype(F32)).astype(BF)
            backs[n][m].start()

    def send_near(n, m, out, arrived):
        lo, hi = parts[n]
        gives[n][m].wait_recv()
        backs[n][m - 2].wait_recv()
        part = pieces[order[m], lo:hi].astype(F32) + rc[m, lo:hi].astype(F32)
        out[lo:hi] = (part + rz[arrived, lo:hi].astype(F32)).astype(BF)
        backs[n][m].start()

    def grads_of(k, carry):
        kv = keys_of(k)
        for j in range(GROUP):
            at = 2 * TOK * j
            dq = dot(kv[0:HD], ps[k, at : at + TOK, :], NT) * 0.125
            gq[pl.ds(pl.multiple_of(HD * (GROUP * k + j), HD), HD), :] = dq.astype(BF)
        back_t = dot(qg[k], ps[k, :, TOK:])
        own[k] = back_t[:, :TOK]
        for d in range(1, 9):
            pieces[d, k] = back_t[:, TOK * d : TOK * (d + 1)].astype(BF)

        @pl.when(k == 0)
        def _():
            pass_on([m0], a0, lambda: sink[core] + k0[...], m1)
            scan_fourth()

        @pl.when(k == 1)
        def _():
            for copy in gives[0]:
                copy.start()

        @pl.when(k == 2)
        def _():
            send_far(0)

        @pl.when(k == 3)
        def _():
            for copy in gives[1]:
                copy.start()

        @pl.when(k == 4)
        def _():
            for copy in gives[2]:
                copy.start()
            send_far(1)
            send_near(0, 2, sy, 1)
            send_near(0, 3, sa, 0)
            send_far(2)
            pass_on(m1, a2, lambda: total(a0[xx, yl], k1), m2)

        return carry

    lax.fori_loop(0, KVH, grads_of, 0)

    send_near(1, 2, sy, 1)
    send_near(1, 3, sa, 0)

    for copy in q4:
        copy.wait_recv()
    for p in range(4):
        n = min(QL, WIDTH - QL * p)
        inc[:, QL * p : QL * p + n] = ob[p, 0].astype(F32)[:, :n]
        adj[:, QL * p : QL * p + n] = ob[p, 1].astype(F32)[:, :n]
    inc_h, adj_h = inc[...].astype(BF), adj[...].astype(BF)
    grad_bm = dot(adj_h, xt[...])
    grad_cm = dot(inc_h, gt[...])

    send_near(2, 2, sy, 1)
    send_near(2, 3, sa, 0)

    for h in range(14, HEADS):
        gram = local_head(h, gram)
    gram = gram.astype(BF)
    gbm[...] = grad_bm + dot(cm[...], gram)
    gcm[...] = grad_cm + dot(bm[...], gram, NT)
    carried = dot(adj_h, bm[...], TN)
    tail = jnp.exp(end - run_t)
    for h in range(HEADS):
        f = slice(HD * h, HD * h + HD)
        gin[f, :] = (loc[f, :] + tail[h : h + 1, :] * carried[f]).astype(BF)

    pass_on(m2, a4, lambda: total(a2[pl.ds(held, 2)], k4), [m3])
    for n in range(3):
        gives[n][4].wait_recv()
        backs[n][2].wait_recv()
        backs[n][3].wait_recv()
    for k in range(KVH):
        mine = own[k] + rc[4, k].astype(F32) + ry[k].astype(F32) + rz[2, k].astype(F32)
        gk[HD * k : HD * k + HD, :] = mine[:HD].astype(BF)
        gv[HD * k : HD * k + HD, :] = mine[HD:].astype(BF)

    m3.wait_recv()
    row, lane = iota((16, TOK), 0), iota((16, TOK), 1)
    first = jnp.zeros((16, 8), F32)
    second = jnp.zeros((16, 8), F32)
    for k in range(2):
        feature = 5 * i + row % 8 - HD * (held + k)
        pick = (row % 8 < 5) & (feature >= 0) & (feature < HD) & (lane == feature + HD * (row // 8))
        pick = pick.astype(BF)
        for part in split3(a4[k]):
            first = first + dot(pick, part, NT)
        for part in split3(k5[k]):
            second = second + dot(pick, part, NT)
    left = jnp.where(core == 0, first, second)
    right = jnp.where(core == 0, second, first)
    for j in range(5):
        for w in range(2):
            gm[j, w : w + 1, 0:8] = left[8 * w + j : 8 * w + j + 1]
            gm[j, w : w + 1, 8:16] = right[8 * w + j : 8 * w + j + 1]

    for copy in q1 + q2 + q3 + q4 + [m0, m3] + m1 + m2:
        copy.wait_send()
    for steps, mates in halves:
        for copy in list(steps) + mates:
            copy.wait_send()
    for copy in sum(gives, []) + sum(backs, []):
        copy.wait_send()


OUTS = (
    ((WIDTH, TOK), BF), ((KVW, TOK), BF), ((KVW, TOK), BF), ((5, 2, 16), F32),
    ((WIDTH, TOK), BF), ((STATE, TOK), F32), ((STATE, TOK), F32),
)


def run_layer(*args):
    dma = pltpu.SemaphoreType.DMA
    vm = pltpu.VMEM
    block = (KVH, TOK, TOK)
    part = (KVH, 8, TOK)
    quarter = (2, STATE, 512)
    return pl.pallas_call(
        layer_kernel,
        out_shape=tuple(jax.ShapeDtypeStruct(s, t) for s, t in OUTS),
        in_specs=[pl.BlockSpec(memory_space=pltpu.SMEM)] + [pl.BlockSpec(memory_space=pl.ANY)] * 10,
        out_specs=(pl.BlockSpec(memory_space=vm),) * 7,
        scratch_shapes=[
            vm((WIDTH, TOK), BF), vm((WIDTH, TOK), BF), vm((WIDTH, TOK), BF),
            vm((STATE, TOK), BF), vm((STATE, TOK), BF), vm((HEADS, 1, TOK), F32), vm((32, TOK), F32),
            vm((WIDTH, TOK), BF), vm((WIDTH, TOK), BF), vm((WIDTH, TOK), F32),
            vm((10,) + block, BF), vm(block, BF), vm((KVH, TOK, 2 * TOK * GROUP), BF),
            vm((TOK, 10 * TOK), jnp.int32), vm((KVH, 2 * TOK * GROUP, 10 * TOK), BF),
            vm((10,) + block, BF), vm(block, F32), vm((2, 4, 2) + part, F32),
            vm((4,) + quarter, BF), vm((4,) + quarter, BF), vm((8, 32), F32), vm((4, 8, 32), F32),
            vm(quarter, BF), vm((4,) + quarter, BF), vm((8, 32), F32), vm((4, 8, 32), F32),
            vm(quarter, BF), vm((4, STATE, 512), BF), vm((8, 32), F32), vm((4, 8, 32), F32),
            vm((4,) + quarter, BF), vm((4,) + quarter, BF), vm((STATE, WIDTH), F32), vm((STATE, WIDTH), F32),
            vm((5,) + block, BF), vm(block, BF), vm((3,) + block, BF),
            vm(block, BF), vm(block, BF), vm(block, BF), vm(block, BF),
            vm((4, 2) + part, F32), vm((4, 2) + part, F32),
            vm((15,) + part, F32), vm(part, F32), vm((15, 2, 8, TOK), F32), vm((2, 8, TOK), F32), vm((2, 8, TOK), F32),
            dma((10,)), dma((8,)), dma((8,)), dma((10,)), dma((10,)),
            dma((6,)), dma((6,)), dma((6,)), dma((6,)), dma((6,)), dma((6,)), dma((3,)), dma((3,)),
            dma((15,)), dma((15,)), dma((12,)), dma((12,)), dma((32,)), dma((32,)), pltpu.SemaphoreType.REGULAR,
        ],
        compiler_params=pltpu.CompilerParams(
            collective_id=0, has_side_effects=True, vmem_limit_bytes=56 * 1024 * 1024
        ),
        name="layer_grads",
    )(*args)


def hand_out_kernel(*refs):
    sources, targets, through, sem = refs[:7], refs[7:14], refs[14:21], refs[21]
    arrive = [pltpu.make_async_copy(a, b, sem.at[n]) for n, (a, b) in enumerate(zip(sources, through))]
    leave = [pltpu.make_async_copy(a, b, sem.at[7 + n]) for n, (a, b) in enumerate(zip(through, targets))]
    for copy in arrive:
        copy.start()
    for first, then in zip(arrive, leave):
        first.wait()
        then.start()
    for copy in leave:
        copy.wait()


def hand_out(arrays):
    return pl.pallas_call(
        hand_out_kernel,
        out_shape=tuple(jax.ShapeDtypeStruct(s, t) for s, t in OUTS),
        in_specs=[pl.BlockSpec(memory_space=pl.ANY)] * 7,
        out_specs=(pl.BlockSpec(memory_space=pl.ANY),) * 7,
        scratch_shapes=[pltpu.VMEM(s, t) for s, t in OUTS] + [pltpu.SemaphoreType.DMA((14,))],
        compiler_params=pltpu.CompilerParams(vmem_limit_bytes=60 * 1024 * 1024),
        name="hand_out",
    )(*arrays)


def local(
    queries, key_vectors, value_vectors, meta_keys, meta_values, windows,
    ssm_input, input_map, output_map, log_decay, cotangent,
):
    def turn(a):
        return jnp.swapaxes(a, -1, -2)

    def by_head(a):
        return turn(a).reshape(KVH, HD, TOK)

    grad_q, grad_k, grad_v, grad_meta, grad_input, grad_bm, grad_cm = hand_out(
        run_layer(
            windows, by_head(key_vectors[0]), by_head(value_vectors[0]), turn(ssm_input[0]), turn(cotangent[0]),
            turn(queries[0]), turn(input_map[0]), turn(output_map[0]), log_decay.transpose(2, 0, 1),
            by_head(meta_keys), by_head(meta_values),
        )
    )
    return (
        turn(grad_q)[None], turn(grad_k)[None], turn(grad_v)[None], grad_meta.transpose(1, 2, 0),
        turn(grad_input)[None], turn(grad_bm)[None], turn(grad_cm)[None],
    )


def solution(mesh):
    seq = P("dp", "ctx", None)
    return jax.shard_map(
        local,
        mesh=mesh,
        in_specs=(seq, seq, seq, P(), P(), P(), seq, seq, seq, seq, seq),
        out_specs=(seq, seq, seq, P(None, "dp", "ctx"), seq, seq, seq),
        check_vma=False,
    )
```

```python
import functools

import jax
import jax.numpy as jnp
from jax import lax
from jax.experimental import pallas as pl
from jax.experimental.pallas import tpu as pltpu
from jax.sharding import PartitionSpec as P

BF = jnp.bfloat16
F32 = jnp.float32
MESH = pl.DeviceIdType.MESH
HEADS, KVH, GROUP, HD = 25, 5, 5, 64
TOK, WIDTH, KVW, STATE = 128, 1600, 320, 16
QL = 448
NT = (((1,), (1,)), ((), ()))
TN = (((0,), (0,)), ((), ()))


def dot(a, b, dims=(((1,), (0,)), ((), ()))):
    return lax.dot_general(a, b, dims, preferred_element_type=F32)


def split3(v):
    hi = v.astype(BF)
    rest = v - hi.astype(F32)
    mid = rest.astype(BF)
    low = (rest - mid.astype(F32)).astype(BF)
    return hi, mid, low


def dot3(v, onehot):
    hi, mid, low = split3(v)
    return dot(hi, onehot) + dot(mid, onehot) + dot(low, onehot)


def iota(shape, dim):
    return lax.broadcasted_iota(jnp.int32, shape, dim)


def places():
    dp, i = lax.axis_index("dp"), lax.axis_index("ctx")
    return dp, i, i % 2, (i // 2) % 2, i // 4


def layer_kernel(
    wins, key, val, xin, gin_, qin, bmin, cmin, ldin, mkin, mvin,
    gq, gk, gv, gm, gin, gbm, gcm,
    x, g, q, bm, cm, ldv, ldp, xt, gt, loc, win, metas, qg, dist, ps, pieces, own, sink,
    stq, r1, d0, d1, s2, r2, d2s, d2, s3, r3, d3s, d3, ib, ob, inc, adj,
    rc, ry, rz, sc, sb, sy, sa, k0, a0, k1, a2, k4, a4, k5,
    in_sem, kv_send, kv_recv, c_send, c_recv, q1_send, q1_recv, q2_send, q2_recv, q3_send, q3_recv,
    q4_send, q4_recv, e_send, e_recv, t_send, t_recv, m_send, m_recv, vouch,
):
    dp, i, core, yh, z = places()
    c = i % 4
    zl, zh = z % 4, z // 4
    xx, yl = dp % 4, dp // 4
    base = i - c
    ahead2, ahead4 = (i + 2) % 64, (i + 4) % 64
    back2, back4 = (i + 62) % 64, (i + 60) % 64
    ahead6, back6 = (i + 6) % 64, (i + 58) % 64
    along_z = [(z + k) % 16 for k in range(1, 16)]
    group = [base + (c + k) % 4 for k in (1, 2, 3)]
    near = [(zh * 4 + (zl + k) % 4) * 4 + c for k in (1, 2, 3)]
    far = [(((zh + k) % 4) * 4 + zl) * 4 + c for k in (1, 2, 3)]
    mate = base + (c + 1 - 2 * core)
    across = base + (c + 2) % 4
    diag = across + 1 - 2 * core
    along_xy = [
        (((yl + a) % 2) * 4 + (xx + k) % 4, base + ((yh + b) % 2) * 2 + core)
        for k in range(4) for a in range(2) for b in range(2) if k + a + b > 0
    ]

    barrier = pltpu.get_barrier_semaphore()
    close = [(z + k) % 16 for k in (1, 2, 3, 4, 12, 13, 14, 15)]
    for to in [(dp, 4 * there + c) for there in close] + along_xy + [(dp, o) for o in (mate, diag, ahead2, back2, ahead6, back6)]:
        pl.semaphore_signal(barrier, inc=1, device_id=to, device_id_type=MESH)

    def fetch(n, src, dst):
        copy = pltpu.make_async_copy(src, dst, in_sem.at[n])
        copy.start()
        return copy

    first_in = [fetch(0, key, win.at[0, :, 0:HD, :]), fetch(1, val, win.at[0, :, HD : 2 * HD, :])]
    scan_in = [fetch(2, ldin, ldv), fetch(3, xin, x), fetch(4, gin_, g), fetch(5, bmin, bm), fetch(6, cmin, cm)]
    late_in = [
        fetch(7, qin, q), fetch(8, mkin, metas.at[:, 0:HD, :]), fetch(9, mvin, metas.at[:, HD : 2 * HD, :])
    ]

    def pair(src, dst, send, recv, n, to):
        return pltpu.make_async_remote_copy(
            src_ref=src, dst_ref=dst, send_sem=send.at[n], recv_sem=recv.at[n],
            device_id=to, device_id_type=MESH,
        )

    for copy in first_in:
        copy.wait()
    pl.semaphore_wait(barrier, 29)
    for k in (4, 12):
        pl.semaphore_signal(
            vouch, inc=1, device_id=(dp, 4 * ((z + k) % 16) + c), device_id_type=MESH
        )

    def kv_copies(n, lo, hi):
        def step(src, dst, m, to):
            return pair(win.at[src, lo:hi], win.at[dst, lo:hi], kv_send, kv_recv, 4 * n + m, (dp, to))

        def to_mate(d, m):
            there = (d + core * 9 + (1 - core)) % 10
            return pair(win.at[d, lo:hi], win.at[there, lo:hi], c_send, c_recv, 5 * n + m, (dp, mate))

        third = step(0, 6, 2, ahead6) if n == 0 else step(2, 6, 2, ahead4)
        steps = (step(0, 2, 0, ahead2), step(0, 4, 1, ahead4), third, step(4, 8, 3, ahead4))
        return steps, [to_mate(d, m) for m, d in enumerate((0, 2, 4, 6, 8))]

    halves = [kv_copies(0, 0, 2), kv_copies(1, 2, KVH)]
    halves[0][0][2].start()
    for steps, mates in halves:
        steps[0].start()
        steps[1].start()
        mates[0].start()

    def forward(n):
        steps, mates = halves[n]
        steps[0].wait_recv()
        if n == 1:
            steps[2].start()
        mates[1].start()
        steps[1].wait_recv()
        steps[3].start()
        mates[2].start()

    def finish(n):
        steps, mates = halves[n]
        steps[2].wait_recv()
        mates[3].start()
        steps[3].wait_recv()
        mates[4].start()

    for copy in scan_in:
        copy.wait()
    rows, cols = iota((TOK, TOK), 0), iota((TOK, TOK), 1)
    tri = (rows >= cols).astype(BF)
    ldp[...] = jnp.zeros((32, TOK), F32)
    for h in range(HEADS):
        ldp[h : h + 1, :] = ldv[h]
    run = jnp.zeros((TOK, 32), F32)
    run_t = jnp.zeros((32, TOK), F32)
    for part in split3(ldp[...]):
        run = run + dot(tri, part, NT)
        run_t = run_t + dot(part, tri, NT)
    end = run_t[:, TOK - 1 : TOK]
    tail = jnp.exp(end - run_t)
    head = jnp.exp(run_t)
    for h in range(HEADS):
        f = slice(HD * h, HD * h + HD)
        xt[f, :] = (tail[h : h + 1, :] * x[f, :].astype(F32)).astype(BF)
        gt[f, :] = (head[h : h + 1, :] * g[f, :].astype(F32)).astype(BF)
    for w, terms in enumerate((dot(bm[...], xt[...], NT), dot(cm[...], gt[...], NT))):
        for p in range(4):
            n = min(QL, WIDTH - QL * p)
            stq[p, w] = jnp.concatenate(
                [terms[:, QL * p : QL * p + n], jnp.zeros((STATE, 512 - n), F32)], axis=1
            ).astype(BF)
    d0[...] = jnp.broadcast_to(jnp.exp(run[TOK - 1 : TOK, :]), (8, 32))
    q1 = []
    for n, k in enumerate((1, 2, 3)):
        q1.append(pair(stq.at[(c + k) % 4], r1.at[c], q1_send, q1_recv, n, (dp, group[n])))
        q1.append(pair(d0, d1.at[c], q1_send, q1_recv, 3 + n, (dp, group[n])))
    for copy in q1:
        copy.start()
    r1[c] = stq[c]
    d1[c] = d0[...]

    inner = dot(cm[...], bm[...], TN)

    def local_head(h, gram):
        f = slice(HD * h, HD * h + HD)
        diff = run[:, h : h + 1] - run_t[h : h + 1, :]
        mix = jnp.where(rows >= cols, jnp.exp(diff), 0.0)
        loc[f, :] = dot(g[f, :], (mix * inner).astype(BF))
        return gram + mix * dot(g[f, :], x[f, :], TN)

    gram = jnp.zeros((TOK, TOK), F32)
    for h in range(0, 8):
        gram = local_head(h, gram)
    forward(0)

    for copy in late_in:
        copy.wait()
    zeros = jnp.zeros((HD, TOK), BF)
    for k in range(KVH):
        for j in range(GROUP):
            f = slice(HD * (GROUP * k + j), HD * (GROUP * k + j) + HD)
            at = 2 * TOK * j
            qg[k, 0:HD, at : at + TOK] = (q[f, :].astype(F32) * 0.125).astype(BF)
            qg[k, 0:HD, at + TOK : at + 2 * TOK] = zeros
            qg[k, HD : 2 * HD, at : at + TOK] = zeros
            qg[k, HD : 2 * HD, at + TOK : at + 2 * TOK] = g[f, :]
    behind_by = rows - cols
    never = jnp.int32(1 << 20)
    dist[:, 0:TOK] = jnp.zeros((TOK, TOK), jnp.int32)
    dist[:, TOK : 2 * TOK] = jnp.where(behind_by >= 0, behind_by, never)
    for d in range(1, 9):
        dist[:, TOK * (d + 1) : TOK * (d + 2)] = jnp.where(i >= d, behind_by + TOK * d, never)
    pieces[9] = jnp.zeros((KVH, TOK, TOK), BF)

    for h in range(8, 14):
        gram = local_head(h, gram)
    finish(0)
    forward(1)

    row, lane = iota((32, 512), 0), iota((32, 512), 1)
    onehot = ((row == 7 * c + lane // HD) & (lane < QL)).astype(BF)

    def expand(d):
        wide = dot3(d[...].reshape(32, 32), onehot)
        return [jnp.broadcast_to(wide[8 * j : 8 * j + 1], (STATE, 512)) for j in range(4)]

    def sums(dec, terms):
        total, back = terms[0, 0].astype(F32), terms[3, 1].astype(F32)
        for j in range(1, 4):
            total = dec[j] * total + terms[j, 0].astype(F32)
            back = dec[3 - j] * back + terms[3 - j, 1].astype(F32)
        return total.astype(BF), back.astype(BF)

    q2 = []
    for n in range(3):
        q2.append(pair(s2, r2.at[zl], q2_send, q2_recv, n, (dp, near[n])))
        q2.append(pair(d2s, d2.at[zl], q2_send, q2_recv, 3 + n, (dp, near[n])))
    q3 = []
    for n, k in enumerate((1, 2, 3)):
        there = (zh + k) % 4
        which = jnp.where(there > zh, 0, 1)
        q3.append(pair(s3.at[which], r3.at[zh], q3_send, q3_recv, n, (dp, far[n])))
        q3.append(pair(d3s, d3.at[zh], q3_send, q3_recv, 3 + n, (dp, far[n])))
    q4 = [
        pair(ib.at[(c + k) % 4], ob.at[c], q4_send, q4_recv, n, (dp, group[n]))
        for n, k in enumerate((1, 2, 3))
    ]

    def scan_second():
        for copy in q1:
            copy.wait_recv()
        s2[0], s2[1] = sums(expand(d1), r1)
        d2s[...] = d1[0] * d1[1] * d1[2] * d1[3]
        for copy in q2:
            copy.start()
        r2[zl] = s2[...]
        d2[zl] = d2s[...]

    def scan_third():
        for copy in q2:
            copy.wait_recv()
        pl.semaphore_wait(vouch, 2)
        s3[0], s3[1] = sums(expand(d2), r2)
        d3s[...] = d2[0] * d2[1] * d2[2] * d2[3]
        for copy in q3:
            copy.start()
        r3[zh] = s3[0]
        d3[zh] = d3s[...]

    def scan_fourth():
        for copy in q3:
            copy.wait_recv()
        dec1, dec2, dec3 = expand(d1), expand(d2), expand(d3)
        ahead = jnp.zeros((STATE, 512), F32)
        behind = ahead
        for j in range(4):
            b = 3 - j
            ahead = jnp.where(j < zh, dec3[j] * ahead + r3[j].astype(F32), ahead)
            behind = jnp.where(b > zh, dec3[b] * behind + r3[b].astype(F32), behind)
        for j in range(4):
            b = 3 - j
            ahead = jnp.where(j < zl, dec2[j] * ahead + r2[j, 0].astype(F32), ahead)
            behind = jnp.where(b > zl, dec2[b] * behind + r2[b, 1].astype(F32), behind)
        for j in range(4):
            b = 3 - j
            ib[j, 0] = ahead.astype(BF)
            ahead = dec1[j] * ahead + r1[j, 0].astype(F32)
            ib[b, 1] = behind.astype(BF)
            behind = dec1[b] * behind + r1[b, 1].astype(F32)
        for copy in q4:
            copy.start()
        ob[c] = ib[c]

    scan_second()
    for copy in halves[0][1]:
        copy.wait_recv()

    def keys_of(k):
        return jnp.concatenate([metas[k]] + [win[d, k] for d in range(9)], axis=1)

    def probs_of(k, carry):
        kv = keys_of(k)
        for j in range(GROUP):
            at = 2 * TOK * j
            both = dot(qg[k, :, at : at + 2 * TOK], kv, TN)
            s, dpr = both[:TOK], both[TOK:]
            s = jnp.where(dist[...] < wins[GROUP * k + j], s, -1e30)
            e = jnp.exp(s - jnp.max(s, axis=1, keepdims=True))
            inv = 1.0 / jnp.sum(e, axis=1, keepdims=True)
            delta = jnp.sum(e * dpr, axis=1, keepdims=True) * inv
            p = e * inv
            ps[k, at : at + TOK, :] = (p * (dpr - delta)).astype(BF)
            ps[k, at + TOK : at + 2 * TOK, :] = p.astype(BF)
        turned = dot(qg[k], ps[k, :, 0:TOK]).T
        for r in range(16):
            sink[r % 2, (r // 2) % 4, r // 8, k] = turned[8 * r : 8 * r + 8]

        @pl.when(k == 0)
        def _():
            finish(1)

        @pl.when(k == 1)
        def _():
            for copy in halves[1][1]:
                copy.wait_recv()
            scan_third()

        return carry

    lax.fori_loop(0, KVH, probs_of, 0)

    held = (20 * z) // 64 - (20 * z) // 256
    m0 = pair(sink.at[1 - core], k0, m_send, m_recv, 0, (dp, mate))
    m1 = [
        pair(a0.at[to[0] % 4, to[0] // 4], k1.at[n], m_send, m_recv, 1 + n, to) for n, to in enumerate(along_xy)
    ]
    m2 = [
        pair(a2.at[pl.ds((20 * to) // 64 - (20 * to) // 256, 2)], k4.at[n], m_send, m_recv, 16 + n, (dp, 4 * to + c))
        for n, to in enumerate(along_z)
    ]
    m3 = pair(a4, k5, m_send, m_recv, 31, (dp, mate))

    def total(own_part, parts):
        for n in range(15):
            own_part = own_part + parts[n]
        return own_part

    def pass_on(arrived, result, value, following):
        for copy in arrived:
            copy.wait_recv()
        result[...] = value()
        for copy in following:
            copy.start()

    m0.start()

    parts = ((0, 2), (2, 4), (4, KVH))
    order = (6, 8, 2, 4, 0)
    gives = [
        [
            pair(
                pieces.at[(d + core + 9 * (1 - core)) % 10, lo:hi], rc.at[m, lo:hi],
                e_send, e_recv, 5 * n + m, (dp, mate),
            )
            for m, d in enumerate(order)
        ]
        for n, (lo, hi) in enumerate(parts)
    ]
    backs = [
        [
            pair(src.at[lo:hi], dst.at[lo:hi], t_send, t_recv, 4 * n + m, (dp, to))
            for m, (src, dst, to) in enumerate(
                ((sb, rz.at[1], back4), (sc, rz.at[0], back4), (sy, ry, back2), (sa, rz.at[2], back4))
            )
        ]
        for n, (lo, hi) in enumerate(parts)
    ]

    def send_far(n):
        lo, hi = parts[n]
        for m, out in ((0, sb), (1, sc)):
            gives[n][m].wait_recv()
            out[lo:hi] = (pieces[order[m], lo:hi].astype(F32) + rc[m, lo:hi].astype(F32)).astype(BF)
            backs[n][m].start()

    def send_near(n, m, out, arrived):
        lo, hi = parts[n]
        gives[n][m].wait_recv()
        backs[n][m - 2].wait_recv()
        part = pieces[order[m], lo:hi].astype(F32) + rc[m, lo:hi].astype(F32)
        out[lo:hi] = (part + rz[arrived, lo:hi].astype(F32)).astype(BF)
        backs[n][m].start()

    def grads_of(k, carry):
        kv = keys_of(k)
        for j in range(GROUP):
            at = 2 * TOK * j
            dq = dot(kv[0:HD], ps[k, at : at + TOK, :], NT) * 0.125
            gq[pl.ds(pl.multiple_of(HD * (GROUP * k + j), HD), HD), :] = dq.astype(BF)
        back_t = dot(qg[k], ps[k, :, TOK:])
        own[k] = back_t[:, :TOK]
        for d in range(1, 9):
            pieces[d, k] = back_t[:, TOK * d : TOK * (d + 1)].astype(BF)

        @pl.when(k == 0)
        def _():
            pass_on([m0], a0, lambda: sink[core] + k0[...], m1)

        @pl.when(k == 1)
        def _():
            for copy in gives[0]:
                copy.start()
            scan_fourth()

        @pl.when(k == 2)
        def _():
            send_far(0)

        @pl.when(k == 3)
        def _():
            for copy in gives[1]:
                copy.start()

        @pl.when(k == 4)
        def _():
            for copy in gives[2]:
                copy.start()
            send_far(1)
            send_near(0, 2, sy, 1)
            send_near(0, 3, sa, 0)
            send_far(2)
            pass_on(m1, a2, lambda: total(a0[xx, yl], k1), m2)

        return carry

    lax.fori_loop(0, KVH, grads_of, 0)

    send_near(1, 2, sy, 1)
    send_near(1, 3, sa, 0)

    for copy in q4:
        copy.wait_recv()
    for p in range(4):
        n = min(QL, WIDTH - QL * p)
        inc[:, QL * p : QL * p + n] = ob[p, 0].astype(F32)[:, :n]
        adj[:, QL * p : QL * p + n] = ob[p, 1].astype(F32)[:, :n]
    inc_h, adj_h = inc[...].astype(BF), adj[...].astype(BF)
    grad_bm = dot(adj_h, xt[...])
    grad_cm = dot(inc_h, gt[...])

    send_near(2, 2, sy, 1)
    send_near(2, 3, sa, 0)

    for h in range(14, HEADS):
        gram = local_head(h, gram)
    gram = gram.astype(BF)
    gbm[...] = grad_bm + dot(cm[...], gram)
    gcm[...] = grad_cm + dot(bm[...], gram, NT)
    carried = dot(adj_h, bm[...], TN)
    tail = jnp.exp(end - run_t)
    for h in range(HEADS):
        f = slice(HD * h, HD * h + HD)
        gin[f, :] = (loc[f, :] + tail[h : h + 1, :] * carried[f]).astype(BF)

    pass_on(m2, a4, lambda: total(a2[pl.ds(held, 2)], k4), [m3])
    for n in range(3):
        gives[n][4].wait_recv()
        backs[n][2].wait_recv()
        backs[n][3].wait_recv()
    for k in range(KVH):
        mine = own[k] + rc[4, k].astype(F32) + ry[k].astype(F32) + rz[2, k].astype(F32)
        gk[HD * k : HD * k + HD, :] = mine[:HD].astype(BF)
        gv[HD * k : HD * k + HD, :] = mine[HD:].astype(BF)

    m3.wait_recv()
    row, lane = iota((16, TOK), 0), iota((16, TOK), 1)
    first = jnp.zeros((16, 8), F32)
    second = jnp.zeros((16, 8), F32)
    for k in range(2):
        feature = 5 * i + row % 8 - HD * (held + k)
        pick = (row % 8 < 5) & (feature >= 0) & (feature < HD) & (lane == feature + HD * (row // 8))
        pick = pick.astype(BF)
        for part in split3(a4[k]):
            first = first + dot(pick, part, NT)
        for part in split3(k5[k]):
            second = second + dot(pick, part, NT)
    left = jnp.where(core == 0, first, second)
    right = jnp.where(core == 0, second, first)
    for j in range(5):
        for w in range(2):
            gm[j, w : w + 1, 0:8] = left[8 * w + j : 8 * w + j + 1]
            gm[j, w : w + 1, 8:16] = right[8 * w + j : 8 * w + j + 1]

    for copy in q1 + q2 + q3 + q4 + [m0, m3] + m1 + m2:
        copy.wait_send()
    for steps, mates in halves:
        for copy in list(steps) + mates:
            copy.wait_send()
    for copy in sum(gives, []) + sum(backs, []):
        copy.wait_send()


OUTS = (
    ((WIDTH, TOK), BF), ((KVW, TOK), BF), ((KVW, TOK), BF), ((5, 2, 16), F32),
    ((WIDTH, TOK), BF), ((STATE, TOK), F32), ((STATE, TOK), F32),
)


def run_layer(*args):
    dma = pltpu.SemaphoreType.DMA
    vm = pltpu.VMEM
    block = (KVH, TOK, TOK)
    part = (KVH, 8, TOK)
    quarter = (2, STATE, 512)
    return pl.pallas_call(
        layer_kernel,
        out_shape=tuple(jax.ShapeDtypeStruct(s, t) for s, t in OUTS),
        in_specs=[pl.BlockSpec(memory_space=pltpu.SMEM)] + [pl.BlockSpec(memory_space=pl.ANY)] * 10,
        out_specs=(pl.BlockSpec(memory_space=vm),) * 7,
        scratch_shapes=[
            vm((WIDTH, TOK), BF), vm((WIDTH, TOK), BF), vm((WIDTH, TOK), BF),
            vm((STATE, TOK), BF), vm((STATE, TOK), BF), vm((HEADS, 1, TOK), F32), vm((32, TOK), F32),
            vm((WIDTH, TOK), BF), vm((WIDTH, TOK), BF), vm((WIDTH, TOK), F32),
            vm((10,) + block, BF), vm(block, BF), vm((KVH, TOK, 2 * TOK * GROUP), BF),
            vm((TOK, 10 * TOK), jnp.int32), vm((KVH, 2 * TOK * GROUP, 10 * TOK), BF),
            vm((10,) + block, BF), vm(block, F32), vm((2, 4, 2) + part, F32),
            vm((4,) + quarter, BF), vm((4,) + quarter, BF), vm((8, 32), F32), vm((4, 8, 32), F32),
            vm(quarter, BF), vm((4,) + quarter, BF), vm((8, 32), F32), vm((4, 8, 32), F32),
            vm(quarter, BF), vm((4, STATE, 512), BF), vm((8, 32), F32), vm((4, 8, 32), F32),
            vm((4,) + quarter, BF), vm((4,) + quarter, BF), vm((STATE, WIDTH), F32), vm((STATE, WIDTH), F32),
            vm((5,) + block, BF), vm(block, BF), vm((3,) + block, BF),
            vm(block, BF), vm(block, BF), vm(block, BF), vm(block, BF),
            vm((4, 2) + part, F32), vm((4, 2) + part, F32),
            vm((15,) + part, F32), vm(part, F32), vm((15, 2, 8, TOK), F32), vm((2, 8, TOK), F32), vm((2, 8, TOK), F32),
            dma((10,)), dma((8,)), dma((8,)), dma((10,)), dma((10,)),
            dma((6,)), dma((6,)), dma((6,)), dma((6,)), dma((6,)), dma((6,)), dma((3,)), dma((3,)),
            dma((15,)), dma((15,)), dma((12,)), dma((12,)), dma((32,)), dma((32,)), pltpu.SemaphoreType.REGULAR,
        ],
        compiler_params=pltpu.CompilerParams(
            collective_id=0, has_side_effects=True, vmem_limit_bytes=56 * 1024 * 1024
        ),
        name="layer_grads",
    )(*args)


def hand_out_kernel(*refs):
    sources, targets, through, sem = refs[:7], refs[7:14], refs[14:21], refs[21]
    arrive = [pltpu.make_async_copy(a, b, sem.at[n]) for n, (a, b) in enumerate(zip(sources, through))]
    leave = [pltpu.make_async_copy(a, b, sem.at[7 + n]) for n, (a, b) in enumerate(zip(through, targets))]
    for copy in arrive:
        copy.start()
    for first, then in zip(arrive, leave):
        first.wait()
        then.start()
    for copy in leave:
        copy.wait()


def hand_out(arrays):
    return pl.pallas_call(
        hand_out_kernel,
        out_shape=tuple(jax.ShapeDtypeStruct(s, t) for s, t in OUTS),
        in_specs=[pl.BlockSpec(memory_space=pl.ANY)] * 7,
        out_specs=(pl.BlockSpec(memory_space=pl.ANY),) * 7,
        scratch_shapes=[pltpu.VMEM(s, t) for s, t in OUTS] + [pltpu.SemaphoreType.DMA((14,))],
        compiler_params=pltpu.CompilerParams(vmem_limit_bytes=60 * 1024 * 1024),
        name="hand_out",
    )(*arrays)


def local(
    queries, key_vectors, value_vectors, meta_keys, meta_values, windows,
    ssm_input, input_map, output_map, log_decay, cotangent,
):
    def turn(a):
        return jnp.swapaxes(a, -1, -2)

    def by_head(a):
        return turn(a).reshape(KVH, HD, TOK)

    grad_q, grad_k, grad_v, grad_meta, grad_input, grad_bm, grad_cm = hand_out(
        run_layer(
            windows, by_head(key_vectors[0]), by_head(value_vectors[0]), turn(ssm_input[0]), turn(cotangent[0]),
            turn(queries[0]), turn(input_map[0]), turn(output_map[0]), log_decay.transpose(2, 0, 1),
            by_head(meta_keys), by_head(meta_values),
        )
    )
    return (
        turn(grad_q)[None], turn(grad_k)[None], turn(grad_v)[None], grad_meta.transpose(1, 2, 0),
        turn(grad_input)[None], turn(grad_bm)[None], turn(grad_cm)[None],
    )


def solution(mesh):
    seq = P("dp", "ctx", None)
    return jax.shard_map(
        local,
        mesh=mesh,
        in_specs=(seq, seq, seq, P(), P(), P(), seq, seq, seq, seq, seq),
        out_specs=(seq, seq, seq, P(None, "dp", "ctx"), seq, seq, seq),
        check_vma=False,
    )
```
